32 devices in a mesh: blk: 2 (over x), wide: 16 (over z, y, core).
Axes of the slice: x: 2, y: 2, z: 4, core: 2. Of those that a mesh axis runs over, the one named last changes fastest.
Arguments:
- tokens: bfloat16 [16, 2048, 768], P('wide', 'blk'), may hold values from -6 to 6
- segments: int32 [16, 2048], P('wide'), may hold values from 0 to 7, as said below
- routes: int32 [16, 2048, 1], P('wide', 'blk'), may hold values from 0 to 15; in each aligned block of 1024 rows (0 to 1023, 1024 to 2047, ..., all dimensions but the last counted through in order) at most 128 rows name the same one
- project_in: bfloat16 [768, 2304], replicated, may hold values from -0.21875 to 0.21875
- project_out: bfloat16 [768, 768], replicated, may hold values from -0.625 to 0.625
- first_gain: float32 [768], replicated, may hold values from 0.5 to 1.5
- first_shift: float32 [768], replicated, may hold values from -1 to 1
- second_gain: float32 [768], replicated, may hold values from 0.5 to 1.5
- second_shift: float32 [768], replicated, may hold values from -1 to 1
- centroids: float32 [16, 768], replicated, may hold values from -0.15625 to 0.15625
- expert_up: bfloat16 [16, 768, 3072], P('wide'), may hold values from -0.21875 to 0.21875
- expert_down: bfloat16 [16, 3072, 768], P('wide'), may hold values from -0.21875 to 0.21875
- cotangent: bfloat16 [16, 2048, 768], P('wide', 'blk'), may hold values from -6 to 6
Outputs:
- result: bfloat16 [16, 2048, 768], P('wide', 'blk')
- input_grad: float32 [16, 2048, 768], P('wide', 'blk')
- project_in_grad: float32 [768, 2304], replicated
- project_out_grad: float32 [768, 768], replicated
- first_gain_grad: float32 [768], replicated
- first_shift_grad: float32 [768], replicated
- second_gain_grad: float32 [768], replicated
- second_shift_grad: float32 [768], replicated
- expert_up_grad: float32 [16, 768, 3072], P('wide', None, 'blk')
- expert_down_grad: float32 [16, 3072, 768], P('wide', 'blk')
The draws below stay inside these ranges and needn't reach their ends.
Inputs may be any that keep to these rules, and one draw needn't show every extreme that they name: `segments`: within a row the numbers never fall. Half of the rows hold eight documents of 256 tokens each, numbered 0 to 7; in each other row one document begins among the row's first 1024 tokens and ends among its last 1024. `routes`: among the 1024 tokens of one row's block on one device (aligned blocks along a row) each expert is named at most 128 times, a bound that some block reaches.
All inputs are finite; a program needn't handle non-finite values.
Results may differ from the reference program's by a relative error of at most 0.024.
Values may be sent and summed in bfloat16 or wider, within the bound.
No kernel may reach another device: no remote copies, remote signals or barrier semaphores. Data moves between devices by JAX's collectives and lax.ppermute only.
A program may use at most 320 MiB of HBM per device.

```python
import math
import jax
import jax.numpy as jnp
import numpy as np
from jax import lax

D = 768
HEAD_DIM = 64
FF = 3072
ROW_LEN = 2048
TOK_DEV = 1024
ROWS = 16
DOC_LEN = 256
EXPERTS = 16
CAP = 128
N_BLK = 2


def draw_segments(key, part):
    key = jax.random.fold_in(key, 7)
    subkeys = jax.random.split(key, 7)
    first_cut = jax.random.randint(subkeys[0], (ROWS, 1), 1, TOK_DEV)
    last_cut = jax.random.randint(subkeys[1], (ROWS, 1), ROW_LEN - TOK_DEV + 1, ROW_LEN)
    cut_one = jax.random.randint(subkeys[2], (ROWS, 1), 0, first_cut)
    cut_two = jax.random.randint(subkeys[3], (ROWS, 1), 0, first_cut)
    cut_three = jax.random.randint(subkeys[4], (ROWS, 1), last_cut, ROW_LEN)
    cut_four = jax.random.randint(subkeys[5], (ROWS, 1), last_cut, ROW_LEN)
    places = lax.iota(jnp.int32, ROW_LEN)[None, :]
    numbers = jnp.zeros((ROWS, ROW_LEN), jnp.int32)
    for cutting in (first_cut, last_cut, cut_one, cut_two, cut_three, cut_four):
        numbers = numbers + (places >= cutting).astype(jnp.int32)
    packed_numbers = places // DOC_LEN
    order = jax.random.permutation(subkeys[6], ROWS)
    packed = (order < ROWS // 2)[:, None]
    return jnp.where(packed, packed_numbers, numbers)


def shard_levels(own_key, dims, cuts, smallest, high):
    factor_of = 1.0
    for axis_at, blocks in cuts:
        heights = jax.random.uniform(jax.random.fold_in(jax.random.fold_in(own_key, 6), axis_at), (blocks,), jnp.float32, smallest / len(cuts), high / len(cuts))
        factor_of = factor_of * jnp.repeat(jnp.exp(heights), dims[axis_at] // blocks).reshape((-1,) + (1,) * (len(dims) - 1 - axis_at))
    return factor_of


def routed_block(stream_key, own, number, rows, count, top, bound, skew):
    order = jax.random.permutation(stream_key, count)
    crowded, usual = portions_of(count, rows * top, bound, skew, True), portions_of(count, rows * top, bound, skew, False)
    places = jnp.arange(count)

    def named(lengths, offset_by):
        used = int((lengths > 0).sum())
        fixed = max(1, used // 4)
        passed = fixed + (places - fixed + offset_by * (used - fixed)) % max(1, count - fixed)
        return jnp.zeros((count,), jnp.int32).at[order[jnp.where(places < fixed, places, passed)]].set(jnp.asarray(lengths, jnp.int32))

    lengths = jnp.where(number % 4 == 0, named(crowded, number // 4), named(usual, number - number // 4 - 1))
    mixed = jax.random.permutation(jax.random.fold_in(own, 3), count)
    donor, receiver = mixed[0:count // 2 * 2:2], mixed[1:count // 2 * 2:2]
    margin = jnp.minimum(lengths[donor] - 1, bound - lengths[receiver]) // 2
    margin = jnp.where((donor == order[0]) | (receiver == order[0]) | (lengths[receiver] == 0), 0, jnp.maximum(margin, 0))
    passed = jax.random.randint(jax.random.fold_in(own, 4), (count // 2,), 0, 1 << 20) % (margin + 1)
    lengths = lengths.at[donor].add(-passed).at[receiver].add(passed)
    labels = jnp.searchsorted(jnp.cumsum(lengths), jnp.arange(rows * top), side="right").astype(jnp.int32)
    listing = labels.reshape(top, rows).T
    listing = listing[jax.random.permutation(jax.random.fold_in(own, 1), rows)]
    offset_by = jax.random.randint(jax.random.fold_in(own, 2), (rows, 1), 0, top)
    return jnp.take_along_axis(listing, (jnp.arange(top)[None, :] + offset_by) % top, axis=1)


def portions_of(amount, total, most, skew, full):
    weights = [(1 << 20) // math.isqrt(standing ** skew) + 1 for standing in range(1, amount + 1)]
    largest = most if full else min(most, max(-(-total // amount), total * weights[0] // sum(weights)))
    least = 1 if total - largest >= amount - 1 else 0
    holding, rest = [largest] + [least] * (amount - 1), total - largest - least * (amount - 1)
    while rest > 0:
        free = [i for i in range(1, amount) if holding[i] < largest] or [i for i in range(1, amount) if holding[i] < most]
        mass, remaining = sum([weights[i] for i in free]), rest
        for i in free:
            more = min(most - holding[i], max(1, remaining * weights[i] // mass), rest)
            holding[i] = holding[i] + more
            rest = rest - more
    return np.array(holding)


def scatter_about(stream_key, shape, deviation, bound, pieces=(), dtype=jnp.bfloat16):
    drawn = jax.random.normal(stream_key, shape, jnp.float32) * deviation
    if len(pieces) > 0:
        drawn = shard_levels(stream_key, shape, pieces, -0.22, 0.18) * drawn
    return jnp.clip(drawn, min=-bound, max=bound).astype(dtype)


def setup_inputs(seed: int = 0) -> dict:
    splits = jax.random.split(jax.random.key(seed), 14)
    tokens = scatter_about(splits[0], (ROWS, ROW_LEN, D), 1.0, 6.0, ((0, 16), (1, 2)))
    segments = draw_segments(jax.random.fold_in(splits[13], 71), 0)
    routes_keys = jax.random.split(jax.random.fold_in(splits[2], 1), ROWS * ROW_LEN // TOK_DEV)
    routes_turns = jax.random.permutation(jax.random.fold_in(splits[2], 3), ROWS * ROW_LEN // TOK_DEV)
    routes = jax.vmap(lambda own, number: routed_block(jax.random.fold_in(splits[2], 2), own, number, TOK_DEV, EXPERTS, 1, CAP, 2))(routes_keys, routes_turns).reshape((ROWS, ROW_LEN, 1))
    project_in = scatter_about(splits[3], (D, 3 * D), D ** -0.5, 0.21875)
    project_out = scatter_about(splits[4], (D, D), (D // 8) ** -0.5, 0.625)
    first_gain = jnp.clip(1.0 + 0.1 * jax.random.normal(splits[5], (D,), jnp.float32), 0.5, 1.5)
    first_shift = scatter_about(splits[6], (D,), 0.2, 1.0, (), jnp.float32)
    second_gain = jnp.clip(1.0 + 0.1 * jax.random.normal(splits[7], (D,), jnp.float32), 0.5, 1.5)
    second_shift = scatter_about(splits[8], (D,), 0.2, 1.0, (), jnp.float32)
    centroids = scatter_about(splits[9], (EXPERTS, D), (D * 5 // 3) ** -0.5, 0.15625, (), jnp.float32)
    expert_up = scatter_about(splits[10], (EXPERTS, D, FF), D ** -0.5, 0.21875, ((0, 16),))
    expert_down = scatter_about(splits[11], (EXPERTS, FF, D), (FF // 4) ** -0.5, 0.21875, ((0, 16),))
    cotangent = scatter_about(splits[12], (ROWS, ROW_LEN, D), 1.0, 6.0, ((0, 16), (1, 2)))
    return dict(tokens=tokens, segments=segments, routes=routes, project_in=project_in, project_out=project_out, first_gain=first_gain, first_shift=first_shift, second_gain=second_gain, second_shift=second_shift, centroids=centroids, expert_up=expert_up, expert_down=expert_down, cotangent=cotangent)


@jax.custom_vjp
def low(v):
    return lax.optimization_barrier(v.astype(jnp.bfloat16)).astype(jnp.float32)

@jax.custom_vjp
def low_back(v):
    return v

def low_keep(v):
    return (low(v), None)

def low_pass(kept, grad):
    return (grad,)

def back_keep(v):
    return (v, None)

def back_low(kept, grad):
    return (low(grad),)
low.defvjp(low_keep, low_pass)
low_back.defvjp(back_keep, back_low)

def layer_norm(inputs, scaling, offsets):
    center = inputs - lax.optimization_barrier(jnp.mean(inputs, -1, keepdims=True))
    variance = lax.optimization_barrier(jnp.mean(center * center, -1, keepdims=True))
    return center * lax.rsqrt(variance + 1e-05) * scaling + offsets

def reference(tokens, segments, routes, project_in, project_out, first_gain, first_shift, second_gain, second_shift, centroids, expert_up, expert_down, cotangent):
    highest = lax.Precision.HIGHEST
    model_width = D
    head_count = model_width // HEAD_DIM
    score_scale = HEAD_DIM ** (-0.5)
    route_flat = routes.reshape(-1)
    most_rows = ROWS * N_BLK * CAP
    places = lax.iota(jnp.int32, ROW_LEN)

    def forward(stream, weight_in, weight_out, gain_one, shift_one, gain_two, shift_two, up_all, down_all):

        def row_step(unused, inputs_row):
            row_tokens, row_segments = inputs_row
            normed = low(layer_norm(row_tokens, gain_one, shift_one))
            joint_proj = low_back(low(jnp.dot(normed, weight_in, precision=highest)))
            queries = joint_proj[:, :model_width].reshape(ROW_LEN, head_count, HEAD_DIM)
            keys_all = joint_proj[:, model_width:2 * model_width].reshape(ROW_LEN, head_count, HEAD_DIM)
            values_all = joint_proj[:, 2 * model_width:].reshape(ROW_LEN, head_count, HEAD_DIM)
            raw_scores = low_back(jnp.einsum('qhd,khd->hqk', queries, keys_all, precision=highest) * score_scale)
            allowed = (places[None, :] <= places[:, None]) & (row_segments[None, :] == row_segments[:, None])
            masked = jnp.where(allowed[None], raw_scores, -1e+30)
            attention = low(jax.nn.softmax(masked, axis=-1))
            context = jnp.einsum('hqk,khd->qhd', attention, values_all, precision=highest).reshape(ROW_LEN, model_width)
            context = low_back(low(context))
            attn_out = low_back(jnp.dot(context, weight_out, precision=highest))
            return (unused, row_tokens + attn_out)
        unused, middle = lax.scan(jax.checkpoint(row_step), jnp.zeros((), jnp.float32), (stream, segments))
        flattened = middle.reshape(-1, model_width)
        normed_two = layer_norm(flattened, gain_two, shift_two)
        dispatched = low_back(low(normed_two))
        gate_value = jax.nn.sigmoid(lax.optimization_barrier(jnp.sum(normed_two * centroids[route_flat], -1)))

        def expert_step(expert_index):
            chosen = route_flat == expert_index
            members = jnp.nonzero(chosen, size=most_rows, fill_value=0)[0]
            filled = (lax.iota(jnp.int32, most_rows) < jnp.sum(chosen.astype(jnp.int32))).astype(jnp.float32)
            picked_rows = dispatched[members] * filled[:, None]
            hidden_pre = low_back(jnp.dot(picked_rows, up_all[expert_index], precision=highest))
            hidden_act = low(jax.nn.gelu(hidden_pre, approximate=False))
            produced = low_back(low(jnp.dot(hidden_act, down_all[expert_index], precision=highest)))
            return (members, produced * filled[:, None])
        members, produced = lax.map(jax.checkpoint(expert_step), lax.iota(jnp.int32, EXPERTS))
        branch = jnp.zeros_like(flattened).at[members.reshape(-1)].add(produced.reshape(-1, model_width))
        output = flattened + gate_value[:, None] * branch
        return output.reshape(ROWS, ROW_LEN, model_width)
    arguments = (tokens.astype(jnp.float32), project_in.astype(jnp.float32), project_out.astype(jnp.float32), first_gain, first_shift, second_gain, second_shift, expert_up.astype(jnp.float32), expert_down.astype(jnp.float32))
    output, backward = jax.vjp(forward, *arguments)
    gradients = backward(cotangent.astype(jnp.float32))
    return (output.astype(jnp.bfloat16), gradients[0], gradients[1], gradients[2], gradients[3], gradients[4], gradients[5], gradients[6], gradients[7], gradients[8])
```

```python
import functools

import jax
import jax.numpy as jnp
from jax import lax
from jax.experimental import pallas as pl
from jax.experimental.pallas import tpu as pltpu
from jax.sharding import PartitionSpec as P

HEAD_DIM = 64
GROUP = 4
LANES = GROUP * HEAD_DIM
NEG = -1e30
f32 = jnp.float32
bf16 = jnp.bfloat16
VMEM_LIMIT = 60 * 1024 * 1024


def tile_of(size, most):
    tile = most
    while size % tile:
        tile //= 2
    return tile


def dot(a, b):
    return jnp.dot(a, b, preferred_element_type=f32)


def dot_nt(a, b):
    return lax.dot_general(a, b, (((1,), (1,)), ((), ())), preferred_element_type=f32)


def flip(a):
    return a.astype(f32).T.astype(a.dtype)


def params(**more):
    return pltpu.CompilerParams(vmem_limit_bytes=VMEM_LIMIT, **more)


def head_rows(transposed, head):
    row = lax.broadcasted_iota(jnp.int32, transposed.shape, 0)
    keep = (row // HEAD_DIM) == (head % 2)
    return jnp.where(keep, transposed, jnp.zeros_like(transposed))


def head_lanes(natural, head):
    lane = lax.broadcasted_iota(jnp.int32, natural.shape, 1)
    keep = (lane // HEAD_DIM) == (head % 2)
    return jnp.where(keep, natural, jnp.zeros_like(natural))


def pair_of(head):
    return slice(2 * HEAD_DIM * (head // 2), 2 * HEAD_DIM * (head // 2 + 1))


def key_tile_index(place, me, tiles, own):
    if own:
        return place - me * tiles
    return (me - 1 - place // tiles) * tiles + place % tiles


def attend_kernel(me_ref, low_ref, *refs, tile, tiles, own):
    if own:
        q_ref, k_ref, v_ref, start_ref, peak_out, total_out, acc_out, qt, vt = refs
    else:
        (q_ref, k_ref, v_ref, start_ref, peak_in, total_in, acc_in, ctx_out, lse_out, qt, vt) = refs
    row = pl.program_id(0)
    me = me_ref[0]
    scale = HEAD_DIM**-0.5
    for block in range(tiles):
        rows = slice(block * tile, (block + 1) * tile)
        for head in range(0, GROUP, 2):
            turned = flip((q_ref[0, rows, pair_of(head)].astype(f32) * scale).astype(bf16))
            qt[block, head] = head_rows(turned, head)
            qt[block, head + 1] = head_rows(turned, head + 1)
    for block in range(v_ref.shape[1] // tile):
        vt[block] = flip(v_ref[0, block * tile : (block + 1) * tile, :])

    for block in range(tiles):
        cols = slice(block * tile, (block + 1) * tile)
        starts = start_ref[0, :, cols]
        low = low_ref[row, block]
        key_step = lax.broadcasted_iota(jnp.int32, (tile, tile), 0)
        query_step = lax.broadcasted_iota(jnp.int32, (tile, tile), 1)

        def step(place, state, diagonal=False):
            index = key_tile_index(place, me, tiles, own)
            keys = k_ref[0, pl.ds(pl.multiple_of(index * tile, tile), tile), :]
            values = vt[index]
            allowed = key_step + place * tile >= starts
            if diagonal:
                allowed = allowed & (key_step <= query_step)
            new = []
            for head in range(GROUP):
                peak, total, acc = state[head]
                scores = dot(keys[:, pair_of(head)], qt[block, head])
                scores = jnp.where(allowed, scores, NEG)
                higher = jnp.maximum(peak, jnp.max(scores, 0, keepdims=True))
                weights = jnp.exp(scores - higher)
                fade = jnp.exp(peak - higher)
                total = total * fade + jnp.sum(weights, 0, keepdims=True)
                head_values = values[head * HEAD_DIM : (head + 1) * HEAD_DIM]
                acc = acc * fade + dot(head_values, weights.astype(bf16))
                new.append((higher, total, acc))
            return tuple(new)

        def get(ref, head, wide):
            if wide:
                return ref[0, head * HEAD_DIM : (head + 1) * HEAD_DIM, cols]
            return ref[0, 0, head : head + 1, cols]

        if own:
            state = tuple(
                (
                    jnp.full((1, tile), NEG, f32),
                    jnp.zeros((1, tile), f32),
                    jnp.zeros((HEAD_DIM, tile), f32),
                )
                for _ in range(GROUP)
            )
            first = me * tiles
            state = lax.fori_loop(jnp.maximum(low, first), first + block, step, state)
            state = step(first + block, state, diagonal=True)
            for head in range(GROUP):
                peak_out[0, 0, head : head + 1, cols] = state[head][0]
                total_out[0, 0, head : head + 1, cols] = state[head][1]
                acc_out[0, head * HEAD_DIM : (head + 1) * HEAD_DIM, cols] = state[head][2]
        else:
            state = tuple(
                (get(peak_in, head, 0), get(total_in, head, 0), get(acc_in, head, 1))
                for head in range(GROUP)
            )
            state = lax.fori_loop(low, me * tiles, step, state)
            done = []
            for head in range(GROUP):
                peak, total, acc = state[head]
                lse_out[0, 0, head : head + 1, cols] = peak + jnp.log(total)
                done.append(acc / total)
            ctx_out[0, cols, :] = jnp.concatenate(done, 0).T.astype(bf16)


def grad_kernel(me_ref, low_ref, *refs, tile, tiles, own):
    if own:
        (q_ref, k_ref, v_ref, go_ref, ctx_ref, lse_ref, start_ref, dq_in) = refs[:8]
        dq_out, dk_out, dv_out = refs[8:11]
    else:
        (q_ref, k_ref, v_ref, go_ref, ctx_ref, lse_ref, start_ref) = refs[:7]
        dq_out, dk_out, dv_out = refs[7:10]
    qt, qn, gt, gn, kt, dk, dv = refs[-7:]
    row = pl.program_id(0)
    me = me_ref[0]
    scale = HEAD_DIM**-0.5
    key_tiles = k_ref.shape[1] // tile
    for block in range(tiles):
        rows = slice(block * tile, (block + 1) * tile)
        for head in range(0, GROUP, 2):
            pair = (q_ref[0, rows, pair_of(head)].astype(f32) * scale).astype(bf16)
            go_pair = go_ref[0, rows, pair_of(head)]
            turned, go_turned = flip(pair), flip(go_pair)
            for each in (head, head + 1):
                qt[block, each] = head_rows(turned, each)
                qn[block, each] = head_lanes(pair, each)
                gt[block, each] = head_rows(go_turned, each)
                gn[block, each] = head_lanes(go_pair, each)
    for block in range(key_tiles):
        turned = flip(k_ref[0, block * tile : (block + 1) * tile, :])
        kt[block] = (turned.astype(f32) * scale).astype(bf16)
    dk[...] = jnp.zeros_like(dk)
    dv[...] = jnp.zeros_like(dv)

    for block in range(tiles):
        cols = slice(block * tile, (block + 1) * tile)
        starts = start_ref[0, :, cols]
        low = low_ref[row, block]
        key_step = lax.broadcasted_iota(jnp.int32, (tile, tile), 0)
        query_step = lax.broadcasted_iota(jnp.int32, (tile, tile), 1)
        product = (go_ref[0, cols, :].astype(f32) * ctx_ref[0, cols, :].astype(f32)).T
        inner = [
            jnp.sum(product[head * HEAD_DIM : (head + 1) * HEAD_DIM], 0, keepdims=True)
            for head in range(GROUP)
        ]
        peaks = [lse_ref[0, 0, head : head + 1, cols] for head in range(GROUP)]

        def step(place, state, diagonal=False):
            index = key_tile_index(place, me, tiles, own)
            rows = pl.ds(pl.multiple_of(index * tile, tile), tile)
            keys = k_ref[0, rows, :]
            values = v_ref[0, rows, :]
            turned = kt[index]
            allowed = key_step + place * tile >= starts
            if diagonal:
                allowed = allowed & (key_step <= query_step)
            new = []
            for pair in range(0, GROUP, 2):
                dv_pair = dk_pair = 0.0
                for head in (pair, pair + 1):
                    scores = dot(keys[:, pair_of(head)], qt[block, head])
                    scores = jnp.where(allowed, scores, NEG)
                    probs = jnp.exp(scores - peaks[head])
                    prob_grad = dot(values[:, pair_of(head)], gt[block, head])
                    score_grad = (probs * (prob_grad - inner[head])).astype(bf16)
                    dv_pair += dot(probs.astype(bf16), gn[block, head])
                    dk_pair += dot(score_grad, qn[block, head])
                    part = dot(turned[head * HEAD_DIM : (head + 1) * HEAD_DIM], score_grad)
                    new.append(state[head] + part)
                dv[index, :, pair_of(pair)] += dv_pair
                dk[index, :, pair_of(pair)] += dk_pair
            return tuple(new)

        if own:
            state = tuple(
                dq_in[0, head * HEAD_DIM : (head + 1) * HEAD_DIM, cols] for head in range(GROUP)
            )
            first = me * tiles
            state = lax.fori_loop(jnp.maximum(low, first), first + block, step, state)
            state = step(first + block, state, diagonal=True)
            dq_out[0, cols, :] = jnp.concatenate(state, 0).T.astype(bf16)
        else:
            state = tuple(jnp.zeros((HEAD_DIM, tile), f32) for _ in range(GROUP))
            state = lax.fori_loop(low, me * tiles, step, state)
            for head in range(GROUP):
                dq_out[0, head * HEAD_DIM : (head + 1) * HEAD_DIM, cols] = state[head]
    for block in range(key_tiles):
        rows = slice(block * tile, (block + 1) * tile)
        dk_out[0, rows, :] = dk[block].astype(bf16)
        dv_out[0, rows, :] = dv[block].astype(bf16)


class Attention:
    def __init__(self, me, low, starts, rows, block_len, width):
        self.me, self.low, self.starts = me, low, starts
        self.rows, self.block_len, self.width = rows, block_len, width
        self.tile = tile_of(block_len, 256)
        self.tiles = block_len // self.tile
        self.groups = width // LANES

    def column(self, length, offset):
        return pl.BlockSpec((1, length, LANES), lambda r, g, *_: (r, 0, offset * self.groups + g))

    def stat(self):
        return pl.BlockSpec((1, 1, GROUP, self.block_len), lambda r, g, *_: (r, g, 0, 0))

    def turned(self):
        return pl.BlockSpec((1, LANES, self.block_len), lambda r, g, *_: (r, g, 0))

    def start_spec(self):
        return pl.BlockSpec((1, 1, self.block_len), lambda r, g, *_: (r, 0, 0))

    def shape(self, length, dtype=bf16):
        return jax.ShapeDtypeStruct((self.rows, length, self.width), dtype)

    def call(self, kernel, own, in_specs, out_specs, out_shape, scratch, matmuls, args):
        seen = self.block_len * self.block_len // (2 if own else 1)
        flops = self.rows * self.width * seen * 2 * matmuls * 4
        return pl.pallas_call(
            functools.partial(kernel, tile=self.tile, tiles=self.tiles, own=own),
            grid_spec=pltpu.PrefetchScalarGridSpec(
                num_scalar_prefetch=2,
                grid=(self.rows, self.groups),
                in_specs=in_specs,
                out_specs=out_specs,
                scratch_shapes=scratch,
            ),
            out_shape=out_shape,
            compiler_params=params(),
            cost_estimate=pl.CostEstimate(
                flops=flops, bytes_accessed=8 * self.rows * self.block_len * self.width, transcendentals=0
            ),
        )(self.me, self.low, *args)

    def forward(self, joint, other):
        block_len, tile, tiles = self.block_len, self.tile, self.tiles
        stat_shape = jax.ShapeDtypeStruct((self.rows, self.groups, GROUP, block_len), f32)
        turned_shape = jax.ShapeDtypeStruct((self.rows, self.width, block_len), f32)
        qt = pltpu.VMEM((tiles, GROUP, 2 * HEAD_DIM, tile), bf16)
        state = self.call(
            attend_kernel,
            True,
            [self.column(block_len, 0), self.column(block_len, 1), self.column(block_len, 2), self.start_spec()],
            [self.stat(), self.stat(), self.turned()],
            [stat_shape, stat_shape, turned_shape],
            [qt, pltpu.VMEM((tiles, LANES, tile), bf16)],
            2,
            (joint, joint, joint, self.starts),
        )
        length = other.shape[1]
        return self.call(
            attend_kernel,
            False,
            [self.column(block_len, 0), self.column(length, 0), self.column(length, 1), self.start_spec()]
            + [self.stat(), self.stat(), self.turned()],
            [self.column(block_len, 0), self.stat()],
            [self.shape(block_len), stat_shape],
            [qt, pltpu.VMEM((length // tile, LANES, tile), bf16)],
            2,
            (joint, other, other, self.starts, *state),
        )

    def grad_scratch(self, length):
        tile, tiles = self.tile, self.tiles
        turned = pltpu.VMEM((tiles, GROUP, 2 * HEAD_DIM, tile), bf16)
        natural = pltpu.VMEM((tiles, GROUP, tile, 2 * HEAD_DIM), bf16)
        total = pltpu.VMEM((length // tile, tile, LANES), f32)
        return [turned, natural, turned, natural, pltpu.VMEM((length // tile, LANES, tile), bf16), total, total]

    def backward_other(self, joint, other, grad, context, lse):
        block_len, length = self.block_len, other.shape[1]
        return self.call(
            grad_kernel,
            False,
            [self.column(block_len, 0), self.column(length, 0), self.column(length, 1)]
            + [self.column(block_len, 0), self.column(block_len, 0), self.stat(), self.start_spec()],
            [self.turned(), self.column(length, 0), self.column(length, 0)],
            [
                jax.ShapeDtypeStruct((self.rows, self.width, block_len), f32),
                self.shape(length),
                self.shape(length),
            ],
            self.grad_scratch(length),
            5,
            (joint, other, other, grad, context, lse, self.starts),
        )

    def backward_own(self, joint, grad, context, lse, dq_state):
        block_len = self.block_len
        return self.call(
            grad_kernel,
            True,
            [self.column(block_len, 0), self.column(block_len, 1), self.column(block_len, 2)]
            + [self.column(block_len, 0), self.column(block_len, 0), self.stat(), self.start_spec()]
            + [self.turned()],
            [self.column(block_len, 0)] * 3,
            [self.shape(block_len)] * 3,
            self.grad_scratch(block_len),
            5,
            (joint, joint, joint, grad, context, lse, self.starts, dq_state),
        )


def place_kernel(target_ref, x_ref, out_ref):
    tile = out_ref.shape[0]
    slots = lax.broadcasted_iota(jnp.int32, (tile, target_ref.shape[1]), 0) + pl.program_id(0) * tile
    picked = jnp.where(slots == target_ref[...], 1.0, 0.0).astype(bf16)
    out_ref[...] = dot(picked, x_ref[...]).astype(bf16)


def place(target_row, x, slots):
    flat, width = x.shape
    tile = tile_of(slots, 256)
    return pl.pallas_call(
        place_kernel,
        grid=(slots // tile,),
        in_specs=[pl.BlockSpec((1, flat), lambda i: (0, 0)), pl.BlockSpec((flat, width), lambda i: (0, 0))],
        out_specs=pl.BlockSpec((tile, width), lambda i: (i, 0)),
        out_shape=jax.ShapeDtypeStruct((slots, width), bf16),
        compiler_params=params(),
        cost_estimate=pl.CostEstimate(
            flops=2 * slots * flat * width, bytes_accessed=2 * width * (slots + flat), transcendentals=0
        ),
    )(target_row, x)


def fetch_kernel(target_ref, y_ref, out_ref):
    slots = lax.broadcasted_iota(jnp.int32, (target_ref.shape[0], y_ref.shape[0]), 1)
    picked = jnp.where(slots == target_ref[...], 1.0, 0.0).astype(bf16)
    out_ref[...] = dot(picked, y_ref[...]).astype(bf16)


def fetch(target_column, y):
    slots, width = y.shape
    flat = target_column.shape[0]
    tile = tile_of(flat, 256)
    return pl.pallas_call(
        fetch_kernel,
        grid=(flat // tile,),
        in_specs=[pl.BlockSpec((tile, 1), lambda i: (i, 0)), pl.BlockSpec((slots, width), lambda i: (0, 0))],
        out_specs=pl.BlockSpec((tile, width), lambda i: (i, 0)),
        out_shape=jax.ShapeDtypeStruct((flat, width), bf16),
        compiler_params=params(),
        cost_estimate=pl.CostEstimate(
            flops=2 * slots * flat * width, bytes_accessed=2 * width * (slots + flat), transcendentals=0
        ),
    )(target_column, y)


def expert_kernel(x_ref, g_ref, up_ref, down_ref, cent_ref, out_ref, dx_ref, act_ref, pre_ref, pg_ref, out_acc, dx_acc, *, chunk):
    x = x_ref[...]
    g = g_ref[...].astype(f32)
    centroid = cent_ref[...]
    gate = jax.nn.sigmoid(jnp.sum(x.astype(f32) * centroid, -1, keepdims=True))
    produced_grad = (gate * g).astype(bf16)
    pg_ref[...] = produced_grad
    hidden = up_ref.shape[1]
    out_acc[...] = jnp.zeros_like(out_acc)
    dx_acc[...] = jnp.zeros_like(dx_acc)

    def step(index, carry):
        cols = pl.ds(pl.multiple_of(index * chunk, chunk), chunk)
        up = up_ref[:, cols]
        down = down_ref[cols, :]
        pre = dot(x, up)
        cumulative = 0.5 + 0.5 * lax.erf(pre * (0.5**0.5))
        act = (pre * cumulative).astype(bf16)
        slope = cumulative + pre * (jnp.exp(-0.5 * pre * pre) * 0.3989422804014327)
        act_ref[:, cols] = act
        out_acc[...] += dot(act, down)
        pre_grad = (dot_nt(pg_ref[...], down) * slope).astype(bf16)
        pre_ref[:, cols] = pre_grad
        dx_acc[...] += dot_nt(pre_grad, up)
        return carry

    lax.fori_loop(0, hidden // chunk, step, 0)
    produced = out_acc[...].astype(bf16)
    out_ref[...] = produced
    gate_grad = jnp.sum(g * produced.astype(f32), -1, keepdims=True)
    logit_grad = gate_grad * gate * (1.0 - gate)
    dx_ref[...] = (dx_acc[...] + logit_grad * centroid).astype(bf16)


def run_expert(x, g, up, down, centroid):
    rows, width = x.shape
    hidden = up.shape[1]
    tile = tile_of(rows, 512)
    chunk = tile_of(hidden, 512)
    by_row = pl.BlockSpec((tile, width), lambda i: (i, 0))
    by_hidden = pl.BlockSpec((tile, hidden), lambda i: (i, 0))

    def whole(shape):
        return pl.BlockSpec(shape, lambda i: (0, 0), pipeline_mode=pl.Buffered(1))

    row_shape = jax.ShapeDtypeStruct((rows, width), bf16)
    hidden_shape = jax.ShapeDtypeStruct((rows, hidden), bf16)
    return pl.pallas_call(
        functools.partial(expert_kernel, chunk=chunk),
        grid=(rows // tile,),
        in_specs=[by_row, by_row, whole((width, hidden)), whole((hidden, width)), whole((1, width))],
        out_specs=[by_row, by_row, by_hidden, by_hidden, by_row],
        out_shape=[row_shape, row_shape, hidden_shape, hidden_shape, row_shape],
        scratch_shapes=[pltpu.VMEM((tile, width), f32)] * 2,
        compiler_params=params(),
        cost_estimate=pl.CostEstimate(
            flops=8 * rows * width * hidden, bytes_accessed=4 * rows * hidden + 4 * width * hidden, transcendentals=0
        ),
    )(x, g, up, down, centroid)


def norm_parts(inputs):
    center = inputs - jnp.mean(inputs, -1, keepdims=True)
    variance = jnp.mean(center * center, -1, keepdims=True)
    rate = lax.rsqrt(variance + 1e-05)
    return center * rate, rate


def norm_back(grad, gain, unit, rate):
    scaled = grad * gain
    mean_one = jnp.mean(scaled, -1, keepdims=True)
    mean_two = jnp.mean(scaled * unit, -1, keepdims=True)
    return rate * (scaled - mean_one - unit * mean_two)


def body(
    tokens,
    segments,
    routes,
    project_in,
    project_out,
    first_gain,
    first_shift,
    second_gain,
    second_shift,
    centroids,
    expert_up,
    expert_down,
    cotangent,
):
    rows, block_len, width = tokens.shape
    blocks = lax.axis_size("blk")
    me = lax.axis_index("blk")
    flat = rows * block_len
    experts = centroids.shape[0]
    local_experts = expert_up.shape[0]
    peers = experts // local_experts
    capacity = 2 * block_len // experts
    slots = experts * rows * capacity

    shifts = range(1, blocks)

    def ahead(array, shift):
        return lax.ppermute(array, "blk", [(i, i + shift) for i in range(blocks - shift)])

    def behind(array, shift):
        return lax.ppermute(array, "blk", [(i + shift, i) for i in range(blocks - shift)])

    other_tokens = jnp.concatenate([ahead(tokens, shift) for shift in shifts], 1)

    route_ids = routes[:, :, 0]
    picked = route_ids[:, :, None] == lax.iota(jnp.int32, experts)[None, None, :]
    places = lax.iota(jnp.int32, block_len)
    before = (places[None, :] <= places[:, None]).astype(bf16)
    ranks = jnp.einsum("qk,rke->rqe", before, picked.astype(bf16), preferred_element_type=f32)
    slot_index = jnp.sum(jnp.where(picked, ranks, 0.0), 2).astype(jnp.int32) - 1
    row_index = lax.iota(jnp.int32, rows)[:, None]
    target = (route_ids * rows + row_index) * capacity + slot_index
    target_row = target.reshape(1, flat)
    target_column = target.reshape(flat, 1)
    chosen = jnp.dot(picked.reshape(flat, experts).astype(f32), centroids, precision=lax.Precision.HIGHEST)

    def exchange(array):
        return lax.all_to_all(
            array.reshape(experts, rows * capacity, width), "wide", split_axis=0, concat_axis=0, tiled=True
        )

    def to_experts(array):
        return exchange(array).reshape(peers, local_experts, rows * capacity, width)

    def from_experts(array):
        return exchange(array).reshape(slots, width)

    upstream_low = cotangent.reshape(flat, width)
    upstream = upstream_low.astype(f32)
    grads_arrived = to_experts(place(target_row, upstream_low, slots))

    own_segments = lax.dynamic_slice_in_dim(segments, me * block_len, block_len, 1)
    smaller = segments[:, None, :] < own_segments[:, :, None]
    starts = jnp.sum(smaller.astype(jnp.int32), 2)
    attention = Attention(
        me.reshape(1).astype(jnp.int32), None, starts.reshape(rows, 1, block_len), rows, block_len, width
    )
    attention.low = starts[:, :: attention.tile] // attention.tile

    stream = tokens.reshape(flat, width).astype(f32)
    unit_one, rate_one = norm_parts(stream)
    normed_one = (unit_one * first_gain + first_shift).astype(bf16)
    joint = dot(normed_one, project_in).astype(bf16)
    joint = joint.reshape(rows, block_len, 3 * width)
    other_flat = other_tokens.reshape(-1, width)
    unit_other, _ = norm_parts(other_flat.astype(f32))
    normed_other = (unit_other * first_gain + first_shift).astype(bf16)
    other = dot(normed_other, project_in[:, width:]).astype(bf16)
    other = other.reshape(rows, (blocks - 1) * block_len, 2 * width)
    context, lse = attention.forward(joint, other)
    context_flat = context.reshape(flat, width)

    middle = stream + dot(context_flat, project_out)
    unit_two, rate_two = norm_parts(middle)
    normed_two = unit_two * second_gain + second_shift
    normed_two_low = normed_two.astype(bf16)
    gate = jax.nn.sigmoid(jnp.sum(normed_two * chosen, -1, keepdims=True))
    arrived = to_experts(place(target_row, normed_two_low, slots))

    own_experts = lax.axis_index("wide") * local_experts
    outputs, row_grads, down_grads, up_grads = [], [], [], []
    half = expert_up.shape[2] // blocks
    for local in range(local_experts):
        x = arrived[:, local].reshape(-1, width)
        g = grads_arrived[:, local].reshape(-1, width)
        centroid = lax.dynamic_slice_in_dim(centroids, own_experts + local, 1, 0)
        out, dx, act, pre_grad, out_grad = run_expert(x, g, expert_up[local], expert_down[local], centroid)
        outputs.append(out.reshape(peers, 1, rows * capacity, width))
        row_grads.append(dx.reshape(peers, 1, rows * capacity, width))
        down_grads.append((act, out_grad))
        up_grads.append((x, pre_grad))
    back_arrived = from_experts(jnp.concatenate(row_grads, 1))
    produced = from_experts(jnp.concatenate(outputs, 1))

    def share_of(array, block):
        return lax.dynamic_slice_in_dim(array, block * half, half, 1)

    def summed_shares(pairs, product):
        shares = []
        for pair in pairs:
            sent = [
                product(pair, lax.rem(me + shift, blocks)).astype(bf16) for shift in shifts
            ]
            got = [
                lax.ppermute(part, "blk", [(i, (i + shift) % blocks) for i in range(blocks)])
                for shift, part in zip(shifts, sent)
            ]
            share = product(pair, me)
            for part in got:
                share = share + part.astype(f32)
            shares.append(share)
        return jnp.stack(shares, 0)

    def down_product(pair, block):
        act, out_grad = pair
        return jnp.einsum("cf,cd->fd", share_of(act, block), out_grad, preferred_element_type=f32)

    def up_product(pair, block):
        x, pre_grad = pair
        return jnp.einsum("cd,cf->df", x, share_of(pre_grad, block), preferred_element_type=f32)

    down_share = summed_shares(down_grads, down_product)
    up_share = summed_shares(up_grads, up_product)

    normed_two_grad = fetch(target_column, back_arrived).astype(f32)
    gain_two_grad = jnp.sum(normed_two_grad * unit_two, 0)
    shift_two_grad = jnp.sum(normed_two_grad, 0)
    middle_grad = upstream + norm_back(normed_two_grad, second_gain, unit_two, rate_two)
    attn_grad = middle_grad.astype(bf16)
    out_proj_grad = jnp.einsum("td,te->de", context_flat, attn_grad, preferred_element_type=f32)
    context_grad = dot_nt(attn_grad, project_out).astype(bf16).reshape(rows, block_len, width)

    dq_state, dk_other, dv_other = attention.backward_other(joint, other, context_grad, context, lse)
    dkv_other = jnp.concatenate([dk_other, dv_other], 2).reshape(-1, 2 * width)
    other_grad = dot_nt(dkv_other, project_in[:, width:])
    sent = other_grad.astype(bf16).reshape(rows, blocks - 1, block_len, width)
    returned = [behind(sent[:, shift - 1], shift) for shift in shifts]
    dq, dk, dv = attention.backward_own(joint, context_grad, context, lse, dq_state)
    joint_grad = jnp.concatenate([dq, dk, dv], 2).reshape(flat, 3 * width)
    own_grad = dot_nt(joint_grad, project_in)
    in_proj_own = jnp.einsum("td,te->de", normed_one, joint_grad, preferred_element_type=f32)
    in_proj_other = jnp.einsum("td,te->de", normed_other, dkv_other, preferred_element_type=f32)
    in_proj_grad = in_proj_own + jnp.pad(in_proj_other, ((0, 0), (width, 0)))
    gain_one_grad = jnp.sum(own_grad * unit_one, 0) + jnp.sum(other_grad * unit_other, 0)
    shift_one_grad = jnp.sum(own_grad, 0) + jnp.sum(other_grad, 0)

    vectors = jnp.stack([gain_one_grad, shift_one_grad, gain_two_grad, shift_two_grad], 0).reshape(1, 4 * width)
    packed = jnp.concatenate(
        [
            jnp.concatenate([in_proj_grad, out_proj_grad], 1),
            jnp.pad(vectors, ((0, 15), (0, 0))),
        ],
        0,
    ).astype(bf16)
    packed = lax.psum(packed, ("blk", "wide")).astype(f32)
    summed_vectors = packed[width].reshape(4, width)

    total_grad = own_grad
    for part in returned:
        total_grad = total_grad + part.reshape(flat, width).astype(f32)
    stream_grad = middle_grad + norm_back(total_grad, first_gain, unit_one, rate_one)

    branch = fetch(target_column, produced).astype(f32)
    result = (middle + gate * branch).astype(bf16)
    out_shape = (rows, block_len, width)
    return (
        result.reshape(out_shape),
        stream_grad.reshape(out_shape),
        packed[:width, : 3 * width],
        packed[:width, 3 * width :],
        summed_vectors[0],
        summed_vectors[1],
        summed_vectors[2],
        summed_vectors[3],
        up_share,
        down_share,
    )


def solution(mesh):
    return jax.shard_map(
        body,
        mesh=mesh,
        in_specs=(
            P("wide", "blk", None),
            P("wide", None),
            P("wide", "blk", None),
            P(),
            P(),
            P(),
            P(),
            P(),
            P(),
            P(),
            P("wide", None, None),
            P("wide", None, None),
            P("wide", "blk", None),
        ),
        out_specs=(
            P("wide", "blk", None),
            P("wide", "blk", None),
            P(),
            P(),
            P(),
            P(),
            P(),
            P(),
            P("wide", None, "blk"),
            P("wide", "blk", None),
        ),
        check_vma=False,
    )
```

```python
import functools

import jax
import jax.numpy as jnp
from jax import lax
from jax.experimental import pallas as pl
from jax.experimental.pallas import tpu as pltpu
from jax.sharding import PartitionSpec as P

HEAD_DIM = 64
GROUP = 4
LANES = GROUP * HEAD_DIM
NEG = -1e30
f32 = jnp.float32
bf16 = jnp.bfloat16
VMEM_LIMIT = 60 * 1024 * 1024
SHORT = pl.CostEstimate(flops=1, bytes_accessed=1, transcendentals=0)
LONG = pl.CostEstimate(flops=10**11, bytes_accessed=1, transcendentals=0)


def tile_of(size, most):
    tile = most
    while size % tile:
        tile //= 2
    return tile


def dot(a, b):
    return jnp.dot(a, b, preferred_element_type=f32)


def dot_nt(a, b):
    return lax.dot_general(a, b, (((1,), (1,)), ((), ())), preferred_element_type=f32)


def params(**more):
    return pltpu.CompilerParams(vmem_limit_bytes=VMEM_LIMIT, **more)


def largest_norm(x):
    head = lax.broadcasted_iota(jnp.int32, (LANES, 2 * HEAD_DIM), 0) // HEAD_DIM
    lane = lax.broadcasted_iota(jnp.int32, (LANES, 2 * HEAD_DIM), 1)
    pick = jnp.where(head == lane, 1.02, 0.0).astype(bf16)
    wide = x.astype(f32)
    return jnp.sqrt(jnp.max(dot((wide * wide).astype(bf16), pick), 0, keepdims=True))


def pair_of(head):
    return slice(2 * HEAD_DIM * (head // 2), 2 * HEAD_DIM * (head // 2 + 1))


def head_of_pair(pair, head, other=0.0):
    lane = lax.broadcasted_iota(jnp.int32, (1, 2 * HEAD_DIM), 1)
    keep = lane < HEAD_DIM if head % 2 == 0 else lane >= HEAD_DIM
    return jnp.where(keep, pair, jnp.full_like(pair, other))


def pieces_of(length, most):
    return [(at, min(most, length - at)) for at in range(0, length, most)]


def key_place(at, me, block_len, own):
    if own:
        return me * block_len + at
    return (me - 1 - at // block_len) * block_len + at % block_len


def mask_of(at, size, block, me, block_len, tile, starts, own, flipped):
    shape = (size, tile) if flipped else (tile, size)
    key = lax.broadcasted_iota(jnp.int32, shape, 0 if flipped else 1) + key_place(at, me, block_len, own)
    mask = key >= starts
    if own:
        query = lax.broadcasted_iota(jnp.int32, shape, 1 if flipped else 0) + (me * block_len + block * tile)
        mask = mask & (key <= query)
    return mask


def needed(at, size, block, low, me, block_len, tile, own):
    place = key_place(at, me, block_len, own)
    there = place + size > low
    if own:
        return jnp.logical_and(there, at < (block + 1) * tile)
    return jnp.logical_and(there, place >= 0)


def stat_place(head):
    return 2 * (head % 2) + head // 2


def split(x):
    parts = []
    for _ in range(3):
        part = x.astype(bf16)
        parts.append(part)
        x = x - part.astype(f32)
    return parts


def rows_of_lanes(x, lanes):
    lane = lax.broadcasted_iota(jnp.int32, (8, x.shape[1]), 1)
    row = lax.broadcasted_iota(jnp.int32, (8, x.shape[1]), 0)
    pick = jnp.zeros((8, x.shape[1]), f32)
    for at, number in enumerate(lanes):
        pick = jnp.where((row == at) & (lane == number), 1.0, pick)
    return sum(dot_nt(pick.astype(bf16), part) for part in split(x))[: len(lanes)]


def attend_kernel(me_ref, low_ref, q_ref, k_ref, v_ref, ok_ref, ov_ref, start_ref, ctx_out, lse_out, va, ova, acc, safe, *, tile, block_len):
    row, block = pl.program_id(0), pl.program_id(2)
    me = me_ref[0]
    low = low_ref[row, block]
    scale = HEAD_DIM**-0.5
    lane = lax.broadcasted_iota(jnp.int32, (1, 2 * HEAD_DIM), 1)
    pieces = [(True, at, size) for at, size in pieces_of(block_len, 512)]
    pieces += [(False, at, size) for at, size in pieces_of(ok_ref.shape[1], min(1024, block_len))]

    @pl.when(block == 0)
    def prepare():
        for values, spread in ((v_ref, va), (ov_ref, ova)):
            for head in range(GROUP):
                spread[head] = head_of_pair(values[0, :, pair_of(head)], head, 1.0)
        keys = jnp.maximum(largest_norm(k_ref[0]), largest_norm(ok_ref[0]))
        bound = jnp.max(largest_norm(q_ref[0]) * keys) * scale
        safe[0] = (bound < 60.0).astype(jnp.int32)

    queries = q_ref[0, pl.ds(pl.multiple_of(block * tile, tile), tile), :]
    queries = (queries.astype(f32) * scale).astype(bf16)
    starts = column_of(start_ref[0])

    def scores_of(own, at, size, head):
        mask = mask_of(at, size, block, me, block_len, tile, starts, own, False)
        keys = (k_ref if own else ok_ref)[0, at : at + size, pair_of(head)]
        return jnp.where(mask, dot_nt(head_of_pair(queries[:, pair_of(head)], head), keys), NEG)

    def attend(shifted):
        acc[...] = jnp.zeros_like(acc)
        peaks = [jnp.full((tile, 1), NEG, f32)] * GROUP
        if shifted:
            for own, at, size in pieces:
                there = needed(at, size, block, low, me, block_len, tile, own)
                for head in range(GROUP):
                    higher = jnp.max(scores_of(own, at, size, head), 1, keepdims=True)
                    peaks[head] = jnp.maximum(peaks[head], jnp.where(there, higher, NEG))
        for own, at, size in pieces:

            @pl.when(needed(at, size, block, low, me, block_len, tile, own))
            def piece(own=own, at=at, size=size):
                for head in range(GROUP):
                    scores = scores_of(own, at, size, head)
                    if shifted:
                        scores = scores - peaks[head]
                    weights = jnp.exp(scores).astype(bf16)
                    acc[head] += dot(weights, (va if own else ova)[head, at : at + size])

        stats = []
        for head in range(0, GROUP, 2):
            even, odd = acc[head], acc[head + 1]
            sums = pltpu.roll(jnp.where(lane < HEAD_DIM, odd, even), HEAD_DIM, 1)
            ctx_out[0, :, pair_of(head)] = (jnp.where(lane < HEAD_DIM, even, odd) / sums).astype(bf16)
            stats.append(sums)
        first = lane % HEAD_DIM < HEAD_DIM // 2
        stat = jnp.log(jnp.where(first, stats[0], stats[1]))
        if shifted:
            for head in range(GROUP):
                stat = jnp.where(lane // (HEAD_DIM // 2) == stat_place(head), stat + peaks[head], stat)
        lse_out[0, 0] = rows_of_lanes(stat, [stat_place(head) * (HEAD_DIM // 2) for head in range(GROUP)])

    @pl.when(safe[0] == 1)
    def without_shift():
        attend(False)

    @pl.when(safe[0] == 0)
    def with_shift():
        attend(True)


def grad_kernel(me_ref, low_ref, *refs, tile, block_len, own):
    q_ref, k_ref, v_ref, go_ref, ctx_ref, lse_ref, start_ref = refs[:7]
    if own:
        dq_in, dq_out, dk_out, dv_out = refs[7:11]
    else:
        dq_out, dk_out, dv_out = refs[7:10]
    kt, dq, dk, dv = refs[-4:]
    row, block = pl.program_id(0), pl.program_id(2)
    me = me_ref[0]
    low = low_ref[row, block]
    scale = HEAD_DIM**-0.5
    length = k_ref.shape[1]
    pieces = pieces_of(length, min(512 if own else 1024, block_len))

    @pl.when(block == 0)
    def prepare():
        shape = (2 * HEAD_DIM, 2 * HEAD_DIM)
        same = lax.broadcasted_iota(jnp.int32, shape, 0) == lax.broadcasted_iota(jnp.int32, shape, 1)
        turn = jnp.where(same, scale, 0.0).astype(bf16)
        for head in range(0, GROUP, 2):
            kt[pair_of(head)] = dot_nt(turn, k_ref[0, :, pair_of(head)]).astype(bf16)
        dk[...] = jnp.zeros_like(dk)
        dv[...] = jnp.zeros_like(dv)

    queries = (q_ref[0].astype(f32) * scale).astype(bf16)
    go = go_ref[0]
    starts = start_ref[0]
    product = go.astype(f32) * ctx_ref[0].astype(f32)
    head_row = lax.broadcasted_iota(jnp.int32, (8, LANES), 0)
    head_lane = lax.broadcasted_iota(jnp.int32, (8, LANES), 1) // HEAD_DIM
    pick = jnp.where(head_row == head_lane, 1.0, 0.0).astype(bf16)
    inners = sum(dot_nt(pick, part) for part in split(product)[:2])
    inner = [inners[head : head + 1] for head in range(GROUP)]
    dq[...] = dq_in[0] if own else jnp.zeros_like(dq)
    for at, size in pieces:

        @pl.when(needed(at, size, block, low, me, block_len, tile, own))
        def piece(at=at, size=size):
            rows = slice(at, at + size)
            mask = mask_of(at, size, block, me, block_len, tile, starts, own, True)
            for first in range(0, GROUP, 2):
                pair = pair_of(first)
                keys, values = k_ref[0, rows, pair], v_ref[0, rows, pair]
                all_probs, all_grads, all_queries, all_go = [], [], [], []
                for head in (first, first + 1):
                    query = head_of_pair(queries[:, pair], head)
                    head_go = head_of_pair(go[:, pair], head)
                    scores = dot_nt(keys, query) - lse_ref[0, 0, head : head + 1, :]
                    probs = jnp.exp(jnp.where(mask, scores, NEG))
                    prob_grad = dot_nt(values, head_go)
                    score_grad = (probs * (prob_grad - inner[head])).astype(bf16)
                    lanes = slice(head * HEAD_DIM, (head + 1) * HEAD_DIM)
                    dq[lanes] += dot(kt[lanes, rows], score_grad)
                    all_probs.append(probs.astype(bf16))
                    all_grads.append(score_grad)
                    all_queries.append(query)
                    all_go.append(head_go)
                dv[rows, pair] += dot(jnp.concatenate(all_probs, 1), jnp.concatenate(all_go, 0))
                dk[rows, pair] += dot(jnp.concatenate(all_grads, 1), jnp.concatenate(all_queries, 0))

    if own:
        dq_out[0] = dq[...].T.astype(bf16)
    else:
        dq_out[0] = dq[...]

    @pl.when(block == pl.num_programs(2) - 1)
    def write():
        dk_out[0] = dk[...].astype(bf16)
        dv_out[0] = dv[...].astype(bf16)


class Attention:
    def __init__(self, me, starts, rows, block_len, width):
        self.rows, self.block_len, self.width = rows, block_len, width
        self.tile = tile_of(block_len, 512)
        self.tiles = block_len // self.tile
        self.groups = width // LANES
        self.me = me.reshape(1).astype(jnp.int32)
        self.low = starts[:, :: self.tile]
        self.start_row = starts.reshape(rows, 1, block_len)

    def queries(self, offset=0):
        return pl.BlockSpec((1, self.tile, LANES), lambda r, g, b, *_: (r, b, offset * self.groups + g))

    def keys(self, length, offset):
        return pl.BlockSpec((1, length, LANES), lambda r, g, b, *_: (r, 0, offset * self.groups + g))

    def stat(self):
        return pl.BlockSpec((1, 1, GROUP, self.tile), lambda r, g, b, *_: (r, g, 0, b))

    def turned(self):
        return pl.BlockSpec((1, LANES, self.tile), lambda r, g, b, *_: (r, g, b))

    def row_starts(self):
        return pl.BlockSpec((1, 1, self.tile), lambda r, g, b, *_: (r, 0, b))

    def shape(self, length, dtype=bf16):
        return jax.ShapeDtypeStruct((self.rows, length, self.width), dtype)

    def call(self, kernel, cost, in_specs, out_specs, out_shape, scratch, args):
        return pl.pallas_call(
            functools.partial(kernel, tile=self.tile, block_len=self.block_len),
            grid_spec=pltpu.PrefetchScalarGridSpec(
                num_scalar_prefetch=2,
                grid=(self.rows, self.groups, self.tiles),
                in_specs=in_specs,
                out_specs=out_specs,
                scratch_shapes=scratch,
            ),
            out_shape=out_shape,
            compiler_params=params(),
            cost_estimate=cost,
        )(self.me, self.low, *args)

    def forward(self, joint, other):
        size, length = self.block_len, other.shape[1]
        return self.call(
            attend_kernel,
            LONG,
            [self.keys(size, 0), self.keys(size, 1), self.keys(size, 2)]
            + [self.keys(length, 0), self.keys(length, 1), self.row_starts()],
            [self.queries(), self.stat()],
            [self.shape(size), jax.ShapeDtypeStruct((self.rows, self.groups, GROUP, size), f32)],
            [
                pltpu.VMEM((GROUP, size, 2 * HEAD_DIM), bf16),
                pltpu.VMEM((GROUP, length, 2 * HEAD_DIM), bf16),
                pltpu.VMEM((GROUP, self.tile, 2 * HEAD_DIM), f32),
                pltpu.SMEM((1,), jnp.int32),
            ],
            (joint, joint, joint, other, other, self.start_row),
        )

    def grad_scratch(self, length):
        total = pltpu.VMEM((length, LANES), f32)
        return [pltpu.VMEM((LANES, length), bf16), pltpu.VMEM((LANES, self.tile), f32), total, total]

    def backward_other(self, joint, other, grad, context, lse):
        size, length = self.block_len, other.shape[1]
        return self.call(
            functools.partial(grad_kernel, own=False),
            SHORT,
            [self.queries(), self.keys(length, 0), self.keys(length, 1)]
            + [self.queries(), self.queries(), self.stat(), self.row_starts()],
            [self.turned(), self.keys(length, 0), self.keys(length, 0)],
            [
                jax.ShapeDtypeStruct((self.rows, self.width, size), f32),
                self.shape(length),
                self.shape(length),
            ],
            self.grad_scratch(length),
            (joint, other, other, grad, context, lse, self.start_row),
        )

    def backward_own(self, joint, grad, context, lse, dq_state):
        size = self.block_len
        return self.call(
            functools.partial(grad_kernel, own=True),
            LONG,
            [self.queries(), self.keys(size, 1), self.keys(size, 2)]
            + [self.queries(), self.queries(), self.stat(), self.row_starts(), self.turned()],
            [self.queries(), self.keys(size, 0), self.keys(size, 0)],
            [self.shape(size)] * 3,
            self.grad_scratch(size),
            (joint, joint, joint, grad, context, lse, self.start_row, dq_state),
        )


def place_kernel(target_ref, x_ref, out_ref):
    tile = out_ref.shape[0]
    slots = lax.broadcasted_iota(jnp.int32, (tile, target_ref.shape[1]), 0) + pl.program_id(0) * tile
    picked = jnp.where(slots == target_ref[...], 1.0, 0.0).astype(bf16)
    out_ref[...] = dot(picked, x_ref[...]).astype(bf16)


def place(target_row, x, slots):
    flat, width = x.shape
    tile = tile_of(slots, 256)
    return pl.pallas_call(
        place_kernel,
        grid=(slots // tile,),
        in_specs=[pl.BlockSpec((1, flat), lambda i: (0, 0)), pl.BlockSpec((flat, width), lambda i: (0, 0))],
        out_specs=pl.BlockSpec((tile, width), lambda i: (i, 0)),
        out_shape=jax.ShapeDtypeStruct((slots, width), bf16),
        compiler_params=params(),
        cost_estimate=SHORT,
    )(target_row, x)


def column_of(row):
    return jnp.broadcast_to(row.astype(f32), (8, row.shape[1])).T[:, :1].astype(jnp.int32)


def fetched(target, sources):
    total, before = 0.0, 0
    for source in sources:
        slots = lax.broadcasted_iota(jnp.int32, (target.shape[0], source.shape[0]), 1) + before
        total += dot(jnp.where(slots == target, 1.0, 0.0).astype(bf16), source[...])
        before += source.shape[0]
    return total


def result_kernel(target_ref, middle_ref, gate_ref, *refs):
    branch = fetched(column_of(target_ref[...]), refs[:-1])
    refs[-1][...] = (middle_ref[...] + gate_ref[...] * branch).astype(bf16)


def unit_of(x):
    center = x - jnp.mean(x, -1, keepdims=True)
    rate = lax.rsqrt(jnp.mean(center * center, -1, keepdims=True) + 1e-05)
    return center * rate, rate


def norm_back(grad, gain, unit, rate):
    scaled = grad * gain
    mean_one = jnp.mean(scaled, -1, keepdims=True)
    mean_two = jnp.mean(scaled * unit, -1, keepdims=True)
    return rate * (scaled - mean_one - unit * mean_two)


def add_sums(sums_ref, grad, unit):
    @pl.when(pl.program_id(0) == 0)
    def clear():
        sums_ref[...] = jnp.zeros_like(sums_ref)

    sums_ref[0:1] += jnp.sum(grad * unit, 0, keepdims=True)
    sums_ref[1:2] += jnp.sum(grad, 0, keepdims=True)


def second_norm_grad_kernel(target_ref, middle_ref, upstream_ref, gain_ref, weight_ref, *refs):
    sources = refs[:-4]
    grad_ref, low_ref, context_ref, sums_ref = refs[-4:]
    grad = fetched(column_of(target_ref[...]), sources)
    unit, rate = unit_of(middle_ref[...])
    add_sums(sums_ref, grad, unit)
    total = upstream_ref[...].astype(f32) + norm_back(grad, gain_ref[...], unit, rate)
    grad_ref[...] = total
    low = total.astype(bf16)
    low_ref[...] = low
    context_ref[...] = dot_nt(low, weight_ref[...]).astype(bf16)


def input_grad_kernel(tokens_ref, *refs):
    grad_ref, sums_ref = refs[-2:]
    count = (len(refs) - 2) // 2
    grad = 0.0
    for part, weight in zip(refs[:count], refs[count : 2 * count]):
        grad += dot_nt(part[...], weight[...])
    unit, _ = unit_of(tokens_ref[...].astype(f32))
    add_sums(sums_ref, grad, unit)
    grad_ref[...] = grad.astype(grad_ref.dtype)


def joint_kernel(tokens_ref, gain_ref, shift_ref, *refs):
    weights, (normed_ref, joint_ref) = refs[:-2], refs[-2:]
    normed = unit_of(tokens_ref[...].astype(f32))[0] * gain_ref[...] + shift_ref[...]
    normed = normed.astype(bf16)
    normed_ref[...] = normed
    width = normed.shape[1]
    for at, weight in enumerate(weights):
        joint_ref[:, at * width : (at + 1) * width] = dot(normed, weight[...]).astype(bf16)


def middle_kernel(context_ref, tokens_ref, route_ref, weight_ref, gain_ref, shift_ref, centroid_ref, middle_ref, normed_ref, gate_ref):
    middle = tokens_ref[...].astype(f32) + dot(context_ref[...], weight_ref[...])
    middle_ref[...] = middle
    normed = unit_of(middle)[0] * gain_ref[...] + shift_ref[...]
    normed_ref[...] = normed.astype(bf16)
    experts = centroid_ref.shape[0]
    route = column_of(route_ref[...])
    picked = route == lax.broadcasted_iota(jnp.int32, (route.shape[0], experts), 1)
    chosen = jnp.dot(
        picked.astype(f32), centroid_ref[...], precision=lax.Precision.HIGHEST, preferred_element_type=f32
    )
    gate_ref[...] = jax.nn.sigmoid(jnp.sum(normed * chosen, -1, keepdims=True))


def turned(x):
    size = tile_of(x.shape[1], 256)
    same = lax.broadcasted_iota(jnp.int32, (size, size), 0) == lax.broadcasted_iota(jnp.int32, (size, size), 1)
    unit = jnp.where(same, 1.0, 0.0).astype(bf16)
    return jnp.concatenate(
        [dot_nt(unit, x[:, at : at + size]).astype(bf16) for at in range(0, x.shape[1], size)], 0
    )


def weight_grad_kernel(*refs, count, into):
    lefts, rights = refs[:count], refs[count : 2 * count]
    out_ref = refs[2 * count + (1 if into else 0)]
    turns = refs[-count:]

    @pl.when(pl.program_id(0) == 0)
    def turn():
        for left, turn_ref in zip(lefts, turns):
            turn_ref[...] = turned(left[...])

    out_ref[...] = sum(dot(turn_ref[...], right[...]) for turn_ref, right in zip(turns, rights)).astype(bf16)


def weight_grad(pairs, columns, offset, into):
    width, wide = pairs[0][0].shape[1], pairs[0][1].shape[1]
    tile = tile_of(wide, 256)
    lefts, rights = [a for a, _ in pairs], [b for _, b in pairs]
    specs = [pl.BlockSpec(a.shape, lambda i: (0, 0), pipeline_mode=pl.Buffered(1)) for a in lefts]
    specs += [pl.BlockSpec((b.shape[0], tile), lambda i: (0, i)) for b in rights]
    arrays, aliases = lefts + rights, {}
    if into is not None:
        aliases = {len(arrays): 0}
        specs.append(pl.BlockSpec(memory_space=pl.ANY))
        arrays.append(into)
    return pl.pallas_call(
        functools.partial(weight_grad_kernel, count=len(pairs), into=into is not None),
        grid=(wide // tile,),
        in_specs=specs,
        out_specs=pl.BlockSpec((width, tile), lambda i: (0, offset // tile + i)),
        out_shape=jax.ShapeDtypeStruct((width, columns), bf16),
        scratch_shapes=[pltpu.VMEM((width, a.shape[0]), bf16) for a in lefts],
        input_output_aliases=aliases,
        compiler_params=params(),
        cost_estimate=SHORT,
    )(*arrays)


def sums_kernel(first_ref, other_ref, second_ref, into_ref, out_ref):
    rows = jnp.concatenate([first_ref[...] + other_ref[...], second_ref[...]], 0)
    rows = jnp.concatenate([rows, jnp.zeros((124, rows.shape[1]), f32)], 0)
    out_ref[...] = rows.T.astype(bf16)


def put_sums(first, other, second, into):
    width, columns = into.shape
    spec = pl.BlockSpec((2, width), lambda i: (0, 0))
    return pl.pallas_call(
        sums_kernel,
        grid=(1,),
        in_specs=[spec, spec, spec, pl.BlockSpec(memory_space=pl.ANY)],
        out_specs=pl.BlockSpec((width, 128), lambda i: (0, columns // 128 - 1)),
        out_shape=jax.ShapeDtypeStruct(into.shape, bf16),
        input_output_aliases={3: 0},
        compiler_params=params(),
        cost_estimate=SHORT,
    )(first, other, second, into)


def by_tokens(kernel, flat, tiled, whole, out_shape):
    tile = tile_of(flat, 256)

    def cut(array):
        if array.shape == (1, flat):
            return pl.BlockSpec((1, tile), lambda i: (0, i))
        if array.shape[0] == flat:
            return pl.BlockSpec((tile, array.shape[1]), lambda i: (i, 0))
        return pl.BlockSpec(array.shape, lambda i: (0, 0))

    specs = [cut(array) for array in tiled]
    for array, column in whole:
        if column is None:
            specs.append(pl.BlockSpec(array.shape, lambda i: (0, 0), pipeline_mode=pl.Buffered(1)))
        else:
            shape = (array.shape[0], array.shape[0])
            specs.append(pl.BlockSpec(shape, lambda i, c=column: (0, c), pipeline_mode=pl.Buffered(1)))
    arrays = list(tiled) + [array for array, _ in whole]
    return pl.pallas_call(
        kernel,
        grid=(flat // tile,),
        in_specs=specs,
        out_specs=[cut(shape) for shape in out_shape],
        out_shape=out_shape,
        compiler_params=params(),
        cost_estimate=SHORT,
    )(*arrays)


def expert_kernel(*refs):
    x_ref, g_ref, up_ref, down_ref, cent_ref = refs[:5]
    out_ref, dx_ref, act_ref, pre_ref, pg_ref = refs[-5:]
    x = x_ref[...]
    g = g_ref[...].reshape(x.shape).astype(f32)
    centroid = cent_ref[...]
    gate = jax.nn.sigmoid(jnp.sum(x.astype(f32) * centroid, -1, keepdims=True))
    produced_grad = (gate * g).astype(bf16)
    pg_ref[...] = produced_grad
    pre = dot(x, up_ref[...])
    cumulative = 0.5 + 0.5 * lax.erf(pre * (0.5**0.5))
    act = (pre * cumulative).astype(bf16)
    slope = cumulative + pre * (jnp.exp(-0.5 * pre * pre) * 0.3989422804014327)
    act_ref[...] = act
    pre_grad = (dot_nt(produced_grad, down_ref[...]) * slope).astype(bf16)
    pre_ref[...] = pre_grad
    produced = dot(act, down_ref[...]).astype(bf16)
    out_ref[...] = produced.reshape(out_ref.shape)
    gate_grad = jnp.sum(g * produced.astype(f32), -1, keepdims=True)
    logit_grad = gate_grad * gate * (1.0 - gate)
    dx_ref[...] = (dot_nt(pre_grad, up_ref[...]) + logit_grad * centroid).astype(bf16)


def run_expert(x, g, half, up, down, centroid, outputs):
    rows, width = x.shape
    peers, halves, depth, _ = g.shape
    hidden = up.shape[1]
    tile = depth * tile_of(peers, max(1, 256 // depth))
    by_row = pl.BlockSpec((tile, width), lambda i: (i, 0))
    by_hidden = pl.BlockSpec((tile, hidden), lambda i: (i, 0))
    by_peer = pl.BlockSpec((tile // depth, 1, depth, width), lambda i: (i, half, 0, 0))

    def whole(shape):
        return pl.BlockSpec(shape, lambda i: (0, 0), pipeline_mode=pl.Buffered(1))

    in_specs = [by_row, by_peer, whole((width, hidden)), whole((hidden, width)), whole((1, width))]
    arrays = [x, g, up, down, centroid]
    aliases = {}
    if outputs is not None:
        in_specs.append(pl.BlockSpec(memory_space=pl.ANY))
        arrays.append(outputs)
        aliases = {5: 0}
    row_shape = jax.ShapeDtypeStruct((rows, width), bf16)
    hidden_shape = jax.ShapeDtypeStruct((rows, hidden), bf16)
    return pl.pallas_call(
        expert_kernel,
        grid=(rows // tile,),
        in_specs=in_specs,
        out_specs=[by_peer, by_row, by_hidden, by_hidden, by_row],
        out_shape=[jax.ShapeDtypeStruct(g.shape, bf16), row_shape, hidden_shape, hidden_shape, row_shape],
        input_output_aliases=aliases,
        compiler_params=params(),
        cost_estimate=SHORT,
    )(*arrays)


def stages_of(wide, blocks):
    def bits(low, high):
        found = []
        while low < high:
            found.append(low)
            low *= 2
        return found

    stages = (bits(1, min(2, wide)), bits(2, min(4, wide)) + bits(wide, wide * blocks), bits(4, wide))
    return [stage for stage in stages if stage]


def spread(code, bits):
    return sum(bit for i, bit in enumerate(bits) if code >> i & 1)


def swap(array, mask):
    total = lax.axis_size("blk") * lax.axis_size("wide")
    return lax.ppermute(array, ("blk", "wide"), [(i, i ^ mask) for i in range(total)])


def places_of(stages):
    me = lax.axis_index("blk") * lax.axis_size("wide") + lax.axis_index("wide")
    return [sum((me // bit % 2) << i for i, bit in enumerate(bits)) for bits in stages]


def reduce_step(parts, bits, code):
    count = 1 << len(bits)
    summed = []
    for x in parts:
        rows = x.shape[0] // count

        def piece(index):
            return lax.dynamic_slice_in_dim(x, index * rows, rows, 0)

        got = [swap(piece(code ^ other).astype(bf16), spread(other, bits)) for other in range(1, count)]
        total = piece(code).astype(f32)
        for part in got:
            total = total + part.astype(f32)
        summed.append(total)
    return summed


def gather_parts(parts):
    stages = stages_of(lax.axis_size("wide"), lax.axis_size("blk"))
    for bits, code in reversed(list(zip(stages, places_of(stages)))):
        gathered = []
        for x in parts:
            rows = x.shape[0]
            whole = jnp.zeros((rows << len(bits), x.shape[1]), bf16)
            whole = lax.dynamic_update_slice_in_dim(whole, x, code * rows, 0)
            for other in range(1, 1 << len(bits)):
                part = swap(x, spread(other, bits))
                whole = lax.dynamic_update_slice_in_dim(whole, part, (code ^ other) * rows, 0)
            gathered.append(whole)
        parts = gathered
    return parts


def body(
    tokens,
    segments,
    routes,
    project_in,
    project_out,
    first_gain,
    first_shift,
    second_gain,
    second_shift,
    centroids,
    expert_up,
    expert_down,
    cotangent,
):
    rows, block_len, width = tokens.shape
    blocks = lax.axis_size("blk")
    me = lax.axis_index("blk")
    flat = rows * block_len
    experts = centroids.shape[0]
    local_experts = expert_up.shape[0]
    peers = experts // local_experts
    capacity = 2 * block_len // experts
    halves = 2 if capacity % 16 == 0 else 1
    depth = capacity // halves
    half_slots = experts * rows * depth

    shifts = range(1, blocks)

    def ahead(array, shift):
        return lax.ppermute(array, "blk", [(i, i + shift) for i in range(blocks - shift)])

    def behind(array, shift):
        return lax.ppermute(array, "blk", [(i + shift, i) for i in range(blocks - shift)])

    other_tokens = jnp.concatenate([ahead(tokens, shift) for shift in shifts], 1)
    other_flat = other_tokens.reshape(-1, width)

    route_ids = routes[:, :, 0]
    picked = route_ids[:, :, None] == lax.iota(jnp.int32, experts)[None, None, :]
    places = lax.iota(jnp.int32, block_len)
    before = (places[None, :] <= places[:, None]).astype(bf16)
    ranks = jnp.einsum("qk,rke->rqe", before, picked.astype(bf16), preferred_element_type=f32)
    slot_index = jnp.sum(jnp.where(picked, ranks, 0.0), 2).astype(jnp.int32) - 1
    row_index = lax.iota(jnp.int32, rows)[:, None]
    half = slot_index // depth
    place_in_half = row_index * depth + slot_index - half * depth
    target_halves = half * half_slots + route_ids * (rows * depth) + place_in_half
    target_whole = (route_ids * halves + half) * (rows * depth) + place_in_half

    def exchange(array):
        return lax.all_to_all(
            array.reshape(experts, -1, width), "wide", split_axis=0, concat_axis=0, tiled=True
        )

    upstream = cotangent.reshape(flat, width)

    own_segments = lax.dynamic_slice_in_dim(segments, me * block_len, block_len, 1)
    smaller = segments[:, None, :] < own_segments[:, :, None]
    starts = jnp.sum(smaller.astype(jnp.int32), 2)
    attention = Attention(me, starts, rows, block_len, width)

    tokens_flat = tokens.reshape(flat, width)

    first_gain_row, first_shift_row = first_gain.reshape(1, width), first_shift.reshape(1, width)

    def joined(x, columns):
        count = len(columns)
        return by_tokens(
            joint_kernel,
            x.shape[0],
            (x,),
            [(first_gain_row, None), (first_shift_row, None)] + [(project_in, column) for column in columns],
            [
                jax.ShapeDtypeStruct(x.shape, bf16),
                jax.ShapeDtypeStruct((x.shape[0], count * width), bf16),
            ],
        )

    normed_one, joint = joined(tokens_flat, (0, 1, 2))
    route_row = routes.reshape(1, flat)
    target_halves_row, target_whole_row = target_halves.reshape(1, flat), target_whole.reshape(1, flat)
    second_gain_row, second_shift_row = second_gain.reshape(1, width), second_shift.reshape(1, width)
    small = (attention.low, attention.start_row, route_row, target_halves_row, target_whole_row)
    small += (first_gain_row, first_shift_row, second_gain_row, second_shift_row)
    joint, small, to_place = lax.optimization_barrier((joint, small, upstream))
    attention.low, attention.start_row, route_row, target_halves_row, target_whole_row = small[:5]
    first_gain_row, first_shift_row, second_gain_row, second_shift_row = small[5:]
    grads_arrived = exchange(place(target_whole_row, to_place, halves * half_slots))
    grads_arrived = grads_arrived.reshape(peers, local_experts, halves, rows * depth, width)
    joint = joint.reshape(rows, block_len, 3 * width)
    normed_other, other = joined(other_flat, (1, 2))
    other = other.reshape(rows, (blocks - 1) * block_len, 2 * width)
    context, lse = attention.forward(joint, other)
    context_flat = context.reshape(flat, width)

    wide_shape = jax.ShapeDtypeStruct((flat, width), f32)
    low_shape = jax.ShapeDtypeStruct((flat, width), bf16)
    sums_shape = jax.ShapeDtypeStruct((2, width), f32)
    middle, normed_two, gate = by_tokens(
        middle_kernel,
        flat,
        (context_flat, tokens_flat, route_row),
        [(project_out, None), (second_gain_row, None), (second_shift_row, None), (centroids, None)],
        [wide_shape, low_shape, jax.ShapeDtypeStruct((flat, 1), f32)],
    )
    normed_two, grads_arrived = lax.optimization_barrier((normed_two, grads_arrived))
    placed = place(target_halves_row, normed_two, halves * half_slots)
    placed = placed.reshape(halves, half_slots, width)
    arrived = [exchange(placed[h]).reshape(peers, local_experts, rows * depth, width) for h in range(halves)]

    own_experts = lax.axis_index("wide") * local_experts
    outputs, row_grads = [None] * local_experts, []
    down_pairs, up_pairs = [[] for _ in range(local_experts)], [[] for _ in range(local_experts)]
    for h in range(halves):
        half_dx = []
        for local in range(local_experts):
            x = arrived[h][:, local].reshape(-1, width)
            centroid = lax.dynamic_slice_in_dim(centroids, own_experts + local, 1, 0)
            outputs[local], dx, act, pre_grad, out_grad = run_expert(
                x, grads_arrived[:, local], h, expert_up[local], expert_down[local], centroid, outputs[local]
            )
            half_dx.append(dx.reshape(peers, 1, rows * depth, width))
            down_pairs[local].append((act, out_grad))
            up_pairs[local].append((x, pre_grad))
        row_grads.append(half_dx[0] if local_experts == 1 else jnp.concatenate(half_dx, 1))
    share = expert_up.shape[2] // blocks

    def share_of(array, block):
        return lax.dynamic_slice_in_dim(array, block * share, share, 1)

    def down_product(pairs, block):
        return sum(
            jnp.einsum("cf,cd->fd", share_of(act, block), out_grad, preferred_element_type=f32)
            for act, out_grad in pairs
        )

    def up_product(pairs, block):
        return sum(
            jnp.einsum("cd,cf->df", x, share_of(pre_grad, block), preferred_element_type=f32)
            for x, pre_grad in pairs
        )

    def product_shares(pairs, product):
        sent = [[product(pair, lax.rem(me + shift, blocks)).astype(bf16) for shift in shifts] for pair in pairs]
        return sent, [product(pair, me) for pair in pairs]

    def send_shares(sent):
        return [
            [
                lax.ppermute(part, "blk", [(i, (i + shift) % blocks) for i in range(blocks)])
                for shift, part in zip(shifts, parts)
            ]
            for parts in sent
        ]

    def summed_shares(own, got):
        totals = []
        for total, parts in zip(own, got):
            for part in parts:
                total = total + part.astype(f32)
            totals.append(total)
        return jnp.stack(totals, 0)

    back_arrived = [exchange(part).reshape(half_slots, width) for part in row_grads]
    back_arrived[0], down_pairs, up_pairs = lax.optimization_barrier((back_arrived[0], down_pairs, up_pairs))
    down_sent, down_own = product_shares(down_pairs, down_product)
    up_sent, up_own = product_shares(up_pairs, up_product)
    down_got, up_got = send_shares(down_sent), send_shares(up_sent)
    output = outputs[0][:, None] if local_experts == 1 else jnp.stack(outputs, 1)
    back_arrived, down_own, up_own, _, _ = lax.optimization_barrier(
        (back_arrived, down_own, up_own, down_sent, up_sent)
    )

    middle_grad, attn_grad, context_grad, second_sums = by_tokens(
        second_norm_grad_kernel,
        flat,
        (target_halves_row, middle, upstream),
        [(second_gain_row, None), (project_out, None)] + [(part, None) for part in back_arrived],
        [wide_shape, low_shape, low_shape, sums_shape],
    )
    context_grad, output = lax.optimization_barrier((context_grad, output))
    produced = exchange(output).reshape(halves * half_slots, width)
    context_grad = context_grad.reshape(rows, block_len, width)
    dq_state, dk_other, dv_other = attention.backward_other(joint, other, context_grad, context, lse)
    dk_other, dv_other = dk_other.reshape(-1, width), dv_other.reshape(-1, width)
    other_len = other_flat.shape[0]
    other_grad, other_sums = by_tokens(
        input_grad_kernel,
        other_len,
        (other_flat, dk_other, dv_other),
        [(project_in, 1), (project_in, 2)],
        [jax.ShapeDtypeStruct((other_len, width), bf16), sums_shape],
    )
    other_grad = other_grad.reshape(rows, blocks - 1, block_len, width)
    context_grad, returned, down_got = lax.optimization_barrier((context_grad, other_grad, down_got))
    returned = [behind(returned[:, shift - 1], shift) for shift in shifts]
    dq, dk, dv = attention.backward_own(joint, context_grad, context, lse, dq_state)
    dq, dk, dv = [part.reshape(flat, width) for part in (dq, dk, dv)]
    dq, dk, dv, produced, down_got, up_got = lax.optimization_barrier((dq, dk, dv, produced, down_got, up_got))

    kv_grad = weight_grad([(normed_one, dk), (normed_other, dk_other)], 2 * width, 0, None)
    kv_grad = weight_grad([(normed_one, dv), (normed_other, dv_other)], 2 * width, width, kv_grad)
    columns = 2 * width + 128
    rest_grad = weight_grad([(context_flat, attn_grad)], columns, width, None)
    rest_grad = weight_grad([(normed_one, dq)], columns, 0, rest_grad)
    own_grad, own_sums = by_tokens(
        input_grad_kernel,
        flat,
        (tokens_flat, dq, dk, dv),
        [(project_in, 0), (project_in, 1), (project_in, 2)],
        [wide_shape, sums_shape],
    )

    rest_grad = put_sums(own_sums, other_sums, second_sums, rest_grad)
    rest_grad, returned = lax.optimization_barrier((rest_grad, returned))
    shares = [kv_grad, rest_grad]
    stages = stages_of(lax.axis_size("wide"), blocks)
    for number, (bits, code) in enumerate(zip(stages, places_of(stages))):
        shares = reduce_step(shares, bits, code)
        if number == 0:
            late = (down_own, up_own, down_got, up_got, middle, produced, own_grad, returned)
            late, shares = lax.optimization_barrier((late, shares))
            down_own, up_own, down_got, up_got, middle, produced, own_grad, returned = late
    shares = [x.astype(bf16) for x in shares]

    down_share = summed_shares(down_own, down_got)
    up_share = summed_shares(up_own, up_got)
    total_grad = own_grad
    for part in returned:
        total_grad = total_grad + part.reshape(flat, width).astype(f32)
    unit_one, rate_one = unit_of(tokens_flat.astype(f32))
    stream_grad = middle_grad + norm_back(total_grad, first_gain, unit_one, rate_one)
    (result,) = by_tokens(
        result_kernel,
        flat,
        (target_whole_row, middle, gate),
        [(produced, None)],
        [low_shape],
    )
    down_share, up_share, stream_grad, result, shares = lax.optimization_barrier(
        (down_share, up_share, stream_grad, result, shares)
    )
    kv_sum, q_sum = [part.astype(f32) for part in gather_parts(shares)]

    out_shape = (rows, block_len, width)
    return (
        result.reshape(out_shape),
        stream_grad.reshape(out_shape),
        jnp.concatenate([q_sum[:, :width], kv_sum], 1),
        q_sum[:, width : 2 * width],
        q_sum[:, 2 * width],
        q_sum[:, 2 * width + 1],
        q_sum[:, 2 * width + 2],
        q_sum[:, 2 * width + 3],
        up_share,
        down_share,
    )


def solution(mesh):
    return jax.shard_map(
        body,
        mesh=mesh,
        in_specs=(
            P("wide", "blk", None),
            P("wide", None),
            P("wide", "blk", None),
            P(),
            P(),
            P(),
            P(),
            P(),
            P(),
            P(),
            P("wide", None, None),
            P("wide", None, None),
            P("wide", "blk", None),
        ),
        out_specs=(
            P("wide", "blk", None),
            P("wide", "blk", None),
            P(),
            P(),
            P(),
            P(),
            P(),
            P(),
            P("wide", None, "blk"),
            P("wide", "blk", None),
        ),
        check_vma=False,
    )
```

```python
import functools

import jax
import jax.numpy as jnp
from jax import lax
from jax.experimental import pallas as pl
from jax.experimental.pallas import tpu as pltpu
from jax.sharding import PartitionSpec as P

HEAD_DIM = 64
GROUP = 4
LANES = GROUP * HEAD_DIM
NEG = -1e30
f32 = jnp.float32
bf16 = jnp.bfloat16
VMEM_LIMIT = 60 * 1024 * 1024
SHORT = pl.CostEstimate(flops=1, bytes_accessed=1, transcendentals=0)
LONG = pl.CostEstimate(flops=10**11, bytes_accessed=1, transcendentals=0)


def tile_of(size, most):
    tile = most
    while size % tile:
        tile //= 2
    return tile


def dot(a, b):
    return jnp.dot(a, b, preferred_element_type=f32)


def dot_nt(a, b):
    return lax.dot_general(a, b, (((1,), (1,)), ((), ())), preferred_element_type=f32)


def params(**more):
    return pltpu.CompilerParams(vmem_limit_bytes=VMEM_LIMIT, **more)


def largest_norm(x):
    head = lax.broadcasted_iota(jnp.int32, (LANES, 2 * HEAD_DIM), 0) // HEAD_DIM
    lane = lax.broadcasted_iota(jnp.int32, (LANES, 2 * HEAD_DIM), 1)
    pick = jnp.where(head == lane, 1.02, 0.0).astype(bf16)
    wide = x.astype(f32)
    return jnp.sqrt(jnp.max(dot((wide * wide).astype(bf16), pick), 0, keepdims=True))


def pair_of(head):
    return slice(2 * HEAD_DIM * (head // 2), 2 * HEAD_DIM * (head // 2 + 1))


def head_of_pair(pair, head, other=0.0):
    lane = lax.broadcasted_iota(jnp.int32, (1, 2 * HEAD_DIM), 1)
    keep = lane < HEAD_DIM if head % 2 == 0 else lane >= HEAD_DIM
    return jnp.where(keep, pair, jnp.full_like(pair, other))


def pieces_of(length, most):
    return [(at, min(most, length - at)) for at in range(0, length, most)]


def key_place(at, me, block_len, own):
    if own:
        return me * block_len + at
    return (me - 1 - at // block_len) * block_len + at % block_len


def mask_of(at, size, block, me, block_len, tile, starts, own, flipped):
    shape = (size, tile) if flipped else (tile, size)
    key = lax.broadcasted_iota(jnp.int32, shape, 0 if flipped else 1) + key_place(at, me, block_len, own)
    mask = key >= starts
    if own:
        query = lax.broadcasted_iota(jnp.int32, shape, 1 if flipped else 0) + (me * block_len + block * tile)
        mask = mask & (key <= query)
    return mask


def needed(at, size, block, low, me, block_len, tile, own):
    place = key_place(at, me, block_len, own)
    there = place + size > low
    if own:
        return jnp.logical_and(there, at < (block + 1) * tile)
    return jnp.logical_and(there, place >= 0)


def stat_place(head):
    return 2 * (head % 2) + head // 2


def split(x):
    parts = []
    for _ in range(3):
        part = x.astype(bf16)
        parts.append(part)
        x = x - part.astype(f32)
    return parts


def rows_of_lanes(x, lanes):
    lane = lax.broadcasted_iota(jnp.int32, (8, x.shape[1]), 1)
    row = lax.broadcasted_iota(jnp.int32, (8, x.shape[1]), 0)
    pick = jnp.zeros((8, x.shape[1]), f32)
    for at, number in enumerate(lanes):
        pick = jnp.where((row == at) & (lane == number), 1.0, pick)
    return sum(dot_nt(pick.astype(bf16), part) for part in split(x))[: len(lanes)]


def attend_kernel(me_ref, low_ref, q_ref, k_ref, v_ref, ok_ref, ov_ref, start_ref, ctx_out, lse_out, va, ova, acc, safe, *, tile, block_len):
    row, block = pl.program_id(0), pl.program_id(2)
    me = me_ref[0]
    low = low_ref[row, block]
    scale = HEAD_DIM**-0.5
    lane = lax.broadcasted_iota(jnp.int32, (1, 2 * HEAD_DIM), 1)
    pieces = [(True, at, size) for at, size in pieces_of(block_len, 512)]
    pieces += [(False, at, size) for at, size in pieces_of(ok_ref.shape[1], min(1024, block_len))]

    @pl.when(block == 0)
    def prepare():
        for values, spread in ((v_ref, va), (ov_ref, ova)):
            for head in range(GROUP):
                spread[head] = head_of_pair(values[0, :, pair_of(head)], head, 1.0)
        keys = jnp.maximum(largest_norm(k_ref[0]), largest_norm(ok_ref[0]))
        bound = jnp.max(largest_norm(q_ref[0]) * keys) * scale
        safe[0] = (bound < 60.0).astype(jnp.int32)

    queries = q_ref[0, pl.ds(pl.multiple_of(block * tile, tile), tile), :]
    queries = (queries.astype(f32) * scale).astype(bf16)
    starts = column_of(start_ref[0])

    def scores_of(own, at, size, head):
        mask = mask_of(at, size, block, me, block_len, tile, starts, own, False)
        keys = (k_ref if own else ok_ref)[0, at : at + size, pair_of(head)]
        return jnp.where(mask, dot_nt(head_of_pair(queries[:, pair_of(head)], head), keys), NEG)

    def attend(shifted):
        acc[...] = jnp.zeros_like(acc)
        peaks = [jnp.full((tile, 1), NEG, f32)] * GROUP
        if shifted:
            for own, at, size in pieces:
                there = needed(at, size, block, low, me, block_len, tile, own)
                for head in range(GROUP):
                    higher = jnp.max(scores_of(own, at, size, head), 1, keepdims=True)
                    peaks[head] = jnp.maximum(peaks[head], jnp.where(there, higher, NEG))
        for own, at, size in pieces:

            @pl.when(needed(at, size, block, low, me, block_len, tile, own))
            def piece(own=own, at=at, size=size):
                for head in range(GROUP):
                    scores = scores_of(own, at, size, head)
                    if shifted:
                        scores = scores - peaks[head]
                    weights = jnp.exp(scores).astype(bf16)
                    acc[head] += dot(weights, (va if own else ova)[head, at : at + size])

        stats = []
        for head in range(0, GROUP, 2):
            even, odd = acc[head], acc[head + 1]
            sums = pltpu.roll(jnp.where(lane < HEAD_DIM, odd, even), HEAD_DIM, 1)
            ctx_out[0, :, pair_of(head)] = (jnp.where(lane < HEAD_DIM, even, odd) / sums).astype(bf16)
            stats.append(sums)
        first = lane % HEAD_DIM < HEAD_DIM // 2
        stat = jnp.log(jnp.where(first, stats[0], stats[1]))
        if shifted:
            for head in range(GROUP):
                stat = jnp.where(lane // (HEAD_DIM // 2) == stat_place(head), stat + peaks[head], stat)
        lse_out[0, 0] = rows_of_lanes(stat, [stat_place(head) * (HEAD_DIM // 2) for head in range(GROUP)])

    @pl.when(safe[0] == 1)
    def without_shift():
        attend(False)

    @pl.when(safe[0] == 0)
    def with_shift():
        attend(True)


def grad_kernel(me_ref, low_ref, *refs, tile, block_len, own):
    q_ref, k_ref, v_ref, go_ref, ctx_ref, lse_ref, start_ref = refs[:7]
    if own:
        dq_in, dq_out, dk_out, dv_out = refs[7:11]
    else:
        dq_out, dk_out, dv_out = refs[7:10]
    kt, dq, dk, dv = refs[-4:]
    row, block = pl.program_id(0), pl.program_id(2)
    me = me_ref[0]
    low = low_ref[row, block]
    scale = HEAD_DIM**-0.5
    length = k_ref.shape[1]
    pieces = pieces_of(length, min(512 if own else 1024, block_len))

    @pl.when(block == 0)
    def prepare():
        shape = (2 * HEAD_DIM, 2 * HEAD_DIM)
        same = lax.broadcasted_iota(jnp.int32, shape, 0) == lax.broadcasted_iota(jnp.int32, shape, 1)
        turn = jnp.where(same, scale, 0.0).astype(bf16)
        for head in range(0, GROUP, 2):
            kt[pair_of(head)] = dot_nt(turn, k_ref[0, :, pair_of(head)]).astype(bf16)
        dk[...] = jnp.zeros_like(dk)
        dv[...] = jnp.zeros_like(dv)

    queries = (q_ref[0].astype(f32) * scale).astype(bf16)
    go = go_ref[0]
    starts = start_ref[0]
    product = go.astype(f32) * ctx_ref[0].astype(f32)
    head_row = lax.broadcasted_iota(jnp.int32, (8, LANES), 0)
    head_lane = lax.broadcasted_iota(jnp.int32, (8, LANES), 1) // HEAD_DIM
    pick = jnp.where(head_row == head_lane, 1.0, 0.0).astype(bf16)
    inners = sum(dot_nt(pick, part) for part in split(product)[:2])
    inner = [inners[head : head + 1] for head in range(GROUP)]
    dq[...] = dq_in[0] if own else jnp.zeros_like(dq)
    for at, size in pieces:

        @pl.when(needed(at, size, block, low, me, block_len, tile, own))
        def piece(at=at, size=size):
            rows = slice(at, at + size)
            mask = mask_of(at, size, block, me, block_len, tile, starts, own, True)
            for first in range(0, GROUP, 2):
                pair = pair_of(first)
                keys, values = k_ref[0, rows, pair], v_ref[0, rows, pair]
                all_probs, all_grads, all_queries, all_go = [], [], [], []
                for head in (first, first + 1):
                    query = head_of_pair(queries[:, pair], head)
                    head_go = head_of_pair(go[:, pair], head)
                    scores = dot_nt(keys, query) - lse_ref[0, 0, head : head + 1, :]
                    probs = jnp.exp(jnp.where(mask, scores, NEG))
                    prob_grad = dot_nt(values, head_go)
                    score_grad = (probs * (prob_grad - inner[head])).astype(bf16)
                    lanes = slice(head * HEAD_DIM, (head + 1) * HEAD_DIM)
                    dq[lanes] += dot(kt[lanes, rows], score_grad)
                    all_probs.append(probs.astype(bf16))
                    all_grads.append(score_grad)
                    all_queries.append(query)
                    all_go.append(head_go)
                dv[rows, pair] += dot(jnp.concatenate(all_probs, 1), jnp.concatenate(all_go, 0))
                dk[rows, pair] += dot(jnp.concatenate(all_grads, 1), jnp.concatenate(all_queries, 0))

    if own:
        dq_out[0] = dq[...].T.astype(bf16)
    else:
        dq_out[0] = dq[...]

    @pl.when(block == pl.num_programs(2) - 1)
    def write():
        dk_out[0] = dk[...].astype(bf16)
        dv_out[0] = dv[...].astype(bf16)


class Attention:
    def __init__(self, me, starts, rows, block_len, width):
        self.rows, self.block_len, self.width = rows, block_len, width
        self.tile = tile_of(block_len, 512)
        self.tiles = block_len // self.tile
        self.groups = width // LANES
        self.me = me.reshape(1).astype(jnp.int32)
        self.low = starts[:, :: self.tile]
        self.start_row = starts.reshape(rows, 1, block_len)

    def queries(self, offset=0):
        return pl.BlockSpec((1, self.tile, LANES), lambda r, g, b, *_: (r, b, offset * self.groups + g))

    def keys(self, length, offset):
        return pl.BlockSpec((1, length, LANES), lambda r, g, b, *_: (r, 0, offset * self.groups + g))

    def stat(self):
        return pl.BlockSpec((1, 1, GROUP, self.tile), lambda r, g, b, *_: (r, g, 0, b))

    def turned(self):
        return pl.BlockSpec((1, LANES, self.tile), lambda r, g, b, *_: (r, g, b))

    def row_starts(self):
        return pl.BlockSpec((1, 1, self.tile), lambda r, g, b, *_: (r, 0, b))

    def shape(self, length, dtype=bf16):
        return jax.ShapeDtypeStruct((self.rows, length, self.width), dtype)

    def call(self, kernel, cost, in_specs, out_specs, out_shape, scratch, args):
        return pl.pallas_call(
            functools.partial(kernel, tile=self.tile, block_len=self.block_len),
            grid_spec=pltpu.PrefetchScalarGridSpec(
                num_scalar_prefetch=2,
                grid=(self.rows, self.groups, self.tiles),
                in_specs=in_specs,
                out_specs=out_specs,
                scratch_shapes=scratch,
            ),
            out_shape=out_shape,
            compiler_params=params(),
            cost_estimate=cost,
        )(self.me, self.low, *args)

    def forward(self, joint, other):
        size, length = self.block_len, other.shape[1]
        return self.call(
            attend_kernel,
            LONG,
            [self.keys(size, 0), self.keys(size, 1), self.keys(size, 2)]
            + [self.keys(length, 0), self.keys(length, 1), self.row_starts()],
            [self.queries(), self.stat()],
            [self.shape(size), jax.ShapeDtypeStruct((self.rows, self.groups, GROUP, size), f32)],
            [
                pltpu.VMEM((GROUP, size, 2 * HEAD_DIM), bf16),
                pltpu.VMEM((GROUP, length, 2 * HEAD_DIM), bf16),
                pltpu.VMEM((GROUP, self.tile, 2 * HEAD_DIM), f32),
                pltpu.SMEM((1,), jnp.int32),
            ],
            (joint, joint, joint, other, other, self.start_row),
        )

    def grad_scratch(self, length):
        total = pltpu.VMEM((length, LANES), f32)
        return [pltpu.VMEM((LANES, length), bf16), pltpu.VMEM((LANES, self.tile), f32), total, total]

    def backward_other(self, joint, other, grad, context, lse):
        size, length = self.block_len, other.shape[1]
        return self.call(
            functools.partial(grad_kernel, own=False),
            SHORT,
            [self.queries(), self.keys(length, 0), self.keys(length, 1)]
            + [self.queries(), self.queries(), self.stat(), self.row_starts()],
            [self.turned(), self.keys(length, 0), self.keys(length, 0)],
            [
                jax.ShapeDtypeStruct((self.rows, self.width, size), f32),
                self.shape(length),
                self.shape(length),
            ],
            self.grad_scratch(length),
            (joint, other, other, grad, context, lse, self.start_row),
        )

    def backward_own(self, joint, grad, context, lse, dq_state):
        size = self.block_len
        return self.call(
            functools.partial(grad_kernel, own=True),
            LONG,
            [self.queries(), self.keys(size, 1), self.keys(size, 2)]
            + [self.queries(), self.queries(), self.stat(), self.row_starts(), self.turned()],
            [self.queries(), self.keys(size, 0), self.keys(size, 0)],
            [self.shape(size)] * 3,
            self.grad_scratch(size),
            (joint, joint, joint, grad, context, lse, self.start_row, dq_state),
        )


def place_kernel(target_ref, x_ref, out_ref):
    tile = out_ref.shape[0]
    slots = lax.broadcasted_iota(jnp.int32, (tile, target_ref.shape[1]), 0) + pl.program_id(0) * tile
    picked = jnp.where(slots == target_ref[...], 1.0, 0.0).astype(bf16)
    out_ref[...] = dot(picked, x_ref[...]).astype(bf16)


def place(target_row, x, slots):
    flat, width = x.shape
    tile = tile_of(slots, 256)
    return pl.pallas_call(
        place_kernel,
        grid=(slots // tile,),
        in_specs=[pl.BlockSpec((1, flat), lambda i: (0, 0)), pl.BlockSpec((flat, width), lambda i: (0, 0))],
        out_specs=pl.BlockSpec((tile, width), lambda i: (i, 0)),
        out_shape=jax.ShapeDtypeStruct((slots, width), bf16),
        compiler_params=params(),
        cost_estimate=SHORT,
    )(target_row, x)


def column_of(row):
    return jnp.broadcast_to(row.astype(f32), (8, row.shape[1])).T[:, :1].astype(jnp.int32)


def fetched(target, sources):
    total, before = 0.0, 0
    for source in sources:
        slots = lax.broadcasted_iota(jnp.int32, (target.shape[0], source.shape[0]), 1) + before
        total += dot(jnp.where(slots == target, 1.0, 0.0).astype(bf16), source[...])
        before += source.shape[0]
    return total


def result_kernel(target_ref, middle_ref, gate_ref, *refs):
    branch = fetched(column_of(target_ref[...]), refs[:-1])
    refs[-1][...] = (middle_ref[...] + gate_ref[...] * branch).astype(bf16)


def unit_of(x):
    center = x - jnp.mean(x, -1, keepdims=True)
    rate = lax.rsqrt(jnp.mean(center * center, -1, keepdims=True) + 1e-05)
    return center * rate, rate


def norm_back(grad, gain, unit, rate):
    scaled = grad * gain
    mean_one = jnp.mean(scaled, -1, keepdims=True)
    mean_two = jnp.mean(scaled * unit, -1, keepdims=True)
    return rate * (scaled - mean_one - unit * mean_two)


def add_sums(sums_ref, grad, unit):
    @pl.when(pl.program_id(0) == 0)
    def clear():
        sums_ref[...] = jnp.zeros_like(sums_ref)

    sums_ref[0:1] += jnp.sum(grad * unit, 0, keepdims=True)
    sums_ref[1:2] += jnp.sum(grad, 0, keepdims=True)


def second_norm_grad_kernel(target_ref, middle_ref, upstream_ref, gain_ref, weight_ref, *refs):
    sources = refs[:-4]
    grad_ref, low_ref, context_ref, sums_ref = refs[-4:]
    grad = fetched(column_of(target_ref[...]), sources)
    unit, rate = unit_of(middle_ref[...])
    add_sums(sums_ref, grad, unit)
    total = upstream_ref[...].astype(f32) + norm_back(grad, gain_ref[...], unit, rate)
    grad_ref[...] = total
    low = total.astype(bf16)
    low_ref[...] = low
    context_ref[...] = dot_nt(low, weight_ref[...]).astype(bf16)


def input_grad_kernel(tokens_ref, *refs):
    grad_ref, sums_ref = refs[-2:]
    count = (len(refs) - 2) // 2
    grad = 0.0
    for part, weight in zip(refs[:count], refs[count : 2 * count]):
        grad += dot_nt(part[...], weight[...])
    unit, _ = unit_of(tokens_ref[...].astype(f32))
    add_sums(sums_ref, grad, unit)
    grad_ref[...] = grad.astype(grad_ref.dtype)


def joint_kernel(tokens_ref, gain_ref, shift_ref, *refs):
    weights, (normed_ref, joint_ref) = refs[:-2], refs[-2:]
    normed = unit_of(tokens_ref[...].astype(f32))[0] * gain_ref[...] + shift_ref[...]
    normed = normed.astype(bf16)
    normed_ref[...] = normed
    width = normed.shape[1]
    for at, weight in enumerate(weights):
        joint_ref[:, at * width : (at + 1) * width] = dot(normed, weight[...]).astype(bf16)


def middle_kernel(context_ref, tokens_ref, route_ref, weight_ref, gain_ref, shift_ref, centroid_ref, middle_ref, normed_ref, gate_ref):
    middle = tokens_ref[...].astype(f32) + dot(context_ref[...], weight_ref[...])
    middle_ref[...] = middle
    normed = unit_of(middle)[0] * gain_ref[...] + shift_ref[...]
    normed_ref[...] = normed.astype(bf16)
    experts = centroid_ref.shape[0]
    route = column_of(route_ref[...])
    picked = route == lax.broadcasted_iota(jnp.int32, (route.shape[0], experts), 1)
    chosen = jnp.dot(
        picked.astype(f32), centroid_ref[...], precision=lax.Precision.HIGHEST, preferred_element_type=f32
    )
    gate_ref[...] = jax.nn.sigmoid(jnp.sum(normed * chosen, -1, keepdims=True))


def turned(x):
    size = tile_of(x.shape[1], 256)
    same = lax.broadcasted_iota(jnp.int32, (size, size), 0) == lax.broadcasted_iota(jnp.int32, (size, size), 1)
    unit = jnp.where(same, 1.0, 0.0).astype(bf16)
    return jnp.concatenate(
        [dot_nt(unit, x[:, at : at + size]).astype(bf16) for at in range(0, x.shape[1], size)], 0
    )


def weight_grads_kernel(*refs):
    early_ref, late_ref = refs[-2:]
    width = early_ref.shape[1] // 2
    own, other, context = [turned(ref[...]) for ref in refs[:3]]
    dq, dk, dv, dk_other, dv_other, attn_grad = [ref[...] for ref in refs[3:9]]
    early_ref[:, :width] = (dot(own, dk) + dot(other, dk_other)).astype(bf16)
    early_ref[:, width:] = (dot(own, dv) + dot(other, dv_other)).astype(bf16)
    late_ref[:, :width] = dot(own, dq).astype(bf16)
    late_ref[:, width:] = dot(context, attn_grad).astype(bf16)


def weight_grads(own, other, context, dq, dk, dv, dk_other, dv_other, attn_grad):
    width = own.shape[1]
    tile = tile_of(width, 256)
    lefts, rights = [own, other, context], [dq, dk, dv, dk_other, dv_other, attn_grad]
    specs = [pl.BlockSpec((left.shape[0], tile), lambda i: (0, i)) for left in lefts]
    specs += [pl.BlockSpec(right.shape, lambda i: (0, 0), pipeline_mode=pl.Buffered(1)) for right in rights]
    shape = jax.ShapeDtypeStruct((width, 2 * width), bf16)
    spec = pl.BlockSpec((tile, 2 * width), lambda i: (i, 0))
    return pl.pallas_call(
        weight_grads_kernel,
        grid=(width // tile,),
        in_specs=specs,
        out_specs=[spec, spec],
        out_shape=[shape, shape],
        compiler_params=params(),
        cost_estimate=SHORT,
    )(*lefts, *rights)


def sums_kernel(*refs):
    rows = jnp.concatenate([refs[0][...] + refs[1][...], refs[2][...]], 0)
    rows = jnp.concatenate([rows, jnp.zeros((124, rows.shape[1]), f32)], 0)
    refs[-1][...] = rows.T.astype(bf16)


def column_sums(own, other, second):
    return pl.pallas_call(
        sums_kernel,
        out_shape=jax.ShapeDtypeStruct((own.shape[1], 128), bf16),
        compiler_params=params(),
        cost_estimate=SHORT,
    )(own, other, second)


def finish_kernel(early_ref, late_ref, in_ref, out_ref, vectors_ref):
    width = out_ref.shape[1]
    in_ref[:, :width] = late_ref[:, :width].astype(f32)
    in_ref[:, width:] = early_ref[...].astype(f32)
    out_ref[...] = late_ref[:, width : 2 * width].astype(f32)
    vectors_ref[...] = late_ref[:, 2 * width :].astype(f32).T[:8]


def finish(early, late):
    width = early.shape[0]
    tile = tile_of(width, 256)

    def cut(array):
        return pl.BlockSpec((tile, array.shape[1]), lambda i: (i, 0))

    in_shape = jax.ShapeDtypeStruct((width, 3 * width), f32)
    out_shape = jax.ShapeDtypeStruct((width, width), f32)
    return pl.pallas_call(
        finish_kernel,
        grid=(width // tile,),
        in_specs=[cut(early), cut(late)],
        out_specs=[cut(in_shape), cut(out_shape), pl.BlockSpec((8, tile), lambda i: (0, i))],
        out_shape=[in_shape, out_shape, jax.ShapeDtypeStruct((8, width), f32)],
        compiler_params=params(),
        cost_estimate=SHORT,
    )(early, late)


def by_tokens(kernel, flat, tiled, whole, out_shape):
    tile = tile_of(flat, 256)

    def cut(array):
        if array.shape == (1, flat):
            return pl.BlockSpec((1, tile), lambda i: (0, i))
        if array.shape[0] == flat:
            return pl.BlockSpec((tile, array.shape[1]), lambda i: (i, 0))
        return pl.BlockSpec(array.shape, lambda i: (0, 0))

    specs = [cut(array) for array in tiled]
    for array, column in whole:
        if column is None:
            specs.append(pl.BlockSpec(array.shape, lambda i: (0, 0), pipeline_mode=pl.Buffered(1)))
        else:
            shape = (array.shape[0], array.shape[0])
            specs.append(pl.BlockSpec(shape, lambda i, c=column: (0, c), pipeline_mode=pl.Buffered(1)))
    arrays = list(tiled) + [array for array, _ in whole]
    return pl.pallas_call(
        kernel,
        grid=(flat // tile,),
        in_specs=specs,
        out_specs=[cut(shape) for shape in out_shape],
        out_shape=out_shape,
        compiler_params=params(),
        cost_estimate=SHORT,
    )(*arrays)


def expert_kernel(*refs):
    x_ref, g_ref, up_ref, down_ref, cent_ref = refs[:5]
    out_ref, dx_ref, act_ref, pre_ref, pg_ref = refs[-5:]
    x = x_ref[...]
    g = g_ref[...].reshape(x.shape).astype(f32)
    centroid = cent_ref[...]
    gate = jax.nn.sigmoid(jnp.sum(x.astype(f32) * centroid, -1, keepdims=True))
    produced_grad = (gate * g).astype(bf16)
    pg_ref[...] = produced_grad
    pre = dot(x, up_ref[...])
    cumulative = 0.5 + 0.5 * lax.erf(pre * (0.5**0.5))
    act = (pre * cumulative).astype(bf16)
    slope = cumulative + pre * (jnp.exp(-0.5 * pre * pre) * 0.3989422804014327)
    act_ref[...] = act
    pre_grad = (dot_nt(produced_grad, down_ref[...]) * slope).astype(bf16)
    pre_ref[...] = pre_grad
    produced = dot(act, down_ref[...]).astype(bf16)
    out_ref[...] = produced.reshape(out_ref.shape)
    gate_grad = jnp.sum(g * produced.astype(f32), -1, keepdims=True)
    logit_grad = gate_grad * gate * (1.0 - gate)
    dx_ref[...] = (dot_nt(pre_grad, up_ref[...]) + logit_grad * centroid).astype(bf16)


def run_expert(x, g, half, up, down, centroid, outputs):
    rows, width = x.shape
    peers, halves, depth, _ = g.shape
    hidden = up.shape[1]
    tile = depth * tile_of(peers, max(1, 256 // depth))
    by_row = pl.BlockSpec((tile, width), lambda i: (i, 0))
    by_hidden = pl.BlockSpec((tile, hidden), lambda i: (i, 0))
    by_peer = pl.BlockSpec((tile // depth, 1, depth, width), lambda i: (i, half, 0, 0))

    def whole(shape):
        return pl.BlockSpec(shape, lambda i: (0, 0), pipeline_mode=pl.Buffered(1))

    in_specs = [by_row, by_peer, whole((width, hidden)), whole((hidden, width)), whole((1, width))]
    arrays = [x, g, up, down, centroid]
    aliases = {}
    if outputs is not None:
        in_specs.append(pl.BlockSpec(memory_space=pl.ANY))
        arrays.append(outputs)
        aliases = {5: 0}
    row_shape = jax.ShapeDtypeStruct((rows, width), bf16)
    hidden_shape = jax.ShapeDtypeStruct((rows, hidden), bf16)
    return pl.pallas_call(
        expert_kernel,
        grid=(rows // tile,),
        in_specs=in_specs,
        out_specs=[by_peer, by_row, by_hidden, by_hidden, by_row],
        out_shape=[jax.ShapeDtypeStruct(g.shape, bf16), row_shape, hidden_shape, hidden_shape, row_shape],
        input_output_aliases=aliases,
        compiler_params=params(),
        cost_estimate=SHORT,
    )(*arrays)


def stages_of(wide, blocks):
    def bits(low, high):
        found = []
        while low < high:
            found.append(low)
            low *= 2
        return found

    stages = (bits(1, min(2, wide)), bits(2, min(4, wide)) + bits(wide, wide * blocks), bits(4, wide))
    return [stage for stage in stages if stage]


def spread(code, bits):
    return sum(bit for i, bit in enumerate(bits) if code >> i & 1)


def swap(array, mask):
    total = lax.axis_size("blk") * lax.axis_size("wide")
    return lax.ppermute(array, ("blk", "wide"), [(i, i ^ mask) for i in range(total)])


def places_of(stages):
    me = lax.axis_index("blk") * lax.axis_size("wide") + lax.axis_index("wide")
    return [sum((me // bit % 2) << i for i, bit in enumerate(bits)) for bits in stages]


def reduce_step(parts, bits, code):
    count = 1 << len(bits)
    summed = []
    for x in parts:
        rows = x.shape[0] // count

        def piece(index):
            return lax.dynamic_slice_in_dim(x, index * rows, rows, 0)

        got = [swap(piece(code ^ other).astype(bf16), spread(other, bits)) for other in range(1, count)]
        total = piece(code).astype(f32)
        for part in got:
            total = total + part.astype(f32)
        summed.append(total)
    return summed


def gather_step(parts, bits, code):
    gathered = []
    for x in parts:
        rows = x.shape[0]
        whole = jnp.zeros((rows << len(bits), x.shape[1]), bf16)
        whole = lax.dynamic_update_slice_in_dim(whole, x, code * rows, 0)
        for other in range(1, 1 << len(bits)):
            part = swap(x, spread(other, bits))
            whole = lax.dynamic_update_slice_in_dim(whole, part, (code ^ other) * rows, 0)
        gathered.append(whole)
    return gathered


def body(
    tokens,
    segments,
    routes,
    project_in,
    project_out,
    first_gain,
    first_shift,
    second_gain,
    second_shift,
    centroids,
    expert_up,
    expert_down,
    cotangent,
):
    rows, block_len, width = tokens.shape
    blocks = lax.axis_size("blk")
    me = lax.axis_index("blk")
    flat = rows * block_len
    experts = centroids.shape[0]
    local_experts = expert_up.shape[0]
    peers = experts // local_experts
    capacity = 2 * block_len // experts
    halves = 2 if capacity % 16 == 0 else 1
    depth = capacity // halves
    half_slots = experts * rows * depth

    shifts = range(1, blocks)

    def ahead(array, shift):
        return lax.ppermute(array, "blk", [(i, i + shift) for i in range(blocks - shift)])

    def behind(array, shift):
        return lax.ppermute(array, "blk", [(i + shift, i) for i in range(blocks - shift)])

    other_tokens = jnp.concatenate([ahead(tokens, shift) for shift in shifts], 1)
    other_flat = other_tokens.reshape(-1, width)

    route_ids = routes[:, :, 0]
    picked = route_ids[:, :, None] == lax.iota(jnp.int32, experts)[None, None, :]
    places = lax.iota(jnp.int32, block_len)
    before = (places[None, :] <= places[:, None]).astype(bf16)
    ranks = jnp.einsum("qk,rke->rqe", before, picked.astype(bf16), preferred_element_type=f32)
    slot_index = jnp.sum(jnp.where(picked, ranks, 0.0), 2).astype(jnp.int32) - 1
    row_index = lax.iota(jnp.int32, rows)[:, None]
    half = slot_index // depth
    place_in_half = row_index * depth + slot_index - half * depth
    target_halves = half * half_slots + route_ids * (rows * depth) + place_in_half
    target_whole = (route_ids * halves + half) * (rows * depth) + place_in_half

    def exchange(array):
        return lax.all_to_all(
            array.reshape(experts, -1, width), "wide", split_axis=0, concat_axis=0, tiled=True
        )

    upstream = cotangent.reshape(flat, width)

    own_segments = lax.dynamic_slice_in_dim(segments, me * block_len, block_len, 1)
    smaller = segments[:, None, :] < own_segments[:, :, None]
    starts = jnp.sum(smaller.astype(jnp.int32), 2)
    attention = Attention(me, starts, rows, block_len, width)

    tokens_flat = tokens.reshape(flat, width)

    first_gain_row, first_shift_row = first_gain.reshape(1, width), first_shift.reshape(1, width)

    def joined(x, columns):
        count = len(columns)
        return by_tokens(
            joint_kernel,
            x.shape[0],
            (x,),
            [(first_gain_row, None), (first_shift_row, None)] + [(project_in, column) for column in columns],
            [
                jax.ShapeDtypeStruct(x.shape, bf16),
                jax.ShapeDtypeStruct((x.shape[0], count * width), bf16),
            ],
        )

    normed_one, joint = joined(tokens_flat, (0, 1, 2))
    route_row = routes.reshape(1, flat)
    target_halves_row, target_whole_row = target_halves.reshape(1, flat), target_whole.reshape(1, flat)
    second_gain_row, second_shift_row = second_gain.reshape(1, width), second_shift.reshape(1, width)
    small = (attention.low, attention.start_row, route_row, target_halves_row, target_whole_row)
    small += (first_gain_row, first_shift_row, second_gain_row, second_shift_row)
    small, to_place = lax.optimization_barrier((small, upstream))
    attention.low, attention.start_row, route_row, target_halves_row, target_whole_row = small[:5]
    first_gain_row, first_shift_row, second_gain_row, second_shift_row = small[5:]
    grads_arrived = exchange(place(target_whole_row, to_place, halves * half_slots))
    grads_arrived = grads_arrived.reshape(peers, local_experts, halves, rows * depth, width)
    joint = joint.reshape(rows, block_len, 3 * width)
    normed_other, other = joined(other_flat, (1, 2))
    other = other.reshape(rows, (blocks - 1) * block_len, 2 * width)
    context, lse = attention.forward(joint, other)
    context_flat = context.reshape(flat, width)

    wide_shape = jax.ShapeDtypeStruct((flat, width), f32)
    low_shape = jax.ShapeDtypeStruct((flat, width), bf16)
    sums_shape = jax.ShapeDtypeStruct((2, width), f32)
    middle, normed_two, gate = by_tokens(
        middle_kernel,
        flat,
        (context_flat, tokens_flat, route_row),
        [(project_out, None), (second_gain_row, None), (second_shift_row, None), (centroids, None)],
        [wide_shape, low_shape, jax.ShapeDtypeStruct((flat, 1), f32)],
    )
    normed_two, grads_arrived = lax.optimization_barrier((normed_two, grads_arrived))
    placed = [place(target_halves_row - h * half_slots, normed_two, half_slots) for h in range(halves)]
    arrived = [exchange(part).reshape(peers, local_experts, rows * depth, width) for part in placed]

    own_experts = lax.axis_index("wide") * local_experts
    outputs, row_grads = [None] * local_experts, []
    down_pairs, up_pairs = [[] for _ in range(local_experts)], [[] for _ in range(local_experts)]
    for h in range(halves):
        half_dx = []
        for local in range(local_experts):
            x = arrived[h][:, local].reshape(-1, width)
            centroid = lax.dynamic_slice_in_dim(centroids, own_experts + local, 1, 0)
            outputs[local], dx, act, pre_grad, out_grad = run_expert(
                x, grads_arrived[:, local], h, expert_up[local], expert_down[local], centroid, outputs[local]
            )
            half_dx.append(dx.reshape(peers, 1, rows * depth, width))
            down_pairs[local].append((act, out_grad))
            up_pairs[local].append((x, pre_grad))
        row_grads.append(half_dx[0] if local_experts == 1 else jnp.concatenate(half_dx, 1))
    share = expert_up.shape[2] // blocks

    def share_of(array, block):
        return lax.dynamic_slice_in_dim(array, block * share, share, 1)

    def down_product(pairs, block):
        return sum(
            jnp.einsum("cf,cd->fd", share_of(act, block), out_grad, preferred_element_type=f32)
            for act, out_grad in pairs
        )

    def up_product(pairs, block):
        return sum(
            jnp.einsum("cd,cf->df", x, share_of(pre_grad, block), preferred_element_type=f32)
            for x, pre_grad in pairs
        )

    def product_shares(pairs, product):
        sent = [[product(pair, lax.rem(me + shift, blocks)).astype(bf16) for shift in shifts] for pair in pairs]
        return sent, [product(pair, me) for pair in pairs]

    def send_shares(sent):
        return [
            [
                lax.ppermute(part, "blk", [(i, (i + shift) % blocks) for i in range(blocks)])
                for shift, part in zip(shifts, parts)
            ]
            for parts in sent
        ]

    def summed_shares(own, got):
        totals = []
        for total, parts in zip(own, got):
            for part in parts:
                total = total + part.astype(f32)
            totals.append(total)
        return jnp.stack(totals, 0)

    back_arrived = [exchange(part).reshape(half_slots, width) for part in row_grads]
    back_arrived[0], down_pairs, up_pairs = lax.optimization_barrier((back_arrived[0], down_pairs, up_pairs))
    down_sent, down_own = product_shares(down_pairs, down_product)
    up_sent, up_own = product_shares(up_pairs, up_product)
    down_got, up_got = send_shares(down_sent), send_shares(up_sent)
    output = outputs[0][:, None] if local_experts == 1 else jnp.stack(outputs, 1)
    back_arrived, down_own, up_own, _, _ = lax.optimization_barrier(
        (back_arrived, down_own, up_own, down_sent, up_sent)
    )

    middle_grad, attn_grad, context_grad, second_sums = by_tokens(
        second_norm_grad_kernel,
        flat,
        (target_halves_row, middle, upstream),
        [(second_gain_row, None), (project_out, None)] + [(part, None) for part in back_arrived],
        [wide_shape, low_shape, low_shape, sums_shape],
    )
    context_grad, output = lax.optimization_barrier((context_grad, output))
    produced = exchange(output).reshape(halves * half_slots, width)
    context_grad = context_grad.reshape(rows, block_len, width)
    dq_state, dk_other, dv_other = attention.backward_other(joint, other, context_grad, context, lse)
    dk_other, dv_other = dk_other.reshape(-1, width), dv_other.reshape(-1, width)
    other_len = other_flat.shape[0]
    other_grad, other_sums = by_tokens(
        input_grad_kernel,
        other_len,
        (other_flat, dk_other, dv_other),
        [(project_in, 1), (project_in, 2)],
        [jax.ShapeDtypeStruct((other_len, width), bf16), sums_shape],
    )
    other_grad = other_grad.reshape(rows, blocks - 1, block_len, width)
    context_grad, returned, down_got = lax.optimization_barrier((context_grad, other_grad, down_got))
    returned = [behind(returned[:, shift - 1], shift) for shift in shifts]
    dq, dk, dv = attention.backward_own(joint, context_grad, context, lse, dq_state)
    dq, dk, dv = [part.reshape(flat, width) for part in (dq, dk, dv)]
    tied = (dq, dk, dv, produced, down_got, up_got, returned)
    dq, dk, dv, produced, down_got, up_got, returned = lax.optimization_barrier(tied)

    early, late = weight_grads(
        normed_one, normed_other, context_flat, dq, dk, dv, dk_other, dv_other, attn_grad
    )
    own_grad, own_sums = by_tokens(
        input_grad_kernel,
        flat,
        (tokens_flat, dq, dk, dv),
        [(project_in, 0), (project_in, 1), (project_in, 2)],
        [wide_shape, sums_shape],
    )
    vectors = column_sums(own_sums, other_sums, second_sums)

    stages = stages_of(lax.axis_size("wide"), blocks)
    steps = list(zip(stages, places_of(stages)))
    early, late, vectors = reduce_step([early, late, vectors], *steps[0])
    rest = (down_own, up_own, down_got, up_got)
    rest, early = lax.optimization_barrier((rest, early))
    down_own, up_own, down_got, up_got = rest
    down_share = summed_shares(down_own, down_got)
    up_share = summed_shares(up_own, up_got)
    shares = [early, jnp.concatenate([late, vectors], 1)]
    for step in steps[1:-1]:
        shares = reduce_step(shares, *step)
    down_share, up_share, shares = lax.optimization_barrier((down_share, up_share, shares))
    shares = reduce_step(shares, *steps[-1])
    shares = [x.astype(bf16) for x in shares]

    shares = gather_step(shares, *steps[-1])
    rest = (middle, produced, own_grad, returned)
    rest, shares = lax.optimization_barrier((rest, shares))
    middle, produced, own_grad, returned = rest
    total_grad = own_grad
    for part in returned:
        total_grad = total_grad + part.reshape(flat, width).astype(f32)
    unit_one, rate_one = unit_of(tokens_flat.astype(f32))
    stream_grad = middle_grad + norm_back(total_grad, first_gain, unit_one, rate_one)
    (result,) = by_tokens(
        result_kernel,
        flat,
        (target_whole_row, middle, gate),
        [(produced, None)],
        [low_shape],
    )
    for step in reversed(steps[1:-1]):
        shares = gather_step(shares, *step)
    stream_grad, result, shares = lax.optimization_barrier((stream_grad, result, shares))
    in_sum, out_sum, vectors = finish(*gather_step(shares, *steps[0]))

    out_shape = (rows, block_len, width)
    return (
        result.reshape(out_shape),
        stream_grad.reshape(out_shape),
        in_sum,
        out_sum,
        vectors[0],
        vectors[1],
        vectors[2],
        vectors[3],
        up_share,
        down_share,
    )


def solution(mesh):
    return jax.shard_map(
        body,
        mesh=mesh,
        in_specs=(
            P("wide", "blk", None),
            P("wide", None),
            P("wide", "blk", None),
            P(),
            P(),
            P(),
            P(),
            P(),
            P(),
            P(),
            P("wide", None, None),
            P("wide", None, None),
            P("wide", "blk", None),
        ),
        out_specs=(
            P("wide", "blk", None),
            P("wide", "blk", None),
            P(),
            P(),
            P(),
            P(),
            P(),
            P(),
            P("wide", None, "blk"),
            P("wide", "blk", None),
        ),
        check_vma=False,
    )
```

```python
import functools

import jax
import jax.numpy as jnp
from jax import lax
from jax.experimental import pallas as pl
from jax.experimental.pallas import tpu as pltpu
from jax.sharding import PartitionSpec as P

HEAD_DIM = 64
GROUP = 4
LANES = GROUP * HEAD_DIM
NEG = -1e30
f32 = jnp.float32
bf16 = jnp.bfloat16
VMEM_LIMIT = 60 * 1024 * 1024
SHORT = pl.CostEstimate(flops=1, bytes_accessed=1, transcendentals=0)
LONG = pl.CostEstimate(flops=10**11, bytes_accessed=1, transcendentals=0)


def tile_of(size, most):
    tile = most
    while size % tile:
        tile //= 2
    return tile


def dot(a, b):
    return jnp.dot(a, b, preferred_element_type=f32)


def dot_nt(a, b):
    return lax.dot_general(a, b, (((1,), (1,)), ((), ())), preferred_element_type=f32)


def params(**more):
    return pltpu.CompilerParams(vmem_limit_bytes=VMEM_LIMIT, **more)


def largest_norm(x):
    head = lax.broadcasted_iota(jnp.int32, (LANES, 2 * HEAD_DIM), 0) // HEAD_DIM
    lane = lax.broadcasted_iota(jnp.int32, (LANES, 2 * HEAD_DIM), 1)
    pick = jnp.where(head == lane, 1.02, 0.0).astype(bf16)
    wide = x.astype(f32)
    return jnp.sqrt(jnp.max(dot((wide * wide).astype(bf16), pick), 0, keepdims=True))


def pair_of(head):
    return slice(2 * HEAD_DIM * (head // 2), 2 * HEAD_DIM * (head // 2 + 1))


def head_of_pair(pair, head, other=0.0):
    lane = lax.broadcasted_iota(jnp.int32, (1, 2 * HEAD_DIM), 1)
    keep = lane < HEAD_DIM if head % 2 == 0 else lane >= HEAD_DIM
    return jnp.where(keep, pair, jnp.full_like(pair, other))


def pieces_of(length, most):
    return [(at, min(most, length - at)) for at in range(0, length, most)]


def key_place(at, me, block_len, own):
    if own:
        return me * block_len + at
    return (me - 1 - at // block_len) * block_len + at % block_len


def mask_of(at, size, block, me, block_len, tile, starts, own, flipped):
    shape = (size, tile) if flipped else (tile, size)
    key = lax.broadcasted_iota(jnp.int32, shape, 0 if flipped else 1) + key_place(at, me, block_len, own)
    mask = key >= starts
    if own:
        query = lax.broadcasted_iota(jnp.int32, shape, 1 if flipped else 0) + (me * block_len + block * tile)
        mask = mask & (key <= query)
    return mask


def needed(at, size, block, low, me, block_len, tile, own):
    place = key_place(at, me, block_len, own)
    there = place + size > low
    if own:
        return jnp.logical_and(there, at < (block + 1) * tile)
    return jnp.logical_and(there, place >= 0)


def stat_place(head):
    return 2 * (head % 2) + head // 2


def split(x):
    parts = []
    for _ in range(3):
        part = x.astype(bf16)
        parts.append(part)
        x = x - part.astype(f32)
    return parts


def rows_of_lanes(x, lanes):
    lane = lax.broadcasted_iota(jnp.int32, (8, x.shape[1]), 1)
    row = lax.broadcasted_iota(jnp.int32, (8, x.shape[1]), 0)
    pick = jnp.zeros((8, x.shape[1]), f32)
    for at, number in enumerate(lanes):
        pick = jnp.where((row == at) & (lane == number), 1.0, pick)
    return sum(dot_nt(pick.astype(bf16), part) for part in split(x))[: len(lanes)]


def attend_kernel(me_ref, low_ref, q_ref, k_ref, v_ref, ok_ref, ov_ref, start_ref, ctx_out, lse_out, va, ova, acc, safe, *, tile, block_len):
    row, block = pl.program_id(0), pl.program_id(2)
    me = me_ref[0]
    low = low_ref[row, block]
    scale = HEAD_DIM**-0.5
    lane = lax.broadcasted_iota(jnp.int32, (1, 2 * HEAD_DIM), 1)
    pieces = [(True, at, size) for at, size in pieces_of(block_len, 512)]
    pieces += [(False, at, size) for at, size in pieces_of(ok_ref.shape[1], min(1024, block_len))]

    @pl.when(block == 0)
    def prepare():
        for values, spread in ((v_ref, va), (ov_ref, ova)):
            for head in range(GROUP):
                spread[head] = head_of_pair(values[0, :, pair_of(head)], head, 1.0)
        keys = jnp.maximum(largest_norm(k_ref[0]), largest_norm(ok_ref[0]))
        bound = jnp.max(largest_norm(q_ref[0]) * keys) * scale
        safe[0] = (bound < 60.0).astype(jnp.int32)

    queries = q_ref[0, pl.ds(pl.multiple_of(block * tile, tile), tile), :]
    queries = (queries.astype(f32) * scale).astype(bf16)
    starts = column_of(start_ref[0])

    def scores_of(own, at, size, head):
        mask = mask_of(at, size, block, me, block_len, tile, starts, own, False)
        keys = (k_ref if own else ok_ref)[0, at : at + size, pair_of(head)]
        return jnp.where(mask, dot_nt(head_of_pair(queries[:, pair_of(head)], head), keys), NEG)

    def attend(shifted):
        acc[...] = jnp.zeros_like(acc)
        peaks = [jnp.full((tile, 1), NEG, f32)] * GROUP
        if shifted:
            for own, at, size in pieces:
                there = needed(at, size, block, low, me, block_len, tile, own)
                for head in range(GROUP):
                    higher = jnp.max(scores_of(own, at, size, head), 1, keepdims=True)
                    peaks[head] = jnp.maximum(peaks[head], jnp.where(there, higher, NEG))
        for own, at, size in pieces:

            @pl.when(needed(at, size, block, low, me, block_len, tile, own))
            def piece(own=own, at=at, size=size):
                for head in range(GROUP):
                    scores = scores_of(own, at, size, head)
                    if shifted:
                        scores = scores - peaks[head]
                    weights = jnp.exp(scores).astype(bf16)
                    acc[head] += dot(weights, (va if own else ova)[head, at : at + size])

        stats = []
        for head in range(0, GROUP, 2):
            even, odd = acc[head], acc[head + 1]
            sums = pltpu.roll(jnp.where(lane < HEAD_DIM, odd, even), HEAD_DIM, 1)
            ctx_out[0, :, pair_of(head)] = (jnp.where(lane < HEAD_DIM, even, odd) / sums).astype(bf16)
            stats.append(sums)
        first = lane % HEAD_DIM < HEAD_DIM // 2
        stat = jnp.log(jnp.where(first, stats[0], stats[1]))
        if shifted:
            for head in range(GROUP):
                stat = jnp.where(lane // (HEAD_DIM // 2) == stat_place(head), stat + peaks[head], stat)
        lse_out[0, 0] = rows_of_lanes(stat, [stat_place(head) * (HEAD_DIM // 2) for head in range(GROUP)])

    @pl.when(safe[0] == 1)
    def without_shift():
        attend(False)

    @pl.when(safe[0] == 0)
    def with_shift():
        attend(True)


def probs_kernel(me_ref, low_ref, q_ref, k_ref, lse_ref, start_ref, out_ref, *, tile, block_len, own):
    row, block = pl.program_id(0), pl.program_id(2)
    me = me_ref[0]
    low = low_ref[row, block]
    queries = (q_ref[0].astype(f32) * HEAD_DIM**-0.5).astype(bf16)
    starts = start_ref[0]
    for at, size in pieces_of(k_ref.shape[1], min(512 if own else 1024, block_len)):

        @pl.when(needed(at, size, block, low, me, block_len, tile, own))
        def piece(at=at, size=size):
            rows = slice(at, at + size)
            mask = mask_of(at, size, block, me, block_len, tile, starts, own, True)
            for head in range(GROUP):
                query = head_of_pair(queries[:, pair_of(head)], head)
                scores = dot_nt(k_ref[0, rows, pair_of(head)], query) - lse_ref[0, 0, head : head + 1, :]
                out_ref[0, head, rows, :] = jnp.exp(jnp.where(mask, scores, NEG)).astype(bf16)


def grad_kernel(me_ref, low_ref, *refs, tile, block_len, own):
    q_ref, k_ref, v_ref, go_ref, ctx_ref, probs_ref = refs[:6]
    if own:
        dq_in, dq_out, dk_out, dv_out = refs[6:10]
    else:
        dq_out, dk_out, dv_out = refs[6:9]
    kt, dq, dk, dv = refs[-4:]
    row, block = pl.program_id(0), pl.program_id(2)
    me = me_ref[0]
    low = low_ref[row, block]
    scale = HEAD_DIM**-0.5
    length = k_ref.shape[1]
    pieces = pieces_of(length, min(512 if own else 1024, block_len))

    @pl.when(block == 0)
    def prepare():
        shape = (2 * HEAD_DIM, 2 * HEAD_DIM)
        same = lax.broadcasted_iota(jnp.int32, shape, 0) == lax.broadcasted_iota(jnp.int32, shape, 1)
        turn = jnp.where(same, scale, 0.0).astype(bf16)
        for head in range(0, GROUP, 2):
            kt[pair_of(head)] = dot_nt(turn, k_ref[0, :, pair_of(head)]).astype(bf16)
        dk[...] = jnp.zeros_like(dk)
        dv[...] = jnp.zeros_like(dv)

    queries = (q_ref[0].astype(f32) * scale).astype(bf16)
    go = go_ref[0]
    product = go.astype(f32) * ctx_ref[0].astype(f32)
    head_row = lax.broadcasted_iota(jnp.int32, (8, LANES), 0)
    head_lane = lax.broadcasted_iota(jnp.int32, (8, LANES), 1) // HEAD_DIM
    pick = jnp.where(head_row == head_lane, 1.0, 0.0).astype(bf16)
    inners = sum(dot_nt(pick, part) for part in split(product)[:2])
    inner = [inners[head : head + 1] for head in range(GROUP)]
    dq[...] = dq_in[0] if own else jnp.zeros_like(dq)
    for at, size in pieces:

        @pl.when(needed(at, size, block, low, me, block_len, tile, own))
        def piece(at=at, size=size):
            rows = slice(at, at + size)
            for first in range(0, GROUP, 2):
                pair = pair_of(first)
                values = v_ref[0, rows, pair]
                all_probs, all_grads, all_queries, all_go = [], [], [], []
                for head in (first, first + 1):
                    head_go = head_of_pair(go[:, pair], head)
                    probs = probs_ref[0, head, rows, :]
                    prob_grad = dot_nt(values, head_go)
                    score_grad = (probs.astype(f32) * (prob_grad - inner[head])).astype(bf16)
                    lanes = slice(head * HEAD_DIM, (head + 1) * HEAD_DIM)
                    dq[lanes] += dot(kt[lanes, rows], score_grad)
                    all_probs.append(probs)
                    all_grads.append(score_grad)
                    all_queries.append(head_of_pair(queries[:, pair], head))
                    all_go.append(head_go)
                dv[rows, pair] += dot(jnp.concatenate(all_probs, 1), jnp.concatenate(all_go, 0))
                dk[rows, pair] += dot(jnp.concatenate(all_grads, 1), jnp.concatenate(all_queries, 0))

    if own:
        dq_out[0] = dq[...].T.astype(bf16)
    else:
        dq_out[0] = dq[...]

    @pl.when(block == pl.num_programs(2) - 1)
    def write():
        dk_out[0] = dk[...].astype(bf16)
        dv_out[0] = dv[...].astype(bf16)


class Attention:
    def __init__(self, me, starts, rows, block_len, width):
        self.rows, self.block_len, self.width = rows, block_len, width
        self.tile = tile_of(block_len, 512)
        self.tiles = block_len // self.tile
        self.groups = width // LANES
        self.me = me.reshape(1).astype(jnp.int32)
        self.low = starts[:, :: self.tile]
        self.start_row = starts.reshape(rows, 1, block_len)

    def queries(self, offset=0):
        return pl.BlockSpec((1, self.tile, LANES), lambda r, g, b, *_: (r, b, offset * self.groups + g))

    def keys(self, length, offset):
        return pl.BlockSpec((1, length, LANES), lambda r, g, b, *_: (r, 0, offset * self.groups + g))

    def stat(self):
        return pl.BlockSpec((1, 1, GROUP, self.tile), lambda r, g, b, *_: (r, g, 0, b))

    def turned(self):
        return pl.BlockSpec((1, LANES, self.tile), lambda r, g, b, *_: (r, g, b))

    def row_starts(self):
        return pl.BlockSpec((1, 1, self.tile), lambda r, g, b, *_: (r, 0, b))

    def shape(self, length, dtype=bf16):
        return jax.ShapeDtypeStruct((self.rows, length, self.width), dtype)

    def call(self, kernel, cost, in_specs, out_specs, out_shape, scratch, args):
        return pl.pallas_call(
            functools.partial(kernel, tile=self.tile, block_len=self.block_len),
            grid_spec=pltpu.PrefetchScalarGridSpec(
                num_scalar_prefetch=2,
                grid=(self.rows, self.groups, self.tiles),
                in_specs=in_specs,
                out_specs=out_specs,
                scratch_shapes=scratch,
            ),
            out_shape=out_shape,
            compiler_params=params(),
            cost_estimate=cost,
        )(self.me, self.low, *args)

    def forward(self, joint, other):
        size, length = self.block_len, other.shape[1]
        return self.call(
            attend_kernel,
            LONG,
            [self.keys(size, 0), self.keys(size, 1), self.keys(size, 2)]
            + [self.keys(length, 0), self.keys(length, 1), self.row_starts()],
            [self.queries(), self.stat()],
            [self.shape(size), jax.ShapeDtypeStruct((self.rows, self.groups, GROUP, size), f32)],
            [
                pltpu.VMEM((GROUP, size, 2 * HEAD_DIM), bf16),
                pltpu.VMEM((GROUP, length, 2 * HEAD_DIM), bf16),
                pltpu.VMEM((GROUP, self.tile, 2 * HEAD_DIM), f32),
                pltpu.SMEM((1,), jnp.int32),
            ],
            (joint, joint, joint, other, other, self.start_row),
        )

    def grad_scratch(self, length):
        total = pltpu.VMEM((length, LANES), f32)
        return [pltpu.VMEM((LANES, length), bf16), pltpu.VMEM((LANES, self.tile), f32), total, total]

    def probs_spec(self, length):
        return pl.BlockSpec((1, GROUP, length, self.tile), lambda r, g, b, *_: (r, g, 0, b))

    def probs(self, joint, keys, lse, own):
        length = keys.shape[1]
        shape = (self.rows, self.groups * GROUP, length, self.block_len)
        (probs,) = self.call(
            functools.partial(probs_kernel, own=own),
            SHORT,
            [self.queries(), self.keys(length, 1 if own else 0), self.stat(), self.row_starts()],
            [self.probs_spec(length)],
            [jax.ShapeDtypeStruct(shape, bf16)],
            [],
            (joint, keys, lse, self.start_row),
        )
        return probs

    def backward_other(self, joint, other, grad, context, probs):
        size, length = self.block_len, other.shape[1]
        return self.call(
            functools.partial(grad_kernel, own=False),
            SHORT,
            [self.queries(), self.keys(length, 0), self.keys(length, 1)]
            + [self.queries(), self.queries(), self.probs_spec(length)],
            [self.turned(), self.keys(length, 0), self.keys(length, 0)],
            [
                jax.ShapeDtypeStruct((self.rows, self.width, size), f32),
                self.shape(length),
                self.shape(length),
            ],
            self.grad_scratch(length),
            (joint, other, other, grad, context, probs),
        )

    def backward_own(self, joint, grad, context, probs, dq_state):
        size = self.block_len
        return self.call(
            functools.partial(grad_kernel, own=True),
            LONG,
            [self.queries(), self.keys(size, 1), self.keys(size, 2)]
            + [self.queries(), self.queries(), self.probs_spec(size), self.turned()],
            [self.queries(), self.keys(size, 0), self.keys(size, 0)],
            [self.shape(size)] * 3,
            self.grad_scratch(size),
            (joint, joint, joint, grad, context, probs, dq_state),
        )


def place_kernel(target_ref, x_ref, out_ref):
    tile = out_ref.shape[0]
    slots = lax.broadcasted_iota(jnp.int32, (tile, target_ref.shape[1]), 0) + pl.program_id(0) * tile
    picked = jnp.where(slots == target_ref[...], 1.0, 0.0).astype(bf16)
    out_ref[...] = dot(picked, x_ref[...]).astype(bf16)


def place(target_row, x, slots):
    flat, width = x.shape
    tile = tile_of(slots, 256)
    return pl.pallas_call(
        place_kernel,
        grid=(slots // tile,),
        in_specs=[pl.BlockSpec((1, flat), lambda i: (0, 0)), pl.BlockSpec((flat, width), lambda i: (0, 0))],
        out_specs=pl.BlockSpec((tile, width), lambda i: (i, 0)),
        out_shape=jax.ShapeDtypeStruct((slots, width), bf16),
        compiler_params=params(),
        cost_estimate=SHORT,
    )(target_row, x)


def column_of(row):
    return jnp.broadcast_to(row.astype(f32), (8, row.shape[1])).T[:, :1].astype(jnp.int32)


def fetched(target, sources):
    total, before = 0.0, 0
    for source in sources:
        slots = lax.broadcasted_iota(jnp.int32, (target.shape[0], source.shape[0]), 1) + before
        total += dot(jnp.where(slots == target, 1.0, 0.0).astype(bf16), source[...])
        before += source.shape[0]
    return total


def result_kernel(target_ref, middle_ref, gate_ref, *refs):
    branch = fetched(column_of(target_ref[...]), refs[:-1])
    refs[-1][...] = (middle_ref[...] + gate_ref[...] * branch).astype(bf16)


def unit_of(x):
    center = x - jnp.mean(x, -1, keepdims=True)
    rate = lax.rsqrt(jnp.mean(center * center, -1, keepdims=True) + 1e-05)
    return center * rate, rate


def norm_back(grad, gain, unit, rate):
    scaled = grad * gain
    mean_one = jnp.mean(scaled, -1, keepdims=True)
    mean_two = jnp.mean(scaled * unit, -1, keepdims=True)
    return rate * (scaled - mean_one - unit * mean_two)


def add_sums(sums_ref, grad, unit):
    @pl.when(pl.program_id(0) == 0)
    def clear():
        sums_ref[...] = jnp.zeros_like(sums_ref)

    sums_ref[0:1] += jnp.sum(grad * unit, 0, keepdims=True)
    sums_ref[1:2] += jnp.sum(grad, 0, keepdims=True)


def second_norm_grad_kernel(target_ref, middle_ref, upstream_ref, gain_ref, weight_ref, *refs):
    sources = refs[:-4]
    grad_ref, low_ref, context_ref, sums_ref = refs[-4:]
    grad = fetched(column_of(target_ref[...]), sources)
    unit, rate = unit_of(middle_ref[...])
    add_sums(sums_ref, grad, unit)
    total = upstream_ref[...].astype(f32) + norm_back(grad, gain_ref[...], unit, rate)
    grad_ref[...] = total
    low = total.astype(bf16)
    low_ref[...] = low
    context_ref[...] = dot_nt(low, weight_ref[...]).astype(bf16)


def input_grad_kernel(tokens_ref, *refs):
    grad_ref, sums_ref = refs[-2:]
    count = (len(refs) - 2) // 2
    grad = 0.0
    for part, weight in zip(refs[:count], refs[count : 2 * count]):
        grad += dot_nt(part[...], weight[...])
    unit, _ = unit_of(tokens_ref[...].astype(f32))
    add_sums(sums_ref, grad, unit)
    grad_ref[...] = grad.astype(grad_ref.dtype)


def joint_kernel(tokens_ref, gain_ref, shift_ref, *refs):
    weights, (normed_ref, joint_ref) = refs[:-2], refs[-2:]
    normed = unit_of(tokens_ref[...].astype(f32))[0] * gain_ref[...] + shift_ref[...]
    normed = normed.astype(bf16)
    normed_ref[...] = normed
    width = normed.shape[1]
    for at, weight in enumerate(weights):
        joint_ref[:, at * width : (at + 1) * width] = dot(normed, weight[...]).astype(bf16)


def middle_kernel(context_ref, tokens_ref, route_ref, weight_ref, gain_ref, shift_ref, centroid_ref, middle_ref, normed_ref, gate_ref):
    middle = tokens_ref[...].astype(f32) + dot(context_ref[...], weight_ref[...])
    middle_ref[...] = middle
    normed = unit_of(middle)[0] * gain_ref[...] + shift_ref[...]
    normed_ref[...] = normed.astype(bf16)
    experts = centroid_ref.shape[0]
    route = column_of(route_ref[...])
    picked = route == lax.broadcasted_iota(jnp.int32, (route.shape[0], experts), 1)
    chosen = jnp.dot(
        picked.astype(f32), centroid_ref[...], precision=lax.Precision.HIGHEST, preferred_element_type=f32
    )
    gate_ref[...] = jax.nn.sigmoid(jnp.sum(normed * chosen, -1, keepdims=True))


def turned(x):
    size = tile_of(x.shape[1], 256)
    same = lax.broadcasted_iota(jnp.int32, (size, size), 0) == lax.broadcasted_iota(jnp.int32, (size, size), 1)
    unit = jnp.where(same, 1.0, 0.0).astype(bf16)
    return jnp.concatenate(
        [dot_nt(unit, x[:, at : at + size]).astype(bf16) for at in range(0, x.shape[1], size)], 0
    )


def weight_grads_kernel(*refs, count, blocks):
    lefts = [turned(ref[...]) for ref in refs[:count]]
    rights, out_ref = refs[count:-1], refs[-1]
    width = out_ref.shape[1] // len(blocks)
    for at, pairs in enumerate(blocks):
        total = sum(dot(lefts[left], rights[right][...]) for left, right in pairs)
        out_ref[:, at * width : (at + 1) * width] = total.astype(bf16)


def weight_grads(lefts, rights, blocks):
    width = lefts[0].shape[1]
    tile = tile_of(width, 256)
    specs = [pl.BlockSpec((left.shape[0], tile), lambda i: (0, i)) for left in lefts]
    specs += [pl.BlockSpec(right.shape, lambda i: (0, 0), pipeline_mode=pl.Buffered(1)) for right in rights]
    columns = len(blocks) * rights[0].shape[1]
    return pl.pallas_call(
        functools.partial(weight_grads_kernel, count=len(lefts), blocks=blocks),
        grid=(width // tile,),
        in_specs=specs,
        out_specs=pl.BlockSpec((tile, columns), lambda i: (i, 0)),
        out_shape=jax.ShapeDtypeStruct((width, columns), bf16),
        compiler_params=params(),
        cost_estimate=SHORT,
    )(*lefts, *rights)


def sums_kernel(*refs):
    rows = jnp.concatenate([refs[0][...] + refs[1][...], refs[2][...]], 0)
    rows = jnp.concatenate([rows, jnp.zeros((124, rows.shape[1]), f32)], 0)
    refs[-1][...] = rows.T.astype(bf16)


def column_sums(own, other, second):
    return pl.pallas_call(
        sums_kernel,
        out_shape=jax.ShapeDtypeStruct((own.shape[1], 128), bf16),
        compiler_params=params(),
        cost_estimate=SHORT,
    )(own, other, second)


def finish_kernel(early_ref, late_ref, in_ref, out_ref, vectors_ref):
    width = out_ref.shape[1]
    in_ref[:, :width] = late_ref[:, :width].astype(f32)
    in_ref[:, width:] = early_ref[...].astype(f32)
    out_ref[...] = late_ref[:, width : 2 * width].astype(f32)
    vectors_ref[...] = late_ref[:, 2 * width :].astype(f32).T[:8]


def finish(early, late):
    width = early.shape[0]
    tile = tile_of(width, 256)

    def cut(array):
        return pl.BlockSpec((tile, array.shape[1]), lambda i: (i, 0))

    in_shape = jax.ShapeDtypeStruct((width, 3 * width), f32)
    out_shape = jax.ShapeDtypeStruct((width, width), f32)
    return pl.pallas_call(
        finish_kernel,
        grid=(width // tile,),
        in_specs=[cut(early), cut(late)],
        out_specs=[cut(in_shape), cut(out_shape), pl.BlockSpec((8, tile), lambda i: (0, i))],
        out_shape=[in_shape, out_shape, jax.ShapeDtypeStruct((8, width), f32)],
        compiler_params=params(),
        cost_estimate=SHORT,
    )(early, late)


def by_tokens(kernel, flat, tiled, whole, out_shape):
    tile = tile_of(flat, 256)

    def cut(array):
        if array.shape == (1, flat):
            return pl.BlockSpec((1, tile), lambda i: (0, i))
        if array.shape[0] == flat:
            return pl.BlockSpec((tile, array.shape[1]), lambda i: (i, 0))
        return pl.BlockSpec(array.shape, lambda i: (0, 0))

    specs = [cut(array) for array in tiled]
    for array, column in whole:
        if column is None:
            specs.append(pl.BlockSpec(array.shape, lambda i: (0, 0), pipeline_mode=pl.Buffered(1)))
        else:
            shape = (array.shape[0], array.shape[0])
            specs.append(pl.BlockSpec(shape, lambda i, c=column: (0, c), pipeline_mode=pl.Buffered(1)))
    arrays = list(tiled) + [array for array, _ in whole]
    return pl.pallas_call(
        kernel,
        grid=(flat // tile,),
        in_specs=specs,
        out_specs=[cut(shape) for shape in out_shape],
        out_shape=out_shape,
        compiler_params=params(),
        cost_estimate=SHORT,
    )(*arrays)


def expert_kernel(*refs):
    x_ref, g_ref, up_ref, down_ref, cent_ref = refs[:5]
    out_ref, dx_ref, act_ref, pre_ref, pg_ref = refs[-5:]
    x = x_ref[...]
    g = g_ref[...].reshape(x.shape).astype(f32)
    centroid = cent_ref[...]
    gate = jax.nn.sigmoid(jnp.sum(x.astype(f32) * centroid, -1, keepdims=True))
    produced_grad = (gate * g).astype(bf16)
    pg_ref[...] = produced_grad
    pre = dot(x, up_ref[...])
    cumulative = 0.5 + 0.5 * lax.erf(pre * (0.5**0.5))
    act = (pre * cumulative).astype(bf16)
    slope = cumulative + pre * (jnp.exp(-0.5 * pre * pre) * 0.3989422804014327)
    act_ref[...] = act
    pre_grad = (dot_nt(produced_grad, down_ref[...]) * slope).astype(bf16)
    pre_ref[...] = pre_grad
    produced = dot(act, down_ref[...]).astype(bf16)
    out_ref[...] = produced.reshape(out_ref.shape)
    gate_grad = jnp.sum(g * produced.astype(f32), -1, keepdims=True)
    logit_grad = gate_grad * gate * (1.0 - gate)
    dx_ref[...] = (dot_nt(pre_grad, up_ref[...]) + logit_grad * centroid).astype(bf16)


def run_expert(x, g, half, up, down, centroid, outputs):
    rows, width = x.shape
    peers, halves, depth, _ = g.shape
    hidden = up.shape[1]
    tile = depth * tile_of(peers, max(1, 256 // depth))
    by_row = pl.BlockSpec((tile, width), lambda i: (i, 0))
    by_hidden = pl.BlockSpec((tile, hidden), lambda i: (i, 0))
    by_peer = pl.BlockSpec((tile // depth, 1, depth, width), lambda i: (i, half, 0, 0))

    def whole(shape):
        return pl.BlockSpec(shape, lambda i: (0, 0), pipeline_mode=pl.Buffered(1))

    in_specs = [by_row, by_peer, whole((width, hidden)), whole((hidden, width)), whole((1, width))]
    arrays = [x, g, up, down, centroid]
    aliases = {}
    if outputs is not None:
        in_specs.append(pl.BlockSpec(memory_space=pl.ANY))
        arrays.append(outputs)
        aliases = {5: 0}
    row_shape = jax.ShapeDtypeStruct((rows, width), bf16)
    hidden_shape = jax.ShapeDtypeStruct((rows, hidden), bf16)
    return pl.pallas_call(
        expert_kernel,
        grid=(rows // tile,),
        in_specs=in_specs,
        out_specs=[by_peer, by_row, by_hidden, by_hidden, by_row],
        out_shape=[jax.ShapeDtypeStruct(g.shape, bf16), row_shape, hidden_shape, hidden_shape, row_shape],
        input_output_aliases=aliases,
        compiler_params=params(),
        cost_estimate=SHORT,
    )(*arrays)


def stages_of(wide, blocks):
    def bits(low, high):
        found = []
        while low < high:
            found.append(low)
            low *= 2
        return found

    stages = (bits(1, min(2, wide)), bits(2, min(4, wide)) + bits(wide, wide * blocks), bits(4, wide))
    return [stage for stage in stages if stage]


def spread(code, bits):
    return sum(bit for i, bit in enumerate(bits) if code >> i & 1)


def swap(array, mask):
    total = lax.axis_size("blk") * lax.axis_size("wide")
    return lax.ppermute(array, ("blk", "wide"), [(i, i ^ mask) for i in range(total)])


def places_of(stages):
    me = lax.axis_index("blk") * lax.axis_size("wide") + lax.axis_index("wide")
    return [sum((me // bit % 2) << i for i, bit in enumerate(bits)) for bits in stages]


def reduce_step(parts, bits, code):
    count = 1 << len(bits)
    summed = []
    for x in parts:
        rows = x.shape[0] // count

        def piece(index):
            return lax.dynamic_slice_in_dim(x, index * rows, rows, 0)

        got = [swap(piece(code ^ other).astype(bf16), spread(other, bits)) for other in range(1, count)]
        total = piece(code).astype(f32)
        for part in got:
            total = total + part.astype(f32)
        summed.append(total)
    return summed


def gather_step(parts, bits, code):
    gathered = []
    for x in parts:
        rows = x.shape[0]
        whole = jnp.zeros((rows << len(bits), x.shape[1]), bf16)
        whole = lax.dynamic_update_slice_in_dim(whole, x, code * rows, 0)
        for other in range(1, 1 << len(bits)):
            part = swap(x, spread(other, bits))
            whole = lax.dynamic_update_slice_in_dim(whole, part, (code ^ other) * rows, 0)
        gathered.append(whole)
    return gathered


def body(
    tokens,
    segments,
    routes,
    project_in,
    project_out,
    first_gain,
    first_shift,
    second_gain,
    second_shift,
    centroids,
    expert_up,
    expert_down,
    cotangent,
):
    rows, block_len, width = tokens.shape
    blocks = lax.axis_size("blk")
    me = lax.axis_index("blk")
    flat = rows * block_len
    experts = centroids.shape[0]
    local_experts = expert_up.shape[0]
    peers = experts // local_experts
    capacity = 2 * block_len // experts
    halves = 2 if capacity % 16 == 0 else 1
    depth = capacity // halves
    half_slots = experts * rows * depth

    shifts = range(1, blocks)

    def ahead(array, shift):
        return lax.ppermute(array, "blk", [(i, i + shift) for i in range(blocks - shift)])

    def behind(array, shift):
        return lax.ppermute(array, "blk", [(i + shift, i) for i in range(blocks - shift)])

    other_tokens = jnp.concatenate([ahead(tokens, shift) for shift in shifts], 1)
    other_flat = other_tokens.reshape(-1, width)

    route_ids = routes[:, :, 0]
    picked = route_ids[:, :, None] == lax.iota(jnp.int32, experts)[None, None, :]
    places = lax.iota(jnp.int32, block_len)
    before = (places[None, :] <= places[:, None]).astype(bf16)
    ranks = jnp.einsum("qk,rke->rqe", before, picked.astype(bf16), preferred_element_type=f32)
    slot_index = jnp.sum(jnp.where(picked, ranks, 0.0), 2).astype(jnp.int32) - 1
    row_index = lax.iota(jnp.int32, rows)[:, None]
    half = slot_index // depth
    place_in_half = row_index * depth + slot_index - half * depth
    target_halves = half * half_slots + route_ids * (rows * depth) + place_in_half
    target_whole = (route_ids * halves + half) * (rows * depth) + place_in_half

    def exchange(array):
        return lax.all_to_all(
            array.reshape(experts, -1, width), "wide", split_axis=0, concat_axis=0, tiled=True
        )

    upstream = cotangent.reshape(flat, width)

    own_segments = lax.dynamic_slice_in_dim(segments, me * block_len, block_len, 1)
    smaller = segments[:, None, :] < own_segments[:, :, None]
    starts = jnp.sum(smaller.astype(jnp.int32), 2)
    attention = Attention(me, starts, rows, block_len, width)

    tokens_flat = tokens.reshape(flat, width)

    first_gain_row, first_shift_row = first_gain.reshape(1, width), first_shift.reshape(1, width)

    def joined(x, columns):
        count = len(columns)
        return by_tokens(
            joint_kernel,
            x.shape[0],
            (x,),
            [(first_gain_row, None), (first_shift_row, None)] + [(project_in, column) for column in columns],
            [
                jax.ShapeDtypeStruct(x.shape, bf16),
                jax.ShapeDtypeStruct((x.shape[0], count * width), bf16),
            ],
        )

    normed_one, joint = joined(tokens_flat, (0, 1, 2))
    route_row = routes.reshape(1, flat)
    target_halves_row, target_whole_row = target_halves.reshape(1, flat), target_whole.reshape(1, flat)
    second_gain_row, second_shift_row = second_gain.reshape(1, width), second_shift.reshape(1, width)
    small = (attention.low, attention.start_row, route_row, target_halves_row, target_whole_row)
    small += (first_gain_row, first_shift_row, second_gain_row, second_shift_row)
    small, to_place = lax.optimization_barrier((small, upstream))
    attention.low, attention.start_row, route_row, target_halves_row, target_whole_row = small[:5]
    first_gain_row, first_shift_row, second_gain_row, second_shift_row = small[5:]
    grads_arrived = exchange(place(target_whole_row, to_place, halves * half_slots))
    grads_arrived = grads_arrived.reshape(peers, local_experts, halves, rows * depth, width)
    joint = joint.reshape(rows, block_len, 3 * width)
    normed_other, other = joined(other_flat, (1, 2))
    other = other.reshape(rows, (blocks - 1) * block_len, 2 * width)
    context, lse = attention.forward(joint, other)
    context_flat = context.reshape(flat, width)

    wide_shape = jax.ShapeDtypeStruct((flat, width), f32)
    low_shape = jax.ShapeDtypeStruct((flat, width), bf16)
    sums_shape = jax.ShapeDtypeStruct((2, width), f32)
    middle, normed_two, gate = by_tokens(
        middle_kernel,
        flat,
        (context_flat, tokens_flat, route_row),
        [(project_out, None), (second_gain_row, None), (second_shift_row, None), (centroids, None)],
        [wide_shape, low_shape, jax.ShapeDtypeStruct((flat, 1), f32)],
    )
    normed_two, grads_arrived = lax.optimization_barrier((normed_two, grads_arrived))
    placed = [place(target_halves_row - h * half_slots, normed_two, half_slots) for h in range(halves)]
    placed[0], lse = lax.optimization_barrier((placed[0], lse))
    probs_own, probs_other = attention.probs(joint, joint, lse, True), attention.probs(joint, other, lse, False)
    placed[-1], probs_own, probs_other = lax.optimization_barrier((placed[-1], probs_own, probs_other))
    arrived = [exchange(part).reshape(peers, local_experts, rows * depth, width) for part in placed]

    own_experts = lax.axis_index("wide") * local_experts
    outputs, row_grads = [None] * local_experts, []
    down_pairs, up_pairs = [[] for _ in range(local_experts)], [[] for _ in range(local_experts)]
    for h in range(halves):
        half_dx = []
        for local in range(local_experts):
            x = arrived[h][:, local].reshape(-1, width)
            centroid = lax.dynamic_slice_in_dim(centroids, own_experts + local, 1, 0)
            outputs[local], dx, act, pre_grad, out_grad = run_expert(
                x, grads_arrived[:, local], h, expert_up[local], expert_down[local], centroid, outputs[local]
            )
            half_dx.append(dx.reshape(peers, 1, rows * depth, width))
            down_pairs[local].append((act, out_grad))
            up_pairs[local].append((x, pre_grad))
        row_grads.append(half_dx[0] if local_experts == 1 else jnp.concatenate(half_dx, 1))
    share = expert_up.shape[2] // blocks

    def share_of(array, block):
        return lax.dynamic_slice_in_dim(array, block * share, share, 1)

    def down_product(pairs, block):
        return sum(
            jnp.einsum("cf,cd->fd", share_of(act, block), out_grad, preferred_element_type=f32)
            for act, out_grad in pairs
        )

    def up_product(pairs, block):
        return sum(
            jnp.einsum("cd,cf->df", x, share_of(pre_grad, block), preferred_element_type=f32)
            for x, pre_grad in pairs
        )

    def product_shares(pairs, product):
        sent = [[product(pair, lax.rem(me + shift, blocks)).astype(bf16) for shift in shifts] for pair in pairs]
        return sent, [product(pair, me) for pair in pairs]

    def send_shares(sent):
        return [
            [
                lax.ppermute(part, "blk", [(i, (i + shift) % blocks) for i in range(blocks)])
                for shift, part in zip(shifts, parts)
            ]
            for parts in sent
        ]

    def summed_shares(own, got):
        totals = []
        for total, parts in zip(own, got):
            for part in parts:
                total = total + part.astype(f32)
            totals.append(total)
        return jnp.stack(totals, 0)

    back_arrived = [exchange(part).reshape(half_slots, width) for part in row_grads]
    back_arrived[0], down_pairs, up_pairs = lax.optimization_barrier((back_arrived[0], down_pairs, up_pairs))
    down_sent, down_own = product_shares(down_pairs, down_product)
    up_sent, up_own = product_shares(up_pairs, up_product)
    down_got, up_got = send_shares(down_sent), send_shares(up_sent)
    output = outputs[0][:, None] if local_experts == 1 else jnp.stack(outputs, 1)
    back_arrived, down_own, up_own, _, _ = lax.optimization_barrier(
        (back_arrived, down_own, up_own, down_sent, up_sent)
    )

    middle_grad, attn_grad, context_grad, second_sums = by_tokens(
        second_norm_grad_kernel,
        flat,
        (target_halves_row, middle, upstream),
        [(second_gain_row, None), (project_out, None)] + [(part, None) for part in back_arrived],
        [wide_shape, low_shape, low_shape, sums_shape],
    )
    context_grad, output = lax.optimization_barrier((context_grad, output))
    produced = exchange(output).reshape(halves * half_slots, width)
    context_grad = context_grad.reshape(rows, block_len, width)
    dq_state, dk_other, dv_other = attention.backward_other(joint, other, context_grad, context, probs_other)
    dk_other, dv_other = dk_other.reshape(-1, width), dv_other.reshape(-1, width)
    other_len = other_flat.shape[0]
    other_grad, other_sums = by_tokens(
        input_grad_kernel,
        other_len,
        (other_flat, dk_other, dv_other),
        [(project_in, 1), (project_in, 2)],
        [jax.ShapeDtypeStruct((other_len, width), bf16), sums_shape],
    )
    other_grad = other_grad.reshape(rows, blocks - 1, block_len, width)
    context_grad, returned, down_got = lax.optimization_barrier((context_grad, other_grad, down_got))
    returned = [behind(returned[:, shift - 1], shift) for shift in shifts]
    dq, dk, dv = attention.backward_own(joint, context_grad, context, probs_own, dq_state)
    dq, dk, dv = [part.reshape(flat, width) for part in (dq, dk, dv)]
    tied = (dq, dk, dv, produced, down_got, up_got)
    dq, dk, dv, produced, down_got, up_got = lax.optimization_barrier(tied)

    early = weight_grads(
        [normed_one, normed_other], [dk, dv, dk_other, dv_other], (((0, 0), (1, 2)), ((0, 1), (1, 3)))
    )
    late = weight_grads([normed_one, context_flat], [dq, attn_grad], (((0, 0),), ((1, 1),)))
    dq, dk, dv, returned = lax.optimization_barrier((dq, dk, dv, returned))
    own_grad, own_sums = by_tokens(
        input_grad_kernel,
        flat,
        (tokens_flat, dq, dk, dv),
        [(project_in, 0), (project_in, 1), (project_in, 2)],
        [wide_shape, sums_shape],
    )
    vectors = column_sums(own_sums, other_sums, second_sums)

    stages = stages_of(lax.axis_size("wide"), blocks)
    steps = list(zip(stages, places_of(stages)))
    early = [early]
    for step in steps:
        early = reduce_step(early, *step)
    early = [x.astype(bf16) for x in early]
    for step in reversed(steps):
        early = gather_step(early, *step)

    late = reduce_step([late, vectors], *steps[0])
    late = [jnp.concatenate(late, 1)]
    rest = (down_own, up_own, down_got, up_got)
    rest, late = lax.optimization_barrier((rest, late))
    down_own, up_own, down_got, up_got = rest
    down_share = summed_shares(down_own, down_got)
    up_share = summed_shares(up_own, up_got)
    for step in steps[1:-1]:
        late = reduce_step(late, *step)
    down_share, up_share, late = lax.optimization_barrier((down_share, up_share, late))
    late = reduce_step(late, *steps[-1])
    late = [x.astype(bf16) for x in late]
    late = gather_step(late, *steps[-1])
    rest = (middle, produced, own_grad, returned)
    rest, late = lax.optimization_barrier((rest, late))
    middle, produced, own_grad, returned = rest
    total_grad = own_grad
    for part in returned:
        total_grad = total_grad + part.reshape(flat, width).astype(f32)
    unit_one, rate_one = unit_of(tokens_flat.astype(f32))
    stream_grad = middle_grad + norm_back(total_grad, first_gain, unit_one, rate_one)
    (result,) = by_tokens(
        result_kernel,
        flat,
        (target_whole_row, middle, gate),
        [(produced, None)],
        [low_shape],
    )
    for step in reversed(steps[1:-1]):
        late = gather_step(late, *step)
    stream_grad, result, late = lax.optimization_barrier((stream_grad, result, late))
    in_sum, out_sum, vectors = finish(*early, *gather_step(late, *steps[0]))

    out_shape = (rows, block_len, width)
    return (
        result.reshape(out_shape),
        stream_grad.reshape(out_shape),
        in_sum,
        out_sum,
        vectors[0],
        vectors[1],
        vectors[2],
        vectors[3],
        up_share,
        down_share,
    )


def solution(mesh):
    return jax.shard_map(
        body,
        mesh=mesh,
        in_specs=(
            P("wide", "blk", None),
            P("wide", None),
            P("wide", "blk", None),
            P(),
            P(),
            P(),
            P(),
            P(),
            P(),
            P(),
            P("wide", None, None),
            P("wide", None, None),
            P("wide", "blk", None),
        ),
        out_specs=(
            P("wide", "blk", None),
            P("wide", "blk", None),
            P(),
            P(),
            P(),
            P(),
            P(),
            P(),
            P("wide", None, "blk"),
            P("wide", "blk", None),
        ),
        check_vma=False,
    )
```

```python
import functools

import jax
import jax.numpy as jnp
from jax import lax
from jax.experimental import pallas as pl
from jax.experimental.pallas import tpu as pltpu
from jax.sharding import PartitionSpec as P

HEAD_DIM = 64
GROUP = 4
LANES = GROUP * HEAD_DIM
NEG = -1e30
f32 = jnp.float32
bf16 = jnp.bfloat16
VMEM_LIMIT = 60 * 1024 * 1024
SHORT = pl.CostEstimate(flops=1, bytes_accessed=1, transcendentals=0)
LONG = pl.CostEstimate(flops=10**11, bytes_accessed=1, transcendentals=0)


def tile_of(size, most):
    tile = most
    while size % tile:
        tile //= 2
    return tile


def dot(a, b):
    return jnp.dot(a, b, preferred_element_type=f32)


def dot_nt(a, b):
    return lax.dot_general(a, b, (((1,), (1,)), ((), ())), preferred_element_type=f32)


def params(**more):
    return pltpu.CompilerParams(vmem_limit_bytes=VMEM_LIMIT, **more)


def largest_norm(x):
    head = lax.broadcasted_iota(jnp.int32, (LANES, 2 * HEAD_DIM), 0) // HEAD_DIM
    lane = lax.broadcasted_iota(jnp.int32, (LANES, 2 * HEAD_DIM), 1)
    pick = jnp.where(head == lane, 1.02, 0.0).astype(bf16)
    wide = x.astype(f32)
    return jnp.sqrt(jnp.max(dot((wide * wide).astype(bf16), pick), 0, keepdims=True))


def pair_of(head):
    return slice(2 * HEAD_DIM * (head // 2), 2 * HEAD_DIM * (head // 2 + 1))


def head_of_pair(pair, head, other=0.0):
    lane = lax.broadcasted_iota(jnp.int32, (1, 2 * HEAD_DIM), 1)
    keep = lane < HEAD_DIM if head % 2 == 0 else lane >= HEAD_DIM
    return jnp.where(keep, pair, jnp.full_like(pair, other))


def pieces_of(length, most):
    return [(at, min(most, length - at)) for at in range(0, length, most)]


def key_place(at, me, block_len, own):
    if own:
        return me * block_len + at
    return (me - 1 - at // block_len) * block_len + at % block_len


def mask_of(at, size, block, me, block_len, tile, starts, own, flipped):
    shape = (size, tile) if flipped else (tile, size)
    key = lax.broadcasted_iota(jnp.int32, shape, 0 if flipped else 1) + key_place(at, me, block_len, own)
    mask = key >= starts
    if own:
        query = lax.broadcasted_iota(jnp.int32, shape, 1 if flipped else 0) + (me * block_len + block * tile)
        mask = mask & (key <= query)
    return mask


def needed(at, size, block, low, me, block_len, tile, own):
    place = key_place(at, me, block_len, own)
    there = place + size > low
    if own:
        return jnp.logical_and(there, at < (block + 1) * tile)
    return jnp.logical_and(there, place >= 0)


def stat_place(head):
    return 2 * (head % 2) + head // 2


def split(x):
    parts = []
    for _ in range(3):
        part = x.astype(bf16)
        parts.append(part)
        x = x - part.astype(f32)
    return parts


def rows_of_lanes(x, lanes):
    lane = lax.broadcasted_iota(jnp.int32, (8, x.shape[1]), 1)
    row = lax.broadcasted_iota(jnp.int32, (8, x.shape[1]), 0)
    pick = jnp.zeros((8, x.shape[1]), f32)
    for at, number in enumerate(lanes):
        pick = jnp.where((row == at) & (lane == number), 1.0, pick)
    return sum(dot_nt(pick.astype(bf16), part) for part in split(x))[: len(lanes)]


def attend_kernel(me_ref, low_ref, q_ref, k_ref, v_ref, ok_ref, ov_ref, start_ref, ctx_out, lse_out, va, ova, acc, safe, *, tile, block_len):
    row, block = pl.program_id(0), pl.program_id(2)
    me = me_ref[0]
    low = low_ref[row, block]
    scale = HEAD_DIM**-0.5
    lane = lax.broadcasted_iota(jnp.int32, (1, 2 * HEAD_DIM), 1)
    pieces = [(True, at, size) for at, size in pieces_of(block_len, 512)]
    pieces += [(False, at, size) for at, size in pieces_of(ok_ref.shape[1], min(1024, block_len))]

    @pl.when(block == 0)
    def prepare():
        for values, spread in ((v_ref, va), (ov_ref, ova)):
            for head in range(GROUP):
                spread[head] = head_of_pair(values[0, :, pair_of(head)], head, 1.0)
        keys = jnp.maximum(largest_norm(k_ref[0]), largest_norm(ok_ref[0]))
        bound = jnp.max(largest_norm(q_ref[0]) * keys) * scale
        safe[0] = (bound < 60.0).astype(jnp.int32)

    queries = q_ref[0, pl.ds(pl.multiple_of(block * tile, tile), tile), :]
    queries = (queries.astype(f32) * scale).astype(bf16)
    starts = column_of(start_ref[0])

    def scores_of(own, at, size, head):
        mask = mask_of(at, size, block, me, block_len, tile, starts, own, False)
        keys = (k_ref if own else ok_ref)[0, at : at + size, pair_of(head)]
        return jnp.where(mask, dot_nt(head_of_pair(queries[:, pair_of(head)], head), keys), NEG)

    def attend(shifted):
        acc[...] = jnp.zeros_like(acc)
        peaks = [jnp.full((tile, 1), NEG, f32)] * GROUP
        if shifted:
            for own, at, size in pieces:
                there = needed(at, size, block, low, me, block_len, tile, own)
                for head in range(GROUP):
                    higher = jnp.max(scores_of(own, at, size, head), 1, keepdims=True)
                    peaks[head] = jnp.maximum(peaks[head], jnp.where(there, higher, NEG))
        for own, at, size in pieces:

            @pl.when(needed(at, size, block, low, me, block_len, tile, own))
            def piece(own=own, at=at, size=size):
                for head in range(GROUP):
                    scores = scores_of(own, at, size, head)
                    if shifted:
                        scores = scores - peaks[head]
                    weights = jnp.exp(scores).astype(bf16)
                    acc[head] += dot(weights, (va if own else ova)[head, at : at + size])

        stats = []
        for head in range(0, GROUP, 2):
            even, odd = acc[head], acc[head + 1]
            sums = pltpu.roll(jnp.where(lane < HEAD_DIM, odd, even), HEAD_DIM, 1)
            ctx_out[0, :, pair_of(head)] = (jnp.where(lane < HEAD_DIM, even, odd) / sums).astype(bf16)
            stats.append(sums)
        first = lane % HEAD_DIM < HEAD_DIM // 2
        stat = jnp.log(jnp.where(first, stats[0], stats[1]))
        if shifted:
            for head in range(GROUP):
                stat = jnp.where(lane // (HEAD_DIM // 2) == stat_place(head), stat + peaks[head], stat)
        lse_out[0, 0] = rows_of_lanes(stat, [stat_place(head) * (HEAD_DIM // 2) for head in range(GROUP)])

    @pl.when(safe[0] == 1)
    def without_shift():
        attend(False)

    @pl.when(safe[0] == 0)
    def with_shift():
        attend(True)


def probs_kernel(me_ref, low_ref, q_ref, k_ref, lse_ref, start_ref, out_ref, *, tile, block_len, own):
    row, block = pl.program_id(0), pl.program_id(2)
    me = me_ref[0]
    low = low_ref[row, block]
    queries = (q_ref[0].astype(f32) * HEAD_DIM**-0.5).astype(bf16)
    starts = start_ref[0]
    for at, size in pieces_of(k_ref.shape[1], min(512 if own else 1024, block_len)):

        @pl.when(needed(at, size, block, low, me, block_len, tile, own))
        def piece(at=at, size=size):
            rows = slice(at, at + size)
            mask = mask_of(at, size, block, me, block_len, tile, starts, own, True)
            for head in range(GROUP):
                query = head_of_pair(queries[:, pair_of(head)], head)
                scores = dot_nt(k_ref[0, rows, pair_of(head)], query) - lse_ref[0, 0, head : head + 1, :]
                out_ref[0, head, rows, :] = jnp.exp(jnp.where(mask, scores, NEG)).astype(bf16)


def grad_kernel(me_ref, low_ref, *refs, tile, block_len, own):
    q_ref, k_ref, v_ref, go_ref, ctx_ref, probs_ref = refs[:6]
    if own:
        dq_in, dq_out, dk_out, dv_out = refs[6:10]
    else:
        dq_out, dk_out, dv_out = refs[6:9]
    kt, dq, dk, dv = refs[-4:]
    row, block = pl.program_id(0), pl.program_id(2)
    me = me_ref[0]
    low = low_ref[row, block]
    scale = HEAD_DIM**-0.5
    length = k_ref.shape[1]
    pieces = pieces_of(length, min(512 if own else 1024, block_len))

    @pl.when(block == 0)
    def prepare():
        shape = (2 * HEAD_DIM, 2 * HEAD_DIM)
        same = lax.broadcasted_iota(jnp.int32, shape, 0) == lax.broadcasted_iota(jnp.int32, shape, 1)
        turn = jnp.where(same, scale, 0.0).astype(bf16)
        for head in range(0, GROUP, 2):
            kt[pair_of(head)] = dot_nt(turn, k_ref[0, :, pair_of(head)]).astype(bf16)
        dk[...] = jnp.zeros_like(dk)
        dv[...] = jnp.zeros_like(dv)

    queries = (q_ref[0].astype(f32) * scale).astype(bf16)
    go = go_ref[0]
    product = go.astype(f32) * ctx_ref[0].astype(f32)
    head_row = lax.broadcasted_iota(jnp.int32, (8, LANES), 0)
    head_lane = lax.broadcasted_iota(jnp.int32, (8, LANES), 1) // HEAD_DIM
    pick = jnp.where(head_row == head_lane, 1.0, 0.0).astype(bf16)
    inners = sum(dot_nt(pick, part) for part in split(product)[:2])
    inner = [inners[head : head + 1] for head in range(GROUP)]
    dq[...] = dq_in[0] if own else jnp.zeros_like(dq)
    for at, size in pieces:

        @pl.when(needed(at, size, block, low, me, block_len, tile, own))
        def piece(at=at, size=size):
            rows = slice(at, at + size)
            for first in range(0, GROUP, 2):
                pair = pair_of(first)
                values = v_ref[0, rows, pair]
                all_probs, all_grads, all_queries, all_go = [], [], [], []
                for head in (first, first + 1):
                    head_go = head_of_pair(go[:, pair], head)
                    probs = probs_ref[0, head, rows, :]
                    prob_grad = dot_nt(values, head_go)
                    score_grad = (probs.astype(f32) * (prob_grad - inner[head])).astype(bf16)
                    lanes = slice(head * HEAD_DIM, (head + 1) * HEAD_DIM)
                    dq[lanes] += dot(kt[lanes, rows], score_grad)
                    all_probs.append(probs)
                    all_grads.append(score_grad)
                    all_queries.append(head_of_pair(queries[:, pair], head))
                    all_go.append(head_go)
                dv[rows, pair] += dot(jnp.concatenate(all_probs, 1), jnp.concatenate(all_go, 0))
                dk[rows, pair] += dot(jnp.concatenate(all_grads, 1), jnp.concatenate(all_queries, 0))

    if own:
        dq_out[0] = dq[...].T.astype(bf16)
    else:
        dq_out[0] = dq[...]

    @pl.when(block == pl.num_programs(2) - 1)
    def write():
        dk_out[0] = dk[...].astype(bf16)
        dv_out[0] = dv[...].astype(bf16)


class Attention:
    def __init__(self, me, starts, rows, block_len, width):
        self.rows, self.block_len, self.width = rows, block_len, width
        self.tile = tile_of(block_len, 512)
        self.tiles = block_len // self.tile
        self.groups = width // LANES
        self.me = me.reshape(1).astype(jnp.int32)
        self.low = starts[:, :: self.tile]
        self.start_row = starts.reshape(rows, 1, block_len)

    def queries(self, offset=0):
        return pl.BlockSpec((1, self.tile, LANES), lambda r, g, b, *_: (r, b, offset * self.groups + g))

    def keys(self, length, offset):
        return pl.BlockSpec((1, length, LANES), lambda r, g, b, *_: (r, 0, offset * self.groups + g))

    def stat(self):
        return pl.BlockSpec((1, 1, GROUP, self.tile), lambda r, g, b, *_: (r, g, 0, b))

    def turned(self):
        return pl.BlockSpec((1, LANES, self.tile), lambda r, g, b, *_: (r, g, b))

    def row_starts(self):
        return pl.BlockSpec((1, 1, self.tile), lambda r, g, b, *_: (r, 0, b))

    def shape(self, length, dtype=bf16):
        return jax.ShapeDtypeStruct((self.rows, length, self.width), dtype)

    def call(self, kernel, cost, in_specs, out_specs, out_shape, scratch, args):
        return pl.pallas_call(
            functools.partial(kernel, tile=self.tile, block_len=self.block_len),
            grid_spec=pltpu.PrefetchScalarGridSpec(
                num_scalar_prefetch=2,
                grid=(self.rows, self.groups, self.tiles),
                in_specs=in_specs,
                out_specs=out_specs,
                scratch_shapes=scratch,
            ),
            out_shape=out_shape,
            compiler_params=params(),
            cost_estimate=cost,
        )(self.me, self.low, *args)

    def forward(self, joint, other):
        size, length = self.block_len, other.shape[1]
        return self.call(
            attend_kernel,
            LONG,
            [self.keys(size, 0), self.keys(size, 1), self.keys(size, 2)]
            + [self.keys(length, 0), self.keys(length, 1), self.row_starts()],
            [self.queries(), self.stat()],
            [self.shape(size), jax.ShapeDtypeStruct((self.rows, self.groups, GROUP, size), f32)],
            [
                pltpu.VMEM((GROUP, size, 2 * HEAD_DIM), bf16),
                pltpu.VMEM((GROUP, length, 2 * HEAD_DIM), bf16),
                pltpu.VMEM((GROUP, self.tile, 2 * HEAD_DIM), f32),
                pltpu.SMEM((1,), jnp.int32),
            ],
            (joint, joint, joint, other, other, self.start_row),
        )

    def grad_scratch(self, length):
        total = pltpu.VMEM((length, LANES), f32)
        return [pltpu.VMEM((LANES, length), bf16), pltpu.VMEM((LANES, self.tile), f32), total, total]

    def probs_spec(self, length):
        return pl.BlockSpec((1, GROUP, length, self.tile), lambda r, g, b, *_: (r, g, 0, b))

    def probs(self, joint, keys, lse, own):
        length = keys.shape[1]
        shape = (self.rows, self.groups * GROUP, length, self.block_len)
        (probs,) = self.call(
            functools.partial(probs_kernel, own=own),
            SHORT,
            [self.queries(), self.keys(length, 1 if own else 0), self.stat(), self.row_starts()],
            [self.probs_spec(length)],
            [jax.ShapeDtypeStruct(shape, bf16)],
            [],
            (joint, keys, lse, self.start_row),
        )
        return probs

    def backward_other(self, joint, other, grad, context, probs):
        size, length = self.block_len, other.shape[1]
        return self.call(
            functools.partial(grad_kernel, own=False),
            SHORT,
            [self.queries(), self.keys(length, 0), self.keys(length, 1)]
            + [self.queries(), self.queries(), self.probs_spec(length)],
            [self.turned(), self.keys(length, 0), self.keys(length, 0)],
            [
                jax.ShapeDtypeStruct((self.rows, self.width, size), f32),
                self.shape(length),
                self.shape(length),
            ],
            self.grad_scratch(length),
            (joint, other, other, grad, context, probs),
        )

    def backward_own(self, joint, grad, context, probs, dq_state):
        size = self.block_len
        return self.call(
            functools.partial(grad_kernel, own=True),
            LONG,
            [self.queries(), self.keys(size, 1), self.keys(size, 2)]
            + [self.queries(), self.queries(), self.probs_spec(size), self.turned()],
            [self.queries(), self.keys(size, 0), self.keys(size, 0)],
            [self.shape(size)] * 3,
            self.grad_scratch(size),
            (joint, joint, joint, grad, context, probs, dq_state),
        )


def place_kernel(target_ref, x_ref, out_ref):
    tile = out_ref.shape[0]
    slots = lax.broadcasted_iota(jnp.int32, (tile, target_ref.shape[1]), 0) + pl.program_id(0) * tile
    picked = jnp.where(slots == target_ref[...], 1.0, 0.0).astype(bf16)
    out_ref[...] = dot(picked, x_ref[...]).astype(bf16)


def place(target_row, x, slots):
    flat, width = x.shape
    tile = tile_of(slots, 256)
    return pl.pallas_call(
        place_kernel,
        grid=(slots // tile,),
        in_specs=[pl.BlockSpec((1, flat), lambda i: (0, 0)), pl.BlockSpec((flat, width), lambda i: (0, 0))],
        out_specs=pl.BlockSpec((tile, width), lambda i: (i, 0)),
        out_shape=jax.ShapeDtypeStruct((slots, width), bf16),
        compiler_params=params(),
        cost_estimate=SHORT,
    )(target_row, x)


def column_of(row):
    return jnp.broadcast_to(row.astype(f32), (8, row.shape[1])).T[:, :1].astype(jnp.int32)


def fetched(target, sources):
    total, before = 0.0, 0
    for source in sources:
        slots = lax.broadcasted_iota(jnp.int32, (target.shape[0], source.shape[0]), 1) + before
        total += dot(jnp.where(slots == target, 1.0, 0.0).astype(bf16), source[...])
        before += source.shape[0]
    return total


def result_kernel(target_ref, middle_ref, gate_ref, *refs):
    branch = fetched(column_of(target_ref[...]), refs[:-1])
    refs[-1][...] = (middle_ref[...] + gate_ref[...] * branch).astype(bf16)


def unit_of(x):
    center = x - jnp.mean(x, -1, keepdims=True)
    rate = lax.rsqrt(jnp.mean(center * center, -1, keepdims=True) + 1e-05)
    return center * rate, rate


def norm_back(grad, gain, unit, rate):
    scaled = grad * gain
    mean_one = jnp.mean(scaled, -1, keepdims=True)
    mean_two = jnp.mean(scaled * unit, -1, keepdims=True)
    return rate * (scaled - mean_one - unit * mean_two)


def add_sums(sums_ref, grad, unit):
    @pl.when(pl.program_id(0) == 0)
    def clear():
        sums_ref[...] = jnp.zeros_like(sums_ref)

    sums_ref[0:1] += jnp.sum(grad * unit, 0, keepdims=True)
    sums_ref[1:2] += jnp.sum(grad, 0, keepdims=True)


def second_norm_grad_kernel(target_ref, middle_ref, upstream_ref, gain_ref, weight_ref, *refs):
    sources = refs[:-4]
    grad_ref, low_ref, context_ref, sums_ref = refs[-4:]
    grad = fetched(column_of(target_ref[...]), sources)
    unit, rate = unit_of(middle_ref[...])
    add_sums(sums_ref, grad, unit)
    total = upstream_ref[...].astype(f32) + norm_back(grad, gain_ref[...], unit, rate)
    grad_ref[...] = total
    low = total.astype(bf16)
    low_ref[...] = low
    context_ref[...] = dot_nt(low, weight_ref[...]).astype(bf16)


def input_grad_kernel(tokens_ref, *refs):
    grad_ref, sums_ref = refs[-2:]
    count = (len(refs) - 2) // 2
    grad = 0.0
    for part, weight in zip(refs[:count], refs[count : 2 * count]):
        grad += dot_nt(part[...], weight[...])
    unit, _ = unit_of(tokens_ref[...].astype(f32))
    add_sums(sums_ref, grad, unit)
    grad_ref[...] = grad.astype(grad_ref.dtype)


def joint_kernel(tokens_ref, gain_ref, shift_ref, *refs):
    weights, (normed_ref, joint_ref) = refs[:-2], refs[-2:]
    normed = unit_of(tokens_ref[...].astype(f32))[0] * gain_ref[...] + shift_ref[...]
    normed = normed.astype(bf16)
    normed_ref[...] = normed
    width = normed.shape[1]
    for at, weight in enumerate(weights):
        joint_ref[:, at * width : (at + 1) * width] = dot(normed, weight[...]).astype(bf16)


def middle_kernel(context_ref, tokens_ref, route_ref, weight_ref, gain_ref, shift_ref, centroid_ref, middle_ref, normed_ref, gate_ref):
    middle = tokens_ref[...].astype(f32) + dot(context_ref[...], weight_ref[...])
    middle_ref[...] = middle
    normed = unit_of(middle)[0] * gain_ref[...] + shift_ref[...]
    normed_ref[...] = normed.astype(bf16)
    experts = centroid_ref.shape[0]
    route = column_of(route_ref[...])
    picked = route == lax.broadcasted_iota(jnp.int32, (route.shape[0], experts), 1)
    chosen = jnp.dot(
        picked.astype(f32), centroid_ref[...], precision=lax.Precision.HIGHEST, preferred_element_type=f32
    )
    gate_ref[...] = jax.nn.sigmoid(jnp.sum(normed * chosen, -1, keepdims=True))


def turned(x):
    size = tile_of(x.shape[1], 256)
    same = lax.broadcasted_iota(jnp.int32, (size, size), 0) == lax.broadcasted_iota(jnp.int32, (size, size), 1)
    unit = jnp.where(same, 1.0, 0.0).astype(bf16)
    return jnp.concatenate(
        [dot_nt(unit, x[:, at : at + size]).astype(bf16) for at in range(0, x.shape[1], size)], 0
    )


def weight_grads_kernel(*refs, count, blocks):
    lefts = [turned(ref[...]) for ref in refs[:count]]
    rights, out_ref = refs[count:-1], refs[-1]
    width = out_ref.shape[1] // len(blocks)
    for at, pairs in enumerate(blocks):
        total = sum(dot(lefts[left], rights[right][...]) for left, right in pairs)
        out_ref[:, at * width : (at + 1) * width] = total.astype(bf16)


def weight_grads(lefts, rights, blocks):
    width = lefts[0].shape[1]
    tile = tile_of(width, 256)
    specs = [pl.BlockSpec((left.shape[0], tile), lambda i: (0, i)) for left in lefts]
    specs += [pl.BlockSpec(right.shape, lambda i: (0, 0), pipeline_mode=pl.Buffered(1)) for right in rights]
    columns = len(blocks) * rights[0].shape[1]
    return pl.pallas_call(
        functools.partial(weight_grads_kernel, count=len(lefts), blocks=blocks),
        grid=(width // tile,),
        in_specs=specs,
        out_specs=pl.BlockSpec((tile, columns), lambda i: (i, 0)),
        out_shape=jax.ShapeDtypeStruct((width, columns), bf16),
        compiler_params=params(),
        cost_estimate=SHORT,
    )(*lefts, *rights)


def sums_kernel(*refs):
    rows = jnp.concatenate([refs[0][...] + refs[1][...], refs[2][...]], 0)
    rows = jnp.concatenate([rows, jnp.zeros((124, rows.shape[1]), f32)], 0)
    refs[-1][...] = rows.T.astype(bf16)


def column_sums(own, other, second):
    return pl.pallas_call(
        sums_kernel,
        out_shape=jax.ShapeDtypeStruct((own.shape[1], 128), bf16),
        compiler_params=params(),
        cost_estimate=SHORT,
    )(own, other, second)


def finish_kernel(early_ref, late_ref, in_ref, out_ref, vectors_ref):
    width = out_ref.shape[1]
    in_ref[:, :width] = late_ref[:, :width].astype(f32)
    in_ref[:, width:] = early_ref[...].astype(f32)
    out_ref[...] = late_ref[:, width : 2 * width].astype(f32)
    vectors_ref[...] = late_ref[:, 2 * width :].astype(f32).T[:8]


def finish(early, late):
    width = early.shape[0]
    tile = tile_of(width, 256)

    def cut(array):
        return pl.BlockSpec((tile, array.shape[1]), lambda i: (i, 0))

    in_shape = jax.ShapeDtypeStruct((width, 3 * width), f32)
    out_shape = jax.ShapeDtypeStruct((width, width), f32)
    return pl.pallas_call(
        finish_kernel,
        grid=(width // tile,),
        in_specs=[cut(early), cut(late)],
        out_specs=[cut(in_shape), cut(out_shape), pl.BlockSpec((8, tile), lambda i: (0, i))],
        out_shape=[in_shape, out_shape, jax.ShapeDtypeStruct((8, width), f32)],
        compiler_params=params(),
        cost_estimate=SHORT,
    )(early, late)


def by_tokens(kernel, flat, tiled, whole, out_shape):
    tile = tile_of(flat, 256)

    def cut(array):
        if array.shape == (1, flat):
            return pl.BlockSpec((1, tile), lambda i: (0, i))
        if array.shape[0] == flat:
            return pl.BlockSpec((tile, array.shape[1]), lambda i: (i, 0))
        return pl.BlockSpec(array.shape, lambda i: (0, 0))

    specs = [cut(array) for array in tiled]
    for array, column in whole:
        if column is None:
            specs.append(pl.BlockSpec(array.shape, lambda i: (0, 0), pipeline_mode=pl.Buffered(1)))
        else:
            shape = (array.shape[0], array.shape[0])
            specs.append(pl.BlockSpec(shape, lambda i, c=column: (0, c), pipeline_mode=pl.Buffered(1)))
    arrays = list(tiled) + [array for array, _ in whole]
    return pl.pallas_call(
        kernel,
        grid=(flat // tile,),
        in_specs=specs,
        out_specs=[cut(shape) for shape in out_shape],
        out_shape=out_shape,
        compiler_params=params(),
        cost_estimate=SHORT,
    )(*arrays)


def expert_kernel(*refs):
    x_ref, g_ref, up_ref, down_ref, cent_ref = refs[:5]
    out_ref, dx_ref, act_ref, pre_ref, pg_ref = refs[-5:]
    x = x_ref[...]
    g = g_ref[...].reshape(x.shape).astype(f32)
    centroid = cent_ref[...]
    gate = jax.nn.sigmoid(jnp.sum(x.astype(f32) * centroid, -1, keepdims=True))
    produced_grad = (gate * g).astype(bf16)
    pg_ref[...] = produced_grad
    pre = dot(x, up_ref[...])
    cumulative = 0.5 + 0.5 * lax.erf(pre * (0.5**0.5))
    act = (pre * cumulative).astype(bf16)
    slope = cumulative + pre * (jnp.exp(-0.5 * pre * pre) * 0.3989422804014327)
    act_ref[...] = act
    pre_grad = (dot_nt(produced_grad, down_ref[...]) * slope).astype(bf16)
    pre_ref[...] = pre_grad
    produced = dot(act, down_ref[...]).astype(bf16)
    out_ref[...] = produced.reshape(out_ref.shape)
    gate_grad = jnp.sum(g * produced.astype(f32), -1, keepdims=True)
    logit_grad = gate_grad * gate * (1.0 - gate)
    dx_ref[...] = (dot_nt(pre_grad, up_ref[...]) + logit_grad * centroid).astype(bf16)


def run_expert(x, g, half, up, down, centroid, outputs):
    rows, width = x.shape
    peers, halves, depth, _ = g.shape
    hidden = up.shape[1]
    tile = depth * tile_of(peers, max(1, 256 // depth))
    by_row = pl.BlockSpec((tile, width), lambda i: (i, 0))
    by_hidden = pl.BlockSpec((tile, hidden), lambda i: (i, 0))
    by_peer = pl.BlockSpec((tile // depth, 1, depth, width), lambda i: (i, half, 0, 0))

    def whole(shape):
        return pl.BlockSpec(shape, lambda i: (0, 0), pipeline_mode=pl.Buffered(1))

    in_specs = [by_row, by_peer, whole((width, hidden)), whole((hidden, width)), whole((1, width))]
    arrays = [x, g, up, down, centroid]
    aliases = {}
    if outputs is not None:
        in_specs.append(pl.BlockSpec(memory_space=pl.ANY))
        arrays.append(outputs)
        aliases = {5: 0}
    row_shape = jax.ShapeDtypeStruct((rows, width), bf16)
    hidden_shape = jax.ShapeDtypeStruct((rows, hidden), bf16)
    return pl.pallas_call(
        expert_kernel,
        grid=(rows // tile,),
        in_specs=in_specs,
        out_specs=[by_peer, by_row, by_hidden, by_hidden, by_row],
        out_shape=[jax.ShapeDtypeStruct(g.shape, bf16), row_shape, hidden_shape, hidden_shape, row_shape],
        input_output_aliases=aliases,
        compiler_params=params(),
        cost_estimate=SHORT,
    )(*arrays)


def stages_of(wide, blocks):
    def bits(low, high):
        found = []
        while low < high:
            found.append(low)
            low *= 2
        return found

    stages = (bits(1, min(2, wide)), bits(2, min(4, wide)) + bits(wide, wide * blocks), bits(4, wide))
    return [stage for stage in stages if stage]


def spread(code, bits):
    return sum(bit for i, bit in enumerate(bits) if code >> i & 1)


def swap(array, mask):
    total = lax.axis_size("blk") * lax.axis_size("wide")
    return lax.ppermute(array, ("blk", "wide"), [(i, i ^ mask) for i in range(total)])


def places_of(stages):
    me = lax.axis_index("blk") * lax.axis_size("wide") + lax.axis_index("wide")
    return [sum((me // bit % 2) << i for i, bit in enumerate(bits)) for bits in stages]


def reduce_step(parts, bits, code):
    count = 1 << len(bits)
    summed = []
    for x in parts:
        rows = x.shape[0] // count

        def piece(index):
            return lax.dynamic_slice_in_dim(x, index * rows, rows, 0)

        got = [swap(piece(code ^ other).astype(bf16), spread(other, bits)) for other in range(1, count)]
        total = piece(code).astype(f32)
        for part in got:
            total = total + part.astype(f32)
        summed.append(total)
    return summed


def gather_step(parts, bits, code):
    gathered = []
    for x in parts:
        rows = x.shape[0]
        if len(bits) == 1:
            part = swap(x, bits[0])
            gathered.append(jnp.where(code == 0, jnp.concatenate([x, part]), jnp.concatenate([part, x])))
            continue
        whole = jnp.zeros((rows << len(bits), x.shape[1]), bf16)
        whole = lax.dynamic_update_slice_in_dim(whole, x, code * rows, 0)
        for other in range(1, 1 << len(bits)):
            part = swap(x, spread(other, bits))
            whole = lax.dynamic_update_slice_in_dim(whole, part, (code ^ other) * rows, 0)
        gathered.append(whole)
    return gathered


def body(
    tokens,
    segments,
    routes,
    project_in,
    project_out,
    first_gain,
    first_shift,
    second_gain,
    second_shift,
    centroids,
    expert_up,
    expert_down,
    cotangent,
):
    rows, block_len, width = tokens.shape
    blocks = lax.axis_size("blk")
    me = lax.axis_index("blk")
    flat = rows * block_len
    experts = centroids.shape[0]
    local_experts = expert_up.shape[0]
    peers = experts // local_experts
    capacity = 2 * block_len // experts
    halves = 2 if capacity % 16 == 0 else 1
    depth = capacity // halves
    half_slots = experts * rows * depth

    shifts = range(1, blocks)

    def ahead(array, shift):
        return lax.ppermute(array, "blk", [(i, i + shift) for i in range(blocks - shift)])

    def behind(array, shift):
        return lax.ppermute(array, "blk", [(i + shift, i) for i in range(blocks - shift)])

    other_tokens = jnp.concatenate([ahead(tokens, shift) for shift in shifts], 1)
    other_flat = other_tokens.reshape(-1, width)

    route_ids = routes[:, :, 0]
    picked = route_ids[:, :, None] == lax.iota(jnp.int32, experts)[None, None, :]
    places = lax.iota(jnp.int32, block_len)
    before = (places[None, :] <= places[:, None]).astype(bf16)
    ranks = jnp.einsum("qk,rke->rqe", before, picked.astype(bf16), preferred_element_type=f32)
    slot_index = jnp.sum(jnp.where(picked, ranks, 0.0), 2).astype(jnp.int32) - 1
    row_index = lax.iota(jnp.int32, rows)[:, None]
    half = slot_index // depth
    place_in_half = row_index * depth + slot_index - half * depth
    target_halves = half * half_slots + route_ids * (rows * depth) + place_in_half
    target_whole = (route_ids * halves + half) * (rows * depth) + place_in_half

    def exchange(array):
        return lax.all_to_all(
            array.reshape(experts, -1, width), "wide", split_axis=0, concat_axis=0, tiled=True
        )

    upstream = cotangent.reshape(flat, width)

    own_segments = lax.dynamic_slice_in_dim(segments, me * block_len, block_len, 1)
    smaller = segments[:, None, :] < own_segments[:, :, None]
    starts = jnp.sum(smaller.astype(jnp.int32), 2)
    attention = Attention(me, starts, rows, block_len, width)

    tokens_flat = tokens.reshape(flat, width)

    first_gain_row, first_shift_row = first_gain.reshape(1, width), first_shift.reshape(1, width)

    def joined(x, columns):
        count = len(columns)
        return by_tokens(
            joint_kernel,
            x.shape[0],
            (x,),
            [(first_gain_row, None), (first_shift_row, None)] + [(project_in, column) for column in columns],
            [
                jax.ShapeDtypeStruct(x.shape, bf16),
                jax.ShapeDtypeStruct((x.shape[0], count * width), bf16),
            ],
        )

    normed_one, joint = joined(tokens_flat, (0, 1, 2))
    route_row = routes.reshape(1, flat)
    target_halves_row, target_whole_row = target_halves.reshape(1, flat), target_whole.reshape(1, flat)
    second_gain_row, second_shift_row = second_gain.reshape(1, width), second_shift.reshape(1, width)
    small = (attention.low, attention.start_row, route_row, target_halves_row, target_whole_row)
    small += (first_gain_row, first_shift_row, second_gain_row, second_shift_row)
    small, to_place = lax.optimization_barrier((small, upstream))
    attention.low, attention.start_row, route_row, target_halves_row, target_whole_row = small[:5]
    first_gain_row, first_shift_row, second_gain_row, second_shift_row = small[5:]
    grads_arrived = exchange(place(target_whole_row, to_place, halves * half_slots))
    grads_arrived = grads_arrived.reshape(peers, local_experts, halves, rows * depth, width)
    joint = joint.reshape(rows, block_len, 3 * width)
    normed_other, other = joined(other_flat, (1, 2))
    other = other.reshape(rows, (blocks - 1) * block_len, 2 * width)
    context, lse = attention.forward(joint, other)
    context_flat = context.reshape(flat, width)

    wide_shape = jax.ShapeDtypeStruct((flat, width), f32)
    low_shape = jax.ShapeDtypeStruct((flat, width), bf16)
    sums_shape = jax.ShapeDtypeStruct((2, width), f32)
    middle, normed_two, gate = by_tokens(
        middle_kernel,
        flat,
        (context_flat, tokens_flat, route_row),
        [(project_out, None), (second_gain_row, None), (second_shift_row, None), (centroids, None)],
        [wide_shape, low_shape, jax.ShapeDtypeStruct((flat, 1), f32)],
    )
    normed_two, grads_arrived = lax.optimization_barrier((normed_two, grads_arrived))
    placed = [place(target_halves_row - h * half_slots, normed_two, half_slots) for h in range(halves)]
    placed[0], lse = lax.optimization_barrier((placed[0], lse))
    probs_own, probs_other = attention.probs(joint, joint, lse, True), attention.probs(joint, other, lse, False)
    placed[-1], probs_own, probs_other = lax.optimization_barrier((placed[-1], probs_own, probs_other))
    arrived = [exchange(part).reshape(peers, local_experts, rows * depth, width) for part in placed]

    own_experts = lax.axis_index("wide") * local_experts
    outputs, row_grads = [None] * local_experts, []
    down_pairs, up_pairs = [[] for _ in range(local_experts)], [[] for _ in range(local_experts)]
    for h in range(halves):
        half_dx = []
        for local in range(local_experts):
            x = arrived[h][:, local].reshape(-1, width)
            centroid = lax.dynamic_slice_in_dim(centroids, own_experts + local, 1, 0)
            outputs[local], dx, act, pre_grad, out_grad = run_expert(
                x, grads_arrived[:, local], h, expert_up[local], expert_down[local], centroid, outputs[local]
            )
            half_dx.append(dx.reshape(peers, 1, rows * depth, width))
            down_pairs[local].append((act, out_grad))
            up_pairs[local].append((x, pre_grad))
        row_grads.append(half_dx[0] if local_experts == 1 else jnp.concatenate(half_dx, 1))
    share = expert_up.shape[2] // blocks

    def share_of(array, block):
        return lax.dynamic_slice_in_dim(array, block * share, share, 1)

    def down_product(pairs, block):
        return sum(
            jnp.einsum("cf,cd->fd", share_of(act, block), out_grad, preferred_element_type=f32)
            for act, out_grad in pairs
        )

    def up_product(pairs, block):
        return sum(
            jnp.einsum("cd,cf->df", x, share_of(pre_grad, block), preferred_element_type=f32)
            for x, pre_grad in pairs
        )

    def product_shares(pairs, product):
        sent = [[product(pair, lax.rem(me + shift, blocks)).astype(bf16) for shift in shifts] for pair in pairs]
        return sent, [product(pair, me) for pair in pairs]

    def send_shares(sent):
        return [
            [
                lax.ppermute(part, "blk", [(i, (i + shift) % blocks) for i in range(blocks)])
                for shift, part in zip(shifts, parts)
            ]
            for parts in sent
        ]

    def summed_shares(own, got):
        totals = []
        for total, parts in zip(own, got):
            for part in parts:
                total = total + part.astype(f32)
            totals.append(total)
        return jnp.stack(totals, 0)

    back_arrived = [exchange(part).reshape(half_slots, width) for part in row_grads]
    back_arrived[0], down_pairs, up_pairs = lax.optimization_barrier((back_arrived[0], down_pairs, up_pairs))
    down_sent, down_own = product_shares(down_pairs, down_product)
    up_sent, up_own = product_shares(up_pairs, up_product)
    down_got, up_got = send_shares(down_sent), send_shares(up_sent)
    output = outputs[0][:, None] if local_experts == 1 else jnp.stack(outputs, 1)
    back_arrived, down_own, up_own, _, _ = lax.optimization_barrier(
        (back_arrived, down_own, up_own, down_sent, up_sent)
    )

    middle_grad, attn_grad, context_grad, second_sums = by_tokens(
        second_norm_grad_kernel,
        flat,
        (target_halves_row, middle, upstream),
        [(second_gain_row, None), (project_out, None)] + [(part, None) for part in back_arrived],
        [wide_shape, low_shape, low_shape, sums_shape],
    )
    context_grad, output = lax.optimization_barrier((context_grad, output))
    produced = exchange(output).reshape(halves * half_slots, width)
    context_grad = context_grad.reshape(rows, block_len, width)
    dq_state, dk_other, dv_other = attention.backward_other(joint, other, context_grad, context, probs_other)
    dk_other, dv_other = dk_other.reshape(-1, width), dv_other.reshape(-1, width)
    other_len = other_flat.shape[0]
    other_grad, other_sums = by_tokens(
        input_grad_kernel,
        other_len,
        (other_flat, dk_other, dv_other),
        [(project_in, 1), (project_in, 2)],
        [jax.ShapeDtypeStruct((other_len, width), bf16), sums_shape],
    )
    other_grad = other_grad.reshape(rows, blocks - 1, block_len, width)
    context_grad, returned, down_got = lax.optimization_barrier((context_grad, other_grad, down_got))
    returned = [behind(returned[:, shift - 1], shift) for shift in shifts]
    dq, dk, dv = attention.backward_own(joint, context_grad, context, probs_own, dq_state)
    dq, dk, dv = [part.reshape(flat, width) for part in (dq, dk, dv)]
    tied = (dq, dk, dv, produced, down_got, up_got)
    dq, dk, dv, produced, down_got, up_got = lax.optimization_barrier(tied)

    early = weight_grads(
        [normed_one, normed_other], [dk, dv, dk_other, dv_other], (((0, 0), (1, 2)), ((0, 1), (1, 3)))
    )
    late = weight_grads([normed_one, context_flat], [dq, attn_grad], (((0, 0),), ((1, 1),)))
    dq, dk, dv, returned = lax.optimization_barrier((dq, dk, dv, returned))
    own_grad, own_sums = by_tokens(
        input_grad_kernel,
        flat,
        (tokens_flat, dq, dk, dv),
        [(project_in, 0), (project_in, 1), (project_in, 2)],
        [wide_shape, sums_shape],
    )
    vectors = column_sums(own_sums, other_sums, second_sums)

    stages = stages_of(lax.axis_size("wide"), blocks)
    steps = list(zip(stages, places_of(stages)))
    early = [early]
    for step in steps:
        early = reduce_step(early, *step)
    early = [x.astype(bf16) for x in early]
    for step in reversed(steps):
        early = gather_step(early, *step)

    late = reduce_step([late, vectors], *steps[0])
    late = [jnp.concatenate(late, 1)]
    rest = (down_own, up_own, down_got, up_got)
    rest, late = lax.optimization_barrier((rest, late))
    down_own, up_own, down_got, up_got = rest
    down_share = summed_shares(down_own, down_got)
    up_share = summed_shares(up_own, up_got)
    for step in steps[1:-1]:
        late = reduce_step(late, *step)
    down_share, up_share, late = lax.optimization_barrier((down_share, up_share, late))
    late = reduce_step(late, *steps[-1])
    late = [x.astype(bf16) for x in late]
    late = gather_step(late, *steps[-1])
    rest = (middle, produced, own_grad, returned)
    rest, late = lax.optimization_barrier((rest, late))
    middle, produced, own_grad, returned = rest
    total_grad = own_grad
    for part in returned:
        total_grad = total_grad + part.reshape(flat, width).astype(f32)
    unit_one, rate_one = unit_of(tokens_flat.astype(f32))
    stream_grad = middle_grad + norm_back(total_grad, first_gain, unit_one, rate_one)
    (result,) = by_tokens(
        result_kernel,
        flat,
        (target_whole_row, middle, gate),
        [(produced, None)],
        [low_shape],
    )
    for step in reversed(steps[1:-1]):
        late = gather_step(late, *step)
    stream_grad, result, late = lax.optimization_barrier((stream_grad, result, late))
    in_sum, out_sum, vectors = finish(*early, *gather_step(late, *steps[0]))

    out_shape = (rows, block_len, width)
    return (
        result.reshape(out_shape),
        stream_grad.reshape(out_shape),
        in_sum,
        out_sum,
        vectors[0],
        vectors[1],
        vectors[2],
        vectors[3],
        up_share,
        down_share,
    )


def solution(mesh):
    return jax.shard_map(
        body,
        mesh=mesh,
        in_specs=(
            P("wide", "blk", None),
            P("wide", None),
            P("wide", "blk", None),
            P(),
            P(),
            P(),
            P(),
            P(),
            P(),
            P(),
            P("wide", None, None),
            P("wide", None, None),
            P("wide", "blk", None),
        ),
        out_specs=(
            P("wide", "blk", None),
            P("wide", "blk", None),
            P(),
            P(),
            P(),
            P(),
            P(),
            P(),
            P("wide", None, "blk"),
            P("wide", "blk", None),
        ),
        check_vma=False,
    )
```
